32 devices in a mesh: chan: 8 (over y, x, core), tm: 4 (over z).
Axes of the slice: x: 2, y: 2, z: 4, core: 2. Of those that a mesh axis runs over, the one named last changes fastest.
Arguments:
- records: bfloat16 [128, 16384], P('chan', 'tm'), may hold values from -100 to 100, as said below
- pair_rows: int32 [8, 16], P('chan'), may hold values from 0 to 15, each once within a row
- fir_taps: float32 [32], replicated, may hold values from -1 to 1
- source_blocks: int32 [2], replicated, may hold values from 0 to 15
Outputs:
- stacks: float32 [2, 8, 128, 1024], P(None, None, 'chan', 'tm')
The draws below stay inside these ranges and needn't reach their ends.
Inputs may be any that keep to these rules, and one draw needn't show every extreme that they name: Seismic noise records, one row a channel.
All inputs are finite; a program needn't handle non-finite values.
Results may differ from the reference program's by a relative error of at most 0.0037.
Values may be sent and summed in bfloat16 or wider, within the bound.
A program may use at most 128 MiB of HBM per device.

```python
import math
import jax
import jax.numpy as jnp
from jax import lax

CR = 16
VS = 8
STEPS = 2
LAGS = 1024
TAPS = 32
CHANNELS = 128
WINDOW = 4096
SAMPLES = 16384
SRC_BLOCKS = 16
N_CHAN = 8


def draw_records(key, part):
    key_scale, key_noise = jax.random.split(key, 2)
    row_scale = jnp.exp(jax.random.uniform(key_scale, (CHANNELS, 1), minval=0.0, maxval=math.log(10.0)))
    envelope = 1.0 + 0.8 * jnp.arange(SAMPLES, dtype=jnp.float32)[None, :] / SAMPLES
    noise = jnp.clip(jax.random.normal(key_noise, (CHANNELS, SAMPLES)), -5.0, 5.0)
    return (noise * row_scale * envelope).astype(jnp.bfloat16)


def scatter_about(key, shape, deviation, bound, held_as=jnp.bfloat16):
    values = jax.random.normal(key, shape, jnp.float32) * deviation
    return jnp.minimum(jnp.maximum(values, -bound), bound).astype(held_as)


def setup_inputs(seed: int = 0) -> dict:
    splits = jax.random.split(jax.random.key(seed), 5)
    records = draw_records(jax.random.fold_in(splits[4], 71), 0)
    pair_rows = jax.vmap(lambda own: jax.random.permutation(own, CR))(jax.random.split(splits[1], N_CHAN)).reshape((N_CHAN, CR)).astype(jnp.int32)
    fir_taps = scatter_about(splits[2], (TAPS,), TAPS ** -0.5, 1.0, jnp.float32)
    source_blocks = jax.random.randint(splits[3], (STEPS,), 0, SRC_BLOCKS).astype(jnp.int32)
    return {"records": records, "pair_rows": pair_rows, "fir_taps": fir_taps, "source_blocks": source_blocks}


def reference(records, pair_rows, fir_taps, source_blocks):
    blocks = records.reshape(N_CHAN, CR, SAMPLES)
    partner_block = (jnp.arange(N_CHAN) + N_CHAN // 2) % N_CHAN
    partner = blocks[partner_block]
    partner = jax.vmap(lambda block_rows, chosen: block_rows[chosen])(partner, pair_rows)
    combined = 0.5 * (records.astype(jnp.float32) + partner.reshape(CHANNELS, SAMPLES).astype(jnp.float32))
    padded = jnp.pad(combined, ((0, 0), (TAPS, 0)))
    filtered = jnp.zeros((CHANNELS, WINDOW), jnp.float32)
    for offset in range(TAPS):
        begin = TAPS + 3 - offset
        filtered = filtered + fir_taps[offset] * padded[:, begin:begin + 4 * WINDOW:4]
    power = lax.optimization_barrier(jnp.sum(filtered * filtered, axis=1)) / WINDOW
    whitened = (filtered * lax.rsqrt(power + 1e-06)[:, None]).astype(jnp.bfloat16)
    picked = []
    for step_index in range(STEPS):
        start_row = (source_blocks[step_index] * VS).astype(jnp.int32)
        picked.append(lax.dynamic_slice_in_dim(whitened, start_row, VS, 0))
    sources = jnp.stack(picked)
    fft_length = 2 * WINDOW
    spectra = jnp.fft.rfft(whitened.astype(jnp.float32), n=fft_length, axis=1)

    def one_source(source_row):
        source_spec = jnp.fft.rfft(source_row.astype(jnp.float32), n=fft_length)
        full_corr = jnp.fft.irfft(jnp.conj(source_spec)[None, :] * spectra, n=fft_length, axis=1)
        return full_corr[:, :LAGS]
    source_rows = sources.reshape(STEPS * VS, WINDOW)
    correlations = lax.map(one_source, source_rows)
    return (correlations.reshape(STEPS, VS, CHANNELS, LAGS) * (1.0 / math.sqrt(WINDOW))).astype(jnp.float32)
```

```python
import functools
import math

import jax
import jax.numpy as jnp
from jax import lax
from jax.experimental import pallas as pl
from jax.experimental.pallas import tpu as pltpu
from jax.sharding import PartitionSpec as P

VS = 8
STEPS = 2
LAGS = 1024
TAPS = 32
LANES = 128
FINE = 16


def body(C, T, rows, taps_hbm, pair_hbm, blocks_hbm, rec_hbm, out_ref,
         taps_ref, pair_ref, blocks_ref, rec_ref, local_s,
         halo, phalo, praw, pw, chw, tw, ts, wp, wall,
         halo_s, halo_r, phalo_s, phalo_r, part_s, part_r, pw_s, pw_r, ch_s, ch_r, tw_s, tw_r, ts_s, ts_r):
    me = lax.axis_index("chan")
    t = lax.axis_index("tm")
    f32, bf16 = jnp.float32, jnp.bfloat16
    samples = rec_ref.shape[1] // 4
    lag_dev = LAGS // T
    P_ = max(1, lag_dev // LANES)
    A_ = min(lag_dev, LANES) // FINE
    window = samples * T

    def at_chan(d):
        return lax.rem(me + d, C)

    def at_tm(d):
        return lax.rem(t + d, T)

    loads = [pltpu.make_async_copy(src, dst, local_s.at[i]) for i, (src, dst) in enumerate((
        (taps_hbm, taps_ref), (rec_hbm, rec_ref), (pair_hbm, pair_ref), (blocks_hbm, blocks_ref)))]
    for load in loads:
        load.start()
    barrier = pltpu.get_barrier_semaphore()
    for d in range(1, C):
        pl.semaphore_signal(barrier, inc=1, device_id={"chan": at_chan(d)}, device_id_type=pl.DeviceIdType.MESH)
    for d in range(1, T):
        pl.semaphore_signal(barrier, inc=1, device_id={"tm": at_tm(d)}, device_id_type=pl.DeviceIdType.MESH)

    pl.semaphore_signal(barrier, inc=1, device_id={"chan": at_chan(C // 2), "tm": at_tm(T - 1)},
                        device_id_type=pl.DeviceIdType.MESH)

    def remote(src, dst, ssem, rsem, where):
        return pltpu.make_async_remote_copy(
            src_ref=src, dst_ref=dst, send_sem=ssem, recv_sem=rsem,
            device_id=where, device_id_type=pl.DeviceIdType.MESH)

    group = 4 * LANES
    depth = LANES + group
    row = lax.broadcasted_iota(jnp.int32, (8, LANES), 0)
    n = lax.broadcasted_iota(jnp.int32, (8, LANES), 1)
    tap = 4 * n + 3 - row
    cell = jnp.zeros((8, LANES), f32)
    loads[0].wait()
    for k in range(TAPS):
        cell = jnp.where(tap == k, taps_ref[k], cell)
    reach = TAPS // 4 + 1
    tiles = []
    for b in range(depth // 8):
        at = 2 * b - LANES // 4
        tile = jnp.zeros_like(cell)
        if at > -reach:
            tile = pltpu.roll(cell, at % LANES, 1) if at else cell
            if at < 0:
                tile = jnp.where(n < reach, tile, 0.0)
            elif at + reach > LANES:
                tile = jnp.where(n >= reach, tile, 0.0)
        tiles.append(tile)
    band = jnp.concatenate(tiles, axis=0)
    hi = band.astype(bf16)
    lo = (band - hi.astype(f32)).astype(bf16)
    band2 = jnp.concatenate([hi, lo], axis=1)

    for load in loads[1:]:
        load.wait()
    pl.semaphore_wait(barrier, C + T - 1)
    tail = rec_ref.shape[1] - LANES
    last = rec_ref.at[:, pl.ds(tail, LANES)]
    phalo_copy = remote(last, phalo, phalo_s, phalo_r, {"chan": at_chan(C // 2), "tm": at_tm(1)})
    halo_copy = remote(last, halo, halo_s, halo_r, {"tm": at_tm(1)})
    part_copy = remote(rec_ref, praw, part_s, part_r, {"chan": at_chan(C // 2)})
    phalo_copy.start()
    halo_copy.start()
    part_copy.start()

    wp[:, window:] = jnp.zeros((rows, wp.shape[1] - window), f32)
    wall[:, window:] = jnp.zeros((wall.shape[0], LANES), bf16)
    rr = lax.broadcasted_iota(jnp.int32, (rows, rows), 0)
    cc = lax.broadcasted_iota(jnp.int32, (rows, rows), 1)
    pick = jnp.zeros((rows, rows), jnp.int32)
    for r in range(rows):
        pick = jnp.where(rr == r, pair_ref[0, r], pick)
    perm = jnp.where(pick == cc, 1.0, 0.0).astype(bf16)

    groups = samples // LANES

    def filter_rows(raw):
        parts = []
        for g in range(groups):
            if g == 0:
                first = jnp.zeros((rows, LANES), bf16)
            else:
                first = raw[:, group * g - LANES:group * g]
            parts.append(jnp.concatenate([first, raw[:, group * g:group * (g + 1)]], axis=1))
        both = jnp.dot(jnp.concatenate(parts, axis=0), band2, preferred_element_type=f32)
        return both[:, :LANES] + both[:, LANES:]

    def permuted(x):
        return jnp.dot(perm, x, preferred_element_type=f32).astype(bf16)

    own = filter_rows(rec_ref[...])
    phalo_copy.wait()
    halo_copy.wait()
    edges = jnp.concatenate([halo[...], permuted(phalo[...])], axis=0)
    edges = jnp.dot(edges, band2[:LANES], preferred_element_type=f32)
    edges = edges[:, :LANES] + edges[:, LANES:]
    edge = edges[:rows] + edges[rows:]
    edge = jnp.where(t > 0, edge, jnp.zeros_like(edge))
    part_copy.wait()
    res = own + filter_rows(permuted(praw[...]))
    filtered = 0.5 * jnp.concatenate(
        [res[:rows] + edge] + [res[rows * g:rows * (g + 1)] for g in range(1, groups)], axis=1)
    sq = filtered * filtered
    acc = sq[:, :LANES]
    for g in range(1, groups):
        acc = acc + sq[:, LANES * g:LANES * (g + 1)]
    pw[t] = acc

    def spread(buf, slot, ssem, rsem, count, axis, place):
        sends = [remote(buf.at[slot], buf.at[slot], ssem.at[d], rsem.at[d], {axis: place(d)})
                 for d in range(1, count)]
        for s in sends:
            s.start()
        return sends

    def arrive(buf, ssem, rsem, count, axis, place):
        for d in range(1, count):
            slot = place(count - d)
            remote(buf.at[slot], buf.at[slot], ssem.at[d], rsem.at[d], {axis: place(d)}).wait_recv()

    pw_sends = spread(pw, t, pw_s, pw_r, T, "tm", at_tm)
    arrive(pw, pw_s, pw_r, T, "tm", at_tm)
    total = pw[0]
    for i in range(1, T):
        total = total + pw[i]
    power = jnp.sum(total, axis=1, keepdims=True) / window
    white = (filtered * lax.rsqrt(power + 1e-6)).astype(bf16)
    chw[me] = white
    tw[t] = white
    ch_sends = spread(chw, me, ch_s, ch_r, C, "chan", at_chan)
    tw_sends = spread(tw, t, tw_s, tw_r, T, "tm", at_tm)

    arrive(chw, ch_s, ch_r, C, "chan", at_chan)
    picked = []
    per = rows // VS
    for step in range(STEPS):
        blk = blocks_ref[step]
        owner = lax.div(blk, per)
        within = lax.rem(blk, per)
        x = chw[owner].astype(f32)
        half = x[:VS]
        for q in range(1, per):
            half = jnp.where(within == q, x[VS * q:VS * (q + 1)], half)
        picked.append(half)
    ts[t] = jnp.concatenate(picked, axis=0).astype(bf16)
    ts_sends = spread(ts, t, ts_s, ts_r, T, "tm", at_tm)
    arrive(tw, tw_s, tw_r, T, "tm", at_tm)
    for i in range(T):
        wp[:, samples * i:samples * (i + 1)] = tw[i].astype(f32)

    lag0 = t * lag_dev
    wide = samples + LANES * P_
    if lag_dev % LANES == 0:
        base, rest = lag0, 0
    else:
        base = lax.div(lag0, LANES) * LANES
        rest = lax.rem(lag0, LANES)

    for i in range(T):
        wrows = wp[:, pl.ds(pl.multiple_of(i * samples + base, LANES), wide)]
        for a in range(A_):
            rolled = wrows
            if lag_dev % LANES:
                rolled = pltpu.roll(wrows, wide - FINE * a - rest, 1)
            elif a:
                rolled = pltpu.roll(wrows, wide - FINE * a, 1)
            for p in range(P_):
                r0 = (p * A_ + a) * rows
                wall[r0:r0 + rows, samples * i:samples * (i + 1)] = (
                    rolled[:, LANES * p:LANES * p + samples].astype(bf16))

    span = samples + LANES

    def term(slot):
        srows = jnp.concatenate([ts[slot].astype(f32), jnp.zeros((rows, LANES), f32)], axis=1)
        xs = []
        for s in range(STEPS * VS):
            one = jnp.broadcast_to(srows[s:s + 1], (FINE, span))
            xs.append(pltpu.roll(one, 0, 1, stride=1, stride_axis=0).astype(bf16))
        ws = wall[:, pl.ds(pl.multiple_of(slot * samples, LANES), span)]
        return lax.dot_general(ws, jnp.concatenate(xs, axis=0),
                               (((1,), (1,)), ((), ())), preferred_element_type=f32)

    z = term(t)
    low = t < T // 2
    edge_dist = jnp.where(low, t, T - 1 - t)
    for k in range(T - 1):
        up = jnp.where(k >= edge_dist, k + 1, k)
        slot = jnp.where(low, up, T - 1 - up)
        d = lax.rem(t - slot + T, T)
        remote(ts.at[slot], ts.at[slot], ts_s.at[d], ts_r.at[d], {"tm": at_tm(d)}).wait_recv()
        z = z + term(slot)
    z = z * (1.0 / math.sqrt(window))

    lane_group = lax.broadcasted_iota(jnp.int32, (rows, LANES), 1) // FINE
    per_tile = LANES // FINE
    width = min(lag_dev, LANES)
    for p in range(P_):
        for lo_s in range(0, STEPS * VS, per_tile):
            turned = []
            for a in range(A_):
                r0 = (p * A_ + a) * rows
                tile = z[r0:r0 + rows, lo_s * FINE:lo_s * FINE + LANES]
                turned.append(pltpu.roll(tile, FINE * a, 1) if a else tile)
            for s in range(per_tile):
                o = turned[0]
                for a in range(1, A_):
                    o = jnp.where(lane_group == (s + a) % per_tile, turned[a], o)
                if s:
                    o = pltpu.roll(o, LANES - FINE * s, 1)
                out_ref[lo_s + s, :, LANES * p:LANES * p + width] = o[:, :width]

    for s in pw_sends + ch_sends + tw_sends + ts_sends:
        s.wait_send()


def shards(records, pair_rows, fir_taps, source_blocks):
    C = lax.axis_size("chan")
    T = lax.axis_size("tm")
    rows, raw = records.shape
    samples = raw // 4
    f32, bf16 = jnp.float32, jnp.bfloat16
    dma = pltpu.SemaphoreType.DMA
    vmem = pl.BlockSpec(memory_space=pltpu.VMEM)
    hbm = pl.BlockSpec(memory_space=pltpu.HBM)
    out = pl.pallas_call(
        functools.partial(body, C, T, rows),
        out_shape=jax.ShapeDtypeStruct((STEPS * VS, rows, LAGS // T), f32),
        in_specs=[hbm] * 4,
        out_specs=vmem,
        scratch_shapes=[
            pltpu.SMEM(fir_taps.shape, f32),
            pltpu.SMEM(pair_rows.shape, jnp.int32),
            pltpu.SMEM(source_blocks.shape, jnp.int32),
            pltpu.VMEM(records.shape, bf16),
            dma((4,)),
            pltpu.VMEM((rows, LANES), bf16),
            pltpu.VMEM((rows, LANES), bf16),
            pltpu.VMEM((rows, raw), bf16),
            pltpu.VMEM((T, rows, LANES), f32),
            pltpu.VMEM((C, rows, samples), bf16),
            pltpu.VMEM((T, rows, samples), bf16),
            pltpu.VMEM((T, rows, samples), bf16),
            pltpu.VMEM((rows, T * samples + LAGS + LANES), f32),
            pltpu.VMEM((LAGS // T // FINE * rows, T * samples + LANES), bf16),
            dma, dma, dma, dma, dma, dma,
            dma((T,)), dma((T,)), dma((C,)), dma((C,)),
            dma((T,)), dma((T,)), dma((T,)), dma((T,)),
        ],
        compiler_params=pltpu.CompilerParams(
            collective_id=0, has_side_effects=True, vmem_limit_bytes=(24 if samples * T <= 8192 else 60) * 2**20),
        cost_estimate=pl.CostEstimate(flops=600_000_000, bytes_accessed=1_000_000, transcendentals=0),
    )(fir_taps, pair_rows, source_blocks, records)
    return out.reshape(STEPS, VS, rows, LAGS // T)


def solution(mesh):
    return jax.shard_map(
        shards,
        mesh=mesh,
        in_specs=(P("chan", "tm"), P("chan", None), P(), P()),
        out_specs=P(None, None, "chan", "tm"),
        check_vma=False,
    )
```

```python
import functools
import math

import jax
import jax.numpy as jnp
from jax import lax
from jax.experimental import pallas as pl
from jax.experimental.pallas import tpu as pltpu
from jax.sharding import PartitionSpec as P

VS = 8
STEPS = 2
LAGS = 1024
TAPS = 32
LANES = 128
FINE = 16


def body(C, T, rows, taps_hbm, pair_hbm, blocks_hbm, rec_hbm, out_ref,
         taps_ref, pair_ref, blocks_ref, rec_ref, local_s,
         halo, phalo, praw, pw, chw, tw, ts, wp, wall,
         halo_s, halo_r, phalo_s, phalo_r, part_s, part_r, pw_s, pw_r, ch_s, ch_r, tw_s, tw_r, ts_s, ts_r):
    me = lax.axis_index("chan")
    t = lax.axis_index("tm")
    f32, bf16 = jnp.float32, jnp.bfloat16
    samples = rec_ref.shape[1] // 4
    lag_dev = LAGS // T
    P_ = max(1, lag_dev // LANES)
    A_ = min(lag_dev, LANES) // FINE
    window = samples * T

    def at_chan(d):
        return lax.rem(me + d, C)

    def at_tm(d):
        return lax.rem(t + d, T)

    loads = [pltpu.make_async_copy(src, dst, local_s.at[i]) for i, (src, dst) in enumerate((
        (taps_hbm, taps_ref), (rec_hbm, rec_ref), (pair_hbm, pair_ref), (blocks_hbm, blocks_ref)))]
    for load in loads:
        load.start()
    barrier = pltpu.get_barrier_semaphore()
    for d in range(1, C):
        pl.semaphore_signal(barrier, inc=1, device_id={"chan": at_chan(d)}, device_id_type=pl.DeviceIdType.MESH)
    for d in range(1, T):
        pl.semaphore_signal(barrier, inc=1, device_id={"tm": at_tm(d)}, device_id_type=pl.DeviceIdType.MESH)

    pl.semaphore_signal(barrier, inc=1, device_id={"chan": at_chan(C // 2), "tm": at_tm(T - 1)},
                        device_id_type=pl.DeviceIdType.MESH)

    def remote(src, dst, ssem, rsem, where):
        return pltpu.make_async_remote_copy(
            src_ref=src, dst_ref=dst, send_sem=ssem, recv_sem=rsem,
            device_id=where, device_id_type=pl.DeviceIdType.MESH)

    group = 4 * LANES
    depth = LANES + group
    row = lax.broadcasted_iota(jnp.int32, (8, LANES), 0)
    n = lax.broadcasted_iota(jnp.int32, (8, LANES), 1)
    tap = 4 * n + 3 - row
    cell = jnp.zeros((8, LANES), f32)
    loads[0].wait()
    for k in range(TAPS):
        cell = jnp.where(tap == k, taps_ref[k], cell)
    reach = TAPS // 4 + 1
    tiles = []
    for b in range(depth // 8):
        at = 2 * b - LANES // 4
        tile = jnp.zeros_like(cell)
        if at > -reach:
            tile = pltpu.roll(cell, at % LANES, 1) if at else cell
            if at < 0:
                tile = jnp.where(n < reach, tile, 0.0)
            elif at + reach > LANES:
                tile = jnp.where(n >= reach, tile, 0.0)
        tiles.append(tile)
    band = jnp.concatenate(tiles, axis=0)
    hi = band.astype(bf16)
    lo = (band - hi.astype(f32)).astype(bf16)
    band2 = jnp.concatenate([hi, lo], axis=1)

    for load in loads[1:]:
        load.wait()
    pl.semaphore_wait(barrier, C + T - 1)
    tail = rec_ref.shape[1] - LANES
    last = rec_ref.at[:, pl.ds(tail, LANES)]
    phalo_copy = remote(last, phalo, phalo_s, phalo_r, {"chan": at_chan(C // 2), "tm": at_tm(1)})
    halo_copy = remote(last, halo, halo_s, halo_r, {"tm": at_tm(1)})
    part_copy = remote(rec_ref, praw, part_s, part_r, {"chan": at_chan(C // 2)})
    phalo_copy.start()
    halo_copy.start()
    part_copy.start()

    wp[:, window:] = jnp.zeros((rows, wp.shape[1] - window), f32)
    wall[:, window:] = jnp.zeros((wall.shape[0], LANES), bf16)
    rr = lax.broadcasted_iota(jnp.int32, (rows, rows), 0)
    cc = lax.broadcasted_iota(jnp.int32, (rows, rows), 1)
    pick = jnp.zeros((rows, rows), jnp.int32)
    for r in range(rows):
        pick = jnp.where(rr == r, pair_ref[0, r], pick)
    perm = jnp.where(pick == cc, 1.0, 0.0).astype(bf16)

    groups = samples // LANES

    def filter_rows(raw):
        parts = []
        for g in range(groups):
            if g == 0:
                first = jnp.zeros((rows, LANES), bf16)
            else:
                first = raw[:, group * g - LANES:group * g]
            parts.append(jnp.concatenate([first, raw[:, group * g:group * (g + 1)]], axis=1))
        both = jnp.dot(jnp.concatenate(parts, axis=0), band2, preferred_element_type=f32)
        return both[:, :LANES] + both[:, LANES:]

    def permuted(x):
        return jnp.dot(perm, x, preferred_element_type=f32).astype(bf16)

    own = filter_rows(rec_ref[...])
    phalo_copy.wait()
    halo_copy.wait()
    edges = jnp.concatenate([halo[...], permuted(phalo[...])], axis=0)
    edges = jnp.dot(edges, band2[:LANES], preferred_element_type=f32)
    edges = edges[:, :LANES] + edges[:, LANES:]
    edge = edges[:rows] + edges[rows:]
    edge = jnp.where(t > 0, edge, jnp.zeros_like(edge))
    part_copy.wait()
    res = own + filter_rows(permuted(praw[...]))
    filtered = 0.5 * jnp.concatenate(
        [res[:rows] + edge] + [res[rows * g:rows * (g + 1)] for g in range(1, groups)], axis=1)
    sq = filtered * filtered
    acc = sq[:, :LANES]
    for g in range(1, groups):
        acc = acc + sq[:, LANES * g:LANES * (g + 1)]
    pw[t] = acc

    def spread(buf, slot, ssem, rsem, count, axis, place):
        sends = [remote(buf.at[slot], buf.at[slot], ssem.at[d], rsem.at[d], {axis: place(d)})
                 for d in range(1, count)]
        for s in sends:
            s.start()
        return sends

    def arrive(buf, ssem, rsem, count, axis, place):
        for d in range(1, count):
            slot = place(count - d)
            remote(buf.at[slot], buf.at[slot], ssem.at[d], rsem.at[d], {axis: place(d)}).wait_recv()

    pw_sends = spread(pw, t, pw_s, pw_r, T, "tm", at_tm)
    arrive(pw, pw_s, pw_r, T, "tm", at_tm)
    total = pw[0]
    for i in range(1, T):
        total = total + pw[i]
    power = jnp.sum(total, axis=1, keepdims=True) / window
    white = (filtered * lax.rsqrt(power + 1e-6)).astype(bf16)
    chw[me] = white
    tw[t] = white
    ch_sends = spread(chw, me, ch_s, ch_r, C, "chan", at_chan)
    tw_sends = spread(tw, t, tw_s, tw_r, T, "tm", at_tm)

    arrive(chw, ch_s, ch_r, C, "chan", at_chan)
    picked = []
    per = rows // VS
    for step in range(STEPS):
        blk = blocks_ref[step]
        owner = lax.div(blk, per)
        within = lax.rem(blk, per)
        x = chw[owner].astype(f32)
        half = x[:VS]
        for q in range(1, per):
            half = jnp.where(within == q, x[VS * q:VS * (q + 1)], half)
        picked.append(half)
    ts[t] = jnp.concatenate(picked, axis=0).astype(bf16)
    ts_sends = spread(ts, t, ts_s, ts_r, T, "tm", at_tm)
    arrive(tw, tw_s, tw_r, T, "tm", at_tm)
    for i in range(T):
        wp[:, samples * i:samples * (i + 1)] = tw[i].astype(f32)

    lag0 = t * lag_dev
    wide = samples + LANES * P_
    if lag_dev % LANES == 0:
        base, rest = lag0, 0
    else:
        base = lax.div(lag0, LANES) * LANES
        rest = lax.rem(lag0, LANES)

    for i in range(T):
        wrows = wp[:, pl.ds(pl.multiple_of(i * samples + base, LANES), wide)]
        for a in range(A_):
            rolled = wrows
            if lag_dev % LANES:
                rolled = pltpu.roll(wrows, wide - FINE * a - rest, 1)
            elif a:
                rolled = pltpu.roll(wrows, wide - FINE * a, 1)
            for p in range(P_):
                r0 = (p * A_ + a) * rows
                wall[r0:r0 + rows, samples * i:samples * (i + 1)] = (
                    rolled[:, LANES * p:LANES * p + samples].astype(bf16))

    span = samples + LANES

    def term(slot):
        srows = jnp.concatenate([ts[slot].astype(f32), jnp.zeros((rows, LANES), f32)], axis=1)
        xs = []
        for s in range(STEPS * VS):
            one = jnp.broadcast_to(srows[s:s + 1], (FINE, span))
            xs.append(pltpu.roll(one, 0, 1, stride=1, stride_axis=0).astype(bf16))
        ws = wall[:, pl.ds(pl.multiple_of(slot * samples, LANES), span)]
        return lax.dot_general(ws, jnp.concatenate(xs, axis=0),
                               (((1,), (1,)), ((), ())), preferred_element_type=f32)

    z = term(t)
    low = t < T // 2
    edge_dist = jnp.where(low, t, T - 1 - t)
    for k in range(T - 1):
        up = jnp.where(k >= edge_dist, k + 1, k)
        slot = jnp.where(low, up, T - 1 - up)
        d = lax.rem(t - slot + T, T)
        remote(ts.at[slot], ts.at[slot], ts_s.at[d], ts_r.at[d], {"tm": at_tm(d)}).wait_recv()
        z = z + term(slot)
    z = z * (1.0 / math.sqrt(window))

    lane_group = lax.broadcasted_iota(jnp.int32, (rows, LANES), 1) // FINE
    per_tile = LANES // FINE
    width = min(lag_dev, LANES)
    for p in range(P_):
        for lo_s in range(0, STEPS * VS, per_tile):
            turned = []
            for a in range(A_):
                r0 = (p * A_ + a) * rows
                tile = z[r0:r0 + rows, lo_s * FINE:lo_s * FINE + LANES]
                turned.append(pltpu.roll(tile, FINE * a, 1) if a else tile)
            for s in range(per_tile):
                o = turned[0]
                for a in range(1, A_):
                    o = jnp.where(lane_group == (s + a) % per_tile, turned[a], o)
                if s:
                    o = pltpu.roll(o, LANES - FINE * s, 1)
                out_ref[lo_s + s, :, LANES * p:LANES * p + width] = o[:, :width]

    for s in pw_sends + ch_sends + tw_sends + ts_sends:
        s.wait_send()


def shards(records, pair_rows, fir_taps, source_blocks):
    C = lax.axis_size("chan")
    T = lax.axis_size("tm")
    rows, raw = records.shape
    samples = raw // 4
    f32, bf16 = jnp.float32, jnp.bfloat16
    dma = pltpu.SemaphoreType.DMA
    vmem = pl.BlockSpec(memory_space=pltpu.VMEM)
    hbm = pl.BlockSpec(memory_space=pltpu.HBM)
    out = pl.pallas_call(
        functools.partial(body, C, T, rows),
        out_shape=pltpu.VMEM((STEPS * VS, rows, LAGS // T), f32),
        in_specs=[hbm] * 4,
        out_specs=vmem,
        scratch_shapes=[
            pltpu.SMEM(fir_taps.shape, f32),
            pltpu.SMEM(pair_rows.shape, jnp.int32),
            pltpu.SMEM(source_blocks.shape, jnp.int32),
            pltpu.VMEM(records.shape, bf16),
            dma((4,)),
            pltpu.VMEM((rows, LANES), bf16),
            pltpu.VMEM((rows, LANES), bf16),
            pltpu.VMEM((rows, raw), bf16),
            pltpu.VMEM((T, rows, LANES), f32),
            pltpu.VMEM((C, rows, samples), bf16),
            pltpu.VMEM((T, rows, samples), bf16),
            pltpu.VMEM((T, rows, samples), bf16),
            pltpu.VMEM((rows, T * samples + LAGS + LANES), f32),
            pltpu.VMEM((LAGS // T // FINE * rows, T * samples + LANES), bf16),
            dma, dma, dma, dma, dma, dma,
            dma((T,)), dma((T,)), dma((C,)), dma((C,)),
            dma((T,)), dma((T,)), dma((T,)), dma((T,)),
        ],
        compiler_params=pltpu.CompilerParams(
            collective_id=0, has_side_effects=True, vmem_limit_bytes=(24 if samples * T <= 8192 else 60) * 2**20),
        cost_estimate=pl.CostEstimate(flops=600_000_000, bytes_accessed=1_000_000, transcendentals=0),
    )(*(pltpu.with_memory_space_constraint(x, pltpu.HBM) for x in (fir_taps, pair_rows, source_blocks, records)))
    return out.reshape(STEPS, VS, rows, LAGS // T)


def solution(mesh):
    return jax.shard_map(
        shards,
        mesh=mesh,
        in_specs=(P("chan", "tm"), P("chan", None), P(), P()),
        out_specs=P(None, None, "chan", "tm"),
        check_vma=False,
    )
```

```python
import functools
import math

import jax
import jax.numpy as jnp
from jax import lax
from jax.experimental import pallas as pl
from jax.experimental.pallas import tpu as pltpu
from jax.sharding import PartitionSpec as P

VS = 8
STEPS = 2
LAGS = 1024
TAPS = 32
LANES = 128
FINE = 16
SPILL = TAPS // 4
FULL = 15


def body(C, T, rows, taps_hbm, pair_hbm, blocks_hbm, rec_hbm, out_ref,
         taps_ref, pair_ref, blocks_ref, rec_ref, local_s,
         plane, own, partner, ts, wp, wall,
         plane_s, plane_r, own_s, own_r, partner_s, partner_r, ts_s, ts_r):
    me = lax.axis_index("chan")
    t = lax.axis_index("tm")
    f32, bf16, i16, i32 = jnp.float32, jnp.bfloat16, jnp.int16, jnp.int32
    samples = rec_ref.shape[1] // 4
    width = samples + LANES
    lag_dev = LAGS // T
    P_ = max(1, lag_dev // LANES)
    A_ = min(lag_dev, LANES) // FINE
    window = samples * T

    def at_chan(d):
        return lax.rem(me + d, C)

    def at_tm(d):
        return lax.rem(t + d, T)

    def remote(src, dst, ssem, rsem, where):
        return pltpu.make_async_remote_copy(
            src_ref=src, dst_ref=dst, send_sem=ssem, recv_sem=rsem,
            device_id=where, device_id_type=pl.DeviceIdType.MESH)

    with jax.named_scope("greet"):
        loads = [pltpu.make_async_copy(src, dst, local_s.at[i]) for i, (src, dst) in enumerate((
            (taps_hbm, taps_ref), (rec_hbm, rec_ref), (pair_hbm, pair_ref), (blocks_hbm, blocks_ref)))]
        for load in loads:
            load.start()
        barrier = pltpu.get_barrier_semaphore()
        for d in range(1, C):
            pl.semaphore_signal(barrier, inc=1, device_id={"chan": at_chan(d)}, device_id_type=pl.DeviceIdType.MESH)
        for d in range(1, T):
            pl.semaphore_signal(barrier, inc=1, device_id={"tm": at_tm(d)}, device_id_type=pl.DeviceIdType.MESH)

    with jax.named_scope("band"):
        group = 4 * LANES
        depth = LANES + group
        row = lax.broadcasted_iota(i32, (8, LANES), 0)
        n = lax.broadcasted_iota(i32, (8, LANES), 1)
        tap = 4 * n + 3 - row
        cell = jnp.zeros((8, LANES), f32)
        loads[0].wait()
        for k in range(TAPS):
            cell = jnp.where(tap == k, taps_ref[k], cell)
        reach = TAPS // 4 + 1
        tiles = []
        for b in range(depth // 8):
            at = 2 * b - LANES // 4
            tile = jnp.zeros_like(cell)
            if at > -reach:
                tile = pltpu.roll(cell, at % LANES, 1) if at else cell
                if at < 0:
                    tile = jnp.where(n < reach, tile, 0.0)
                elif at + reach > LANES:
                    tile = jnp.where(n >= reach, tile, 0.0)
            tiles.append(tile)
        band = jnp.concatenate(tiles, axis=0)
        hi = band.astype(bf16)
        lo = (band - hi.astype(f32)).astype(bf16)
        band2 = jnp.concatenate([hi, lo], axis=1)
        for load in loads[1:]:
            load.wait()

    groups = samples // LANES
    lane = lax.broadcasted_iota(i32, (rows, LANES), 1)

    def encode(x, note):
        peak = jnp.maximum(jnp.max(jnp.abs(x), axis=1, keepdims=True), 1e-30)
        e = jnp.floor(jnp.log2(peak)) + 1.0
        q = jnp.clip(jnp.round(x * jnp.exp2(FULL - e)), -32767.0, 32767.0).astype(i32)
        last = jnp.where(lane == SPILL, e.astype(i32), jnp.where(lane == SPILL + 1, note, q[:, samples:]))
        return jnp.concatenate([q[:, :samples], last], axis=1).astype(i16)

    def scaled(v):
        return v * jnp.exp2(v[:, samples + SPILL:samples + SPILL + 1] - (FULL + 1))

    def plain(x):
        return x.astype(i32).astype(f32)

    def permuted(onehot, x):
        v = x.astype(i32)
        pair = jnp.concatenate([(v >> 8).astype(f32).astype(bf16), (v & 255).astype(f32).astype(bf16)], axis=1)
        both = jnp.dot(onehot, pair, preferred_element_type=f32)
        return 256.0 * both[:, :width] + both[:, width:]

    with jax.named_scope("filter"):
        raw = rec_ref[...]
        parts = []
        for g in range(groups):
            if g == 0:
                first = jnp.zeros((rows, LANES), bf16)
            else:
                first = raw[:, group * g - LANES:group * g]
            parts.append(jnp.concatenate([first, raw[:, group * g:group * (g + 1)]], axis=1))
        both = jnp.dot(jnp.concatenate(parts, axis=0), band2, preferred_element_type=f32)
        both = both[:, :LANES] + both[:, LANES:]
        edge = jnp.dot(raw[:, group * groups - LANES:], band2[:LANES], preferred_element_type=f32)
        edge = edge[:, :LANES] + edge[:, LANES:]
        filtered = jnp.concatenate([both[rows * g:rows * (g + 1)] for g in range(groups)] + [edge], axis=1)
        rr = lax.broadcasted_iota(i32, (rows, LANES), 0)
        pick = jnp.zeros((rows, LANES), i32)
        for r in range(rows):
            pick = jnp.where(rr == r, pair_ref[0, r], pick)
        perm = jnp.where(pick[:, :rows] == lax.broadcasted_iota(i32, (rows, rows), 1), 1.0, 0.0).astype(bf16)
        code = encode(filtered, pick)
        plane[me] = code
        own[t] = code

    with jax.named_scope("wait_greeting"):
        pl.semaphore_wait(barrier, C + T - 2)

    half = C // 2
    with jax.named_scope("send_filtered"):
        order = [half] + [d for d in range(1, C) if d != half]
        sends = [remote(plane.at[me], plane.at[me], plane_s.at[d], plane_r.at[d], {"chan": at_chan(d)}) for d in order]
        sends += [remote(own.at[t], own.at[t], own_s.at[d], own_r.at[d], {"tm": at_tm(d)}) for d in range(1, T)]
        for s in sends[:1] + sends[C - 1:] + sends[1:C - 1]:
            s.start()

    with jax.named_scope("clear"):
        wp[:, window:] = jnp.zeros((rows, wp.shape[1] - window), f32)
        wall[:, window:] = jnp.zeros((wall.shape[0], LANES), bf16)

    low = t < T // 2
    edge_dist = jnp.where(low, t, T - 1 - t)

    def near(k):
        up = jnp.where(k >= edge_dist, k + 1, k)
        slot = jnp.where(low, up, T - 1 - up)
        return slot, lax.rem(t - slot + T, T)

    relays = []

    def relay(k):
        slot, d = near(k)
        remote(own.at[slot], own.at[slot], own_s.at[d], own_r.at[d], {"tm": at_tm(d)}).wait_recv()
        s = remote(own.at[slot], partner.at[slot], partner_s.at[d], partner_r.at[d], {"chan": at_chan(half)})
        s.start()
        relays.append(s)

    with jax.named_scope("relay_first"):
        relay(0)

    with jax.named_scope("wait_plane"):
        for d in order:
            slot = at_chan(C - d)
            remote(plane.at[slot], plane.at[slot], plane_s.at[d], plane_r.at[d], {"chan": at_chan(d)}).wait_recv()

    with jax.named_scope("pick"):
        picked = []
        per = rows // VS

        def halved(x, within):
            y = x[:VS]
            for q in range(1, per):
                y = jnp.where(within == q, x[VS * q:VS * (q + 1)], y)
            return y

        for step in range(STEPS):
            blk = blocks_ref[step]
            owner = lax.div(blk, per)
            within = lax.rem(blk, per)
            mine = halved(plain(plane[owner]), within)
            pair = mine[:, samples + SPILL + 1:samples + SPILL + 2]
            onehot = jnp.where(pair == lax.broadcasted_iota(i32, (VS, rows), 1).astype(f32), 1.0, 0.0).astype(bf16)
            theirs = permuted(onehot, plane[lax.rem(owner + half, C)])
            picked.append(scaled(mine) + scaled(theirs))
        ts[t] = encode(jnp.concatenate(picked, axis=0), jnp.zeros((rows, LANES), i32))
        ts_sends = [remote(ts.at[t], ts.at[t], ts_s.at[d], ts_r.at[d], {"tm": at_tm(d)}) for d in range(1, T)]
        for s in ts_sends:
            s.start()

    with jax.named_scope("relay_rest"):
        for k in range(1, T - 1):
            relay(k)

    def assemble(blocks):
        out = []
        for i, x in enumerate(blocks):
            head = x[:, :LANES]
            if i:
                head = head + jnp.where(lane < SPILL, blocks[i - 1][:, samples:], 0.0)
            out.append(jnp.concatenate([head, x[:, LANES:samples]], axis=1))
        return out

    def whiten(blocks):
        acc = jnp.zeros((rows, LANES), f32)
        for x in blocks:
            sq = x * x
            for g in range(groups):
                acc = acc + sq[:, LANES * g:LANES * (g + 1)]
        scale = lax.rsqrt(jnp.sum(acc, axis=1, keepdims=True) / window + 1e-6)
        return [(x * scale).astype(bf16) for x in blocks]

    with jax.named_scope("wait_partner"):
        partner[t] = plane[at_chan(half)]
        for k in range(T - 1):
            slot, d = near(k)
            remote(partner.at[slot], partner.at[slot], partner_s.at[d], partner_r.at[d],
                   {"chan": at_chan(half)}).wait_recv()

    with jax.named_scope("white"):
        white = whiten(assemble([scaled(plain(own[i])) + scaled(permuted(perm, partner[i])) for i in range(T)]))
        for i in range(T):
            wp[:, samples * i:samples * (i + 1)] = white[i].astype(f32)

    with jax.named_scope("wall"):
        lag0 = t * lag_dev
        wide = samples + LANES * P_
        if lag_dev % LANES == 0:
            base, rest = lag0, 0
        else:
            base = lax.div(lag0, LANES) * LANES
            rest = lax.rem(lag0, LANES)
        for i in range(T):
            wrows = wp[:, pl.ds(pl.multiple_of(i * samples + base, LANES), wide)]
            for a in range(A_):
                rolled = wrows
                if lag_dev % LANES:
                    rolled = pltpu.roll(wrows, wide - FINE * a - rest, 1)
                elif a:
                    rolled = pltpu.roll(wrows, wide - FINE * a, 1)
                for p in range(P_):
                    r0 = (p * A_ + a) * rows
                    wall[r0:r0 + rows, samples * i:samples * (i + 1)] = (
                        rolled[:, LANES * p:LANES * p + samples].astype(bf16))

    with jax.named_scope("wait_sources"):
        for k in range(T - 1):
            slot, d = near(k)
            remote(ts.at[slot], ts.at[slot], ts_s.at[d], ts_r.at[d], {"tm": at_tm(d)}).wait_recv()

    with jax.named_scope("sources"):
        sources = whiten(assemble([2.0 * scaled(plain(ts[i])) for i in range(T)]))

    span = samples + LANES
    with jax.named_scope("correlate"):
        z = None
        for i in range(T):
            srows = jnp.concatenate([sources[i].astype(f32), jnp.zeros((rows, LANES), f32)], axis=1)
            xs = []
            for s in range(STEPS * VS):
                one = jnp.broadcast_to(srows[s:s + 1], (FINE, span))
                xs.append(pltpu.roll(one, 0, 1, stride=1, stride_axis=0).astype(bf16))
            ws = wall[:, samples * i:samples * i + span]
            term = lax.dot_general(ws, jnp.concatenate(xs, axis=0),
                                   (((1,), (1,)), ((), ())), preferred_element_type=f32)
            z = term if z is None else z + term
        z = z * (1.0 / math.sqrt(window))

    with jax.named_scope("result"):
        lane_group = lane // FINE
        per_tile = LANES // FINE
        span_out = min(lag_dev, LANES)
        for p in range(P_):
            for lo_s in range(0, STEPS * VS, per_tile):
                turned = []
                for a in range(A_):
                    r0 = (p * A_ + a) * rows
                    tile = z[r0:r0 + rows, lo_s * FINE:lo_s * FINE + LANES]
                    turned.append(pltpu.roll(tile, FINE * a, 1) if a else tile)
                for s in range(per_tile):
                    o = turned[0]
                    for a in range(1, A_):
                        o = jnp.where(lane_group == (s + a) % per_tile, turned[a], o)
                    if s:
                        o = pltpu.roll(o, LANES - FINE * s, 1)
                    out_ref[lo_s + s, :, LANES * p:LANES * p + span_out] = o[:, :span_out]

    with jax.named_scope("wait_sends"):
        for s in sends + relays + ts_sends:
            s.wait_send()


def shards(records, pair_rows, fir_taps, source_blocks):
    C = lax.axis_size("chan")
    T = lax.axis_size("tm")
    rows, raw = records.shape
    samples = raw // 4
    f32, bf16, i16 = jnp.float32, jnp.bfloat16, jnp.int16
    dma = pltpu.SemaphoreType.DMA
    hbm = pl.BlockSpec(memory_space=pltpu.HBM)
    operands = [pltpu.with_memory_space_constraint(x, pltpu.HBM)
                for x in (fir_taps, pair_rows, source_blocks, records)]
    out = pl.pallas_call(
        functools.partial(body, C, T, rows),
        out_shape=pltpu.VMEM((STEPS * VS, rows, LAGS // T), f32),
        in_specs=[hbm] * 4,
        out_specs=pl.BlockSpec(memory_space=pltpu.VMEM),
        scratch_shapes=[
            pltpu.SMEM(fir_taps.shape, f32),
            pltpu.SMEM(pair_rows.shape, jnp.int32),
            pltpu.SMEM(source_blocks.shape, jnp.int32),
            pltpu.VMEM(records.shape, bf16),
            dma((4,)),
            pltpu.VMEM((C, rows, samples + LANES), i16),
            pltpu.VMEM((T, rows, samples + LANES), i16),
            pltpu.VMEM((T, rows, samples + LANES), i16),
            pltpu.VMEM((T, rows, samples + LANES), i16),
            pltpu.VMEM((rows, T * samples + LAGS + LANES), f32),
            pltpu.VMEM((LAGS // T // FINE * rows, T * samples + LANES), bf16),
            dma((C,)), dma((C,)), dma((T,)), dma((T,)), dma((T,)), dma((T,)), dma((T,)), dma((T,)),
        ],
        compiler_params=pltpu.CompilerParams(
            collective_id=0, has_side_effects=True,
            vmem_limit_bytes=(24 if samples * T <= 8192 else 60) * 2**20),
        cost_estimate=pl.CostEstimate(flops=600_000_000, bytes_accessed=1_000_000, transcendentals=0),
    )(*operands)
    return out.reshape(STEPS, VS, rows, LAGS // T)


def solution(mesh):
    return jax.shard_map(
        shards,
        mesh=mesh,
        in_specs=(P("chan", "tm"), P("chan", None), P(), P()),
        out_specs=P(None, None, "chan", "tm"),
        check_vma=False,
    )
```

```python
import functools
import math

import jax
import jax.numpy as jnp
from jax import lax
from jax.experimental import pallas as pl
from jax.experimental.pallas import tpu as pltpu
from jax.sharding import PartitionSpec as P

VS = 8
STEPS = 2
LAGS = 1024
TAPS = 32
LANES = 128
FINE = 16
SPILL = TAPS // 4
FULL = 15


def body(C, T, rows, taps_hbm, pair_hbm, blocks_hbm, rec_hbm, out_ref,
         taps_ref, pair_ref, blocks_ref, rec_ref, local_s,
         halves, plane, own, partner, small, body_, wp, wall,
         plane_s, plane_r, own_s, own_r, partner_s, partner_r, small_s, small_r, body_s, body_r, twin_s, twin_r):
    me = lax.axis_index("chan")
    t = lax.axis_index("tm")
    f32, bf16, i16, i32 = jnp.float32, jnp.bfloat16, jnp.int16, jnp.int32
    samples = rec_ref.shape[1] // 4
    width = samples + LANES
    part = samples // 2
    half = C // 2
    side = lax.rem(me, 2)
    twin = me + 1 - 2 * side
    lag_dev = LAGS // T
    P_ = max(1, lag_dev // LANES)
    A_ = min(lag_dev, LANES) // FINE
    window = samples * T

    def at_chan(d):
        return lax.rem(me + d, C)

    def at_tm(d):
        return lax.rem(t + d, T)

    def remote(src, dst, ssem, rsem, where):
        return pltpu.make_async_remote_copy(
            src_ref=src, dst_ref=dst, send_sem=ssem, recv_sem=rsem,
            device_id=where, device_id_type=pl.DeviceIdType.MESH)

    with jax.named_scope("greet"):
        loads = [pltpu.make_async_copy(src, dst, local_s.at[i]) for i, (src, dst) in enumerate((
            (taps_hbm, taps_ref), (rec_hbm, rec_ref), (pair_hbm, pair_ref), (blocks_hbm, blocks_ref)))]
        for load in loads:
            load.start()
        barrier = pltpu.get_barrier_semaphore()
        for d in range(1, C):
            pl.semaphore_signal(barrier, inc=1, device_id={"chan": at_chan(d)}, device_id_type=pl.DeviceIdType.MESH)
        for d in range(1, T):
            pl.semaphore_signal(barrier, inc=1, device_id={"tm": at_tm(d)}, device_id_type=pl.DeviceIdType.MESH)
            pl.semaphore_signal(barrier, inc=1, device_id={"chan": twin, "tm": at_tm(d)},
                                device_id_type=pl.DeviceIdType.MESH)

    with jax.named_scope("band"):
        group = 4 * LANES
        depth = LANES + group
        row = lax.broadcasted_iota(i32, (8, LANES), 0)
        n = lax.broadcasted_iota(i32, (8, LANES), 1)
        tap = 4 * n + 3 - row
        cell = jnp.zeros((8, LANES), f32)
        loads[0].wait()
        for k in range(TAPS):
            cell = jnp.where(tap == k, taps_ref[k], cell)
        reach = TAPS // 4 + 1
        tiles = []
        for b in range(depth // 8):
            at = 2 * b - LANES // 4
            tile = jnp.zeros_like(cell)
            if at > -reach:
                tile = pltpu.roll(cell, at % LANES, 1) if at else cell
                if at < 0:
                    tile = jnp.where(n < reach, tile, 0.0)
                elif at + reach > LANES:
                    tile = jnp.where(n >= reach, tile, 0.0)
            tiles.append(tile)
        band = jnp.concatenate(tiles, axis=0)
        hi = band.astype(bf16)
        lo = (band - hi.astype(f32)).astype(bf16)
        band2 = jnp.concatenate([hi, lo], axis=1)
        for load in loads[1:]:
            load.wait()

    groups = samples // LANES
    lane = lax.broadcasted_iota(i32, (rows, LANES), 1)

    def encode(x):
        peak = jnp.maximum(jnp.max(jnp.abs(x), axis=1, keepdims=True), 1e-30)
        e = jnp.floor(jnp.log2(peak)) + 1.0
        return jnp.clip(jnp.round(x * jnp.exp2(FULL - e)), -32767.0, 32767.0).astype(i32), e

    def scaled(v):
        at = v.shape[1] - LANES + SPILL
        return v * jnp.exp2(v[:, at:at + 1] - (FULL + 1))

    def plain(x):
        return x.astype(i32).astype(f32)

    def permuted(onehot, x):
        v = x.astype(i32)
        pair = jnp.concatenate([(v >> 8).astype(f32).astype(bf16), (v & 255).astype(f32).astype(bf16)], axis=1)
        both = jnp.dot(onehot, pair, preferred_element_type=f32)
        return 256.0 * both[:, :x.shape[1]] + both[:, x.shape[1]:]

    with jax.named_scope("filter"):
        raw = rec_ref[...]
        parts = []
        for g in range(groups):
            if g == 0:
                first = jnp.zeros((rows, LANES), bf16)
            else:
                first = raw[:, group * g - LANES:group * g]
            parts.append(jnp.concatenate([first, raw[:, group * g:group * (g + 1)]], axis=1))
        both = jnp.dot(jnp.concatenate(parts, axis=0), band2, preferred_element_type=f32)
        both = both[:, :LANES] + both[:, LANES:]
        edge = jnp.dot(raw[:, group * groups - LANES:], band2[:LANES], preferred_element_type=f32)
        edge = edge[:, :LANES] + edge[:, LANES:]
        filtered = jnp.concatenate([both[rows * g:rows * (g + 1)] for g in range(groups)] + [edge], axis=1)
        rr = lax.broadcasted_iota(i32, (rows, LANES), 0)
        pick = jnp.zeros((rows, LANES), i32)
        for r in range(rows):
            pick = jnp.where(rr == r, pair_ref[0, r], pick)
        perm = jnp.where(pick[:, :rows] == lax.broadcasted_iota(i32, (rows, rows), 1), 1.0, 0.0).astype(bf16)
        q, e = encode(filtered)
        note = jnp.where(lane == SPILL, e.astype(i32), jnp.where(lane == SPILL + 1, pick, q[:, samples:])).astype(i16)
        q = q[:, :samples].astype(i16)
        own[t] = jnp.concatenate([q, note], axis=1)
        halves[0] = jnp.concatenate([q[:, :part], note], axis=1)
        halves[1] = jnp.concatenate([q[:, part:], note], axis=1)
        plane[me] = halves[side]

    with jax.named_scope("wait_greeting"):
        pl.semaphore_wait(barrier, C + 2 * T - 3)

    with jax.named_scope("send_filtered"):
        others = [d for d in range(1, C) if d != half]
        sends = [remote(own.at[t], partner.at[t], partner_s.at[0], partner_r.at[0], {"chan": at_chan(half)})]
        sends += [remote(own.at[t], own.at[t], own_s.at[d], own_r.at[d], {"tm": at_tm(d)}) for d in range(1, T)]
        sends += [remote(halves.at[lax.rem(side + d, 2)], plane.at[me], plane_s.at[d], plane_r.at[d],
                         {"chan": at_chan(d)}) for d in others]
        for s in sends:
            s.start()

    with jax.named_scope("clear"):
        wp[:, window:] = jnp.zeros((rows, wp.shape[1] - window), f32)
        wall[:, window:] = jnp.zeros((wall.shape[0], LANES), bf16)

    low = t < T // 2
    edge_dist = jnp.where(low, t, T - 1 - t)

    def near(k):
        up = jnp.where(k >= edge_dist, k + 1, k)
        slot = jnp.where(low, up, T - 1 - up)
        return slot, lax.rem(t - slot + T, T)

    relays = []

    def relay(k):
        slot, d = near(k)
        remote(own.at[slot], own.at[slot], own_s.at[d], own_r.at[d], {"tm": at_tm(d)}).wait_recv()
        s = remote(own.at[slot], partner.at[slot], partner_s.at[d], partner_r.at[d], {"chan": at_chan(half)})
        s.start()
        relays.append(s)

    with jax.named_scope("relay_first"):
        relay(0)

    with jax.named_scope("wait_plane"):
        for d in others:
            slot = at_chan(C - d)
            remote(halves.at[0], plane.at[slot], plane_s.at[d], plane_r.at[d], {"chan": at_chan(d)}).wait_recv()
        remote(own.at[t], partner.at[t], partner_s.at[0], partner_r.at[0], {"chan": at_chan(half)}).wait_recv()

    with jax.named_scope("relay_rest"):
        for k in range(1, max(1, T - 2)):
            relay(k)

    with jax.named_scope("pick"):
        mate = partner[t]
        body_half = jnp.where(side == 0, plain(mate[:, :part]), plain(mate[:, part:samples]))
        plane[at_chan(half)] = jnp.concatenate([body_half.astype(i32).astype(i16), mate[:, samples:]], axis=1)
        picked = []
        per = rows // VS

        def halved(x, within):
            y = x[:VS]
            for q in range(1, per):
                y = jnp.where(within == q, x[VS * q:VS * (q + 1)], y)
            return y

        for step in range(STEPS):
            blk = blocks_ref[step]
            owner = lax.div(blk, per)
            within = lax.rem(blk, per)
            mine = halved(plain(plane[owner]), within)
            pair = mine[:, part + SPILL + 1:part + SPILL + 2]
            onehot = jnp.where(pair == lax.broadcasted_iota(i32, (VS, rows), 1).astype(f32), 1.0, 0.0).astype(bf16)
            theirs = permuted(onehot, plane[lax.rem(owner + half, C)])
            picked.append(scaled(mine) + scaled(theirs))
        x = jnp.concatenate(picked, axis=0)
        q, e = encode(x[:, :part])
        spill, head = x[:, part:], x[:, :LANES]
        sq = jnp.where((lane < SPILL) & (side == 0), 0.0, head * head)
        for g in range(1, part // LANES):
            y = x[:, LANES * g:LANES * (g + 1)]
            sq = sq + y * y
        facts = jnp.where(lane < SPILL, spill, jnp.where(lane < 2 * SPILL, pltpu.roll(head, SPILL, 1), jnp.where(
            lane == 2 * SPILL, jnp.exp2(e - FULL), jnp.sum(sq, axis=1, keepdims=True))))
        low_lane = lane[:VS] < LANES // 2
        mine_at = 2 * t + side
        small[mine_at] = jnp.where(low_lane, facts[:VS], pltpu.roll(facts[VS:], LANES // 2, 1))
        body_[mine_at] = q.astype(i16)
        away = [(d, p) for d in range(T) for p in range(2) if d or p]

        def small_copy(d, p, at):
            where = {"tm": at_tm(d)} if p == 0 else {"chan": twin, "tm": at_tm(d)}
            return remote(small.at[at], small.at[at], small_s.at[2 * d + p], small_r.at[2 * d + p], where)

        def twin_copy(d, at):
            return remote(body_.at[at], body_.at[at], twin_s.at[d], twin_r.at[d], {"chan": twin})

        def body_copy(d, at):
            return remote(body_.at[at], body_.at[at], body_s.at[d], body_r.at[d], {"tm": at_tm(d)})

        ts_sends = [small_copy(d, p, mine_at) for d, p in away if d]
        ts_sends += [body_copy(d, mine_at) for d in range(1, T)]
        ts_sends += [small_copy(0, 1, mine_at), twin_copy(0, mine_at)]
        for s in ts_sends:
            s.start()

    with jax.named_scope("relay_last"):
        for k in range(max(1, T - 2), T - 1):
            relay(k)

    def assemble(blocks):
        out = []
        for i, x in enumerate(blocks):
            head = x[:, :LANES]
            if i:
                head = head + jnp.where(lane < SPILL, blocks[i - 1][:, samples:], 0.0)
            out.append(jnp.concatenate([head, x[:, LANES:samples]], axis=1))
        return out

    def whiten(blocks):
        acc = jnp.zeros((rows, LANES), f32)
        for x in blocks:
            sq = x * x
            for g in range(groups):
                acc = acc + sq[:, LANES * g:LANES * (g + 1)]
        scale = lax.rsqrt(jnp.sum(acc, axis=1, keepdims=True) / window + 1e-6)
        return [(x * scale).astype(bf16) for x in blocks]

    with jax.named_scope("wait_partner"):
        for k in range(T - 1):
            slot, d = near(k)
            remote(partner.at[slot], partner.at[slot], partner_s.at[d], partner_r.at[d],
                   {"chan": at_chan(half)}).wait_recv()

    with jax.named_scope("white"):
        white = whiten(assemble([scaled(plain(own[i])) + scaled(permuted(perm, partner[i])) for i in range(T)]))
        for i in range(T):
            wp[:, samples * i:samples * (i + 1)] = white[i].astype(f32)

    with jax.named_scope("wall"):
        lag0 = t * lag_dev
        wide = samples + LANES * P_
        if lag_dev % LANES == 0:
            base, rest = lag0, 0
        else:
            base = lax.div(lag0, LANES) * LANES
            rest = lax.rem(lag0, LANES)
        for i in range(T):
            wrows = wp[:, pl.ds(pl.multiple_of(i * samples + base, LANES), wide)]
            for a in range(A_):
                rolled = wrows
                if lag_dev % LANES:
                    rolled = pltpu.roll(wrows, wide - FINE * a - rest, 1)
                elif a:
                    rolled = pltpu.roll(wrows, wide - FINE * a, 1)
                for p in range(P_):
                    r0 = (p * A_ + a) * rows
                    wall[r0:r0 + rows, samples * i:samples * (i + 1)] = (
                        rolled[:, LANES * p:LANES * p + samples].astype(bf16))

    with jax.named_scope("wait_small"):
        for d, p in away:
            from_side = side if p == 0 else 1 - side
            small_copy(d, p, 2 * at_tm(T - d) + from_side).wait_recv()

    with jax.named_scope("hand_to_twin"):
        for k in range(T - 1):
            slot, d = near(k)
            body_copy(d, 2 * slot + side).wait_recv()
            s = twin_copy(d, 2 * slot + side)
            s.start()
            relays.append(s)

    with jax.named_scope("source_power"):
        def facts_of(at):
            x = small[at]
            return jnp.concatenate([x, pltpu.roll(x, LANES // 2, 1)], axis=0)

        total = jnp.zeros((rows, LANES), f32)
        before = None
        for i in range(T):
            first, second = facts_of(2 * i), facts_of(2 * i + 1)
            head = pltpu.roll(first, LANES - SPILL, 1)
            if before is not None:
                head = head + before
            before = second
            total = total + jnp.where(lane < SPILL, head * head, jnp.where(lane == 2 * SPILL + 1, first + second, 0.0))
        source_scale = lax.rsqrt(jnp.sum(total, axis=1, keepdims=True) / window + 1e-6)

    span = samples + LANES

    def term(slot):
        first, second = facts_of(2 * slot), facts_of(2 * slot + 1)
        before = jnp.where((slot > 0) & (lane < SPILL), facts_of(2 * jnp.maximum(slot, 1) - 1), 0.0)
        x = jnp.concatenate([plain(body_[2 * slot]) * first[:, 2 * SPILL:2 * SPILL + 1],
                             plain(body_[2 * slot + 1]) * second[:, 2 * SPILL:2 * SPILL + 1]], axis=1)
        x = jnp.concatenate([x[:, :LANES] + before, x[:, LANES:]], axis=1) * source_scale
        x = x.astype(bf16).astype(f32)
        srows = jnp.concatenate([x, jnp.zeros((rows, LANES), f32)], axis=1)
        xs = []
        for s in range(STEPS * VS):
            one = jnp.broadcast_to(srows[s:s + 1], (FINE, span))
            xs.append(pltpu.roll(one, 0, 1, stride=1, stride_axis=0).astype(bf16))
        ws = wall[:, pl.ds(pl.multiple_of(slot * samples, LANES), span)]
        return lax.dot_general(ws, jnp.concatenate(xs, axis=0),
                               (((1,), (1,)), ((), ())), preferred_element_type=f32)

    with jax.named_scope("wait_twin_own"):
        twin_copy(0, 2 * t + 1 - side).wait_recv()
    with jax.named_scope("correlate"):
        z = term(t)
    for k in range(T - 1):
        slot, d = near(k)
        with jax.named_scope("wait_twin"):
            twin_copy(d, 2 * slot + 1 - side).wait_recv()
        with jax.named_scope("correlate"):
            z = z + term(slot)
    z = z * (1.0 / math.sqrt(window))

    with jax.named_scope("result"):
        lane_group = lane // FINE
        per_tile = LANES // FINE
        span_out = min(lag_dev, LANES)
        for p in range(P_):
            for lo_s in range(0, STEPS * VS, per_tile):
                turned = []
                for a in range(A_):
                    r0 = (p * A_ + a) * rows
                    tile = z[r0:r0 + rows, lo_s * FINE:lo_s * FINE + LANES]
                    turned.append(pltpu.roll(tile, FINE * a, 1) if a else tile)
                for s in range(per_tile):
                    o = turned[0]
                    for a in range(1, A_):
                        o = jnp.where(lane_group == (s + a) % per_tile, turned[a], o)
                    if s:
                        o = pltpu.roll(o, LANES - FINE * s, 1)
                    out_ref[lo_s + s, :, LANES * p:LANES * p + span_out] = o[:, :span_out]

    with jax.named_scope("wait_sends"):
        for s in sends + relays + ts_sends:
            s.wait_send()


def shards(records, pair_rows, fir_taps, source_blocks):
    C = lax.axis_size("chan")
    T = lax.axis_size("tm")
    rows, raw = records.shape
    samples = raw // 4
    f32, bf16, i16 = jnp.float32, jnp.bfloat16, jnp.int16
    dma = pltpu.SemaphoreType.DMA
    hbm = pl.BlockSpec(memory_space=pltpu.HBM)
    operands = [pltpu.with_memory_space_constraint(x, pltpu.HBM)
                for x in (fir_taps, pair_rows, source_blocks, records)]
    out = pl.pallas_call(
        functools.partial(body, C, T, rows),
        out_shape=pltpu.VMEM((STEPS * VS, rows, LAGS // T), f32),
        in_specs=[hbm] * 4,
        out_specs=pl.BlockSpec(memory_space=pltpu.VMEM),
        scratch_shapes=[
            pltpu.SMEM(fir_taps.shape, f32),
            pltpu.SMEM(pair_rows.shape, jnp.int32),
            pltpu.SMEM(source_blocks.shape, jnp.int32),
            pltpu.VMEM(records.shape, bf16),
            dma((4,)),
            pltpu.VMEM((2, rows, samples // 2 + LANES), i16),
            pltpu.VMEM((C, rows, samples // 2 + LANES), i16),
            pltpu.VMEM((T, rows, samples + LANES), i16),
            pltpu.VMEM((T, rows, samples + LANES), i16),
            pltpu.VMEM((2 * T, VS, LANES), f32),
            pltpu.VMEM((2 * T, rows, samples // 2), i16),
            pltpu.VMEM((rows, T * samples + LAGS + LANES), f32),
            pltpu.VMEM((LAGS // T // FINE * rows, T * samples + LANES), bf16),
            dma((C,)), dma((C,)), dma((T,)), dma((T,)), dma((T,)), dma((T,)),
            dma((2 * T,)), dma((2 * T,)), dma((T,)), dma((T,)), dma((T,)), dma((T,)),
        ],
        compiler_params=pltpu.CompilerParams(
            collective_id=0, has_side_effects=True,
            vmem_limit_bytes=(24 if samples * T <= 8192 else 60) * 2**20),
        cost_estimate=pl.CostEstimate(flops=600_000_000, bytes_accessed=1_000_000, transcendentals=0),
    )(*operands)
    return out.reshape(STEPS, VS, rows, LAGS // T)


def solution(mesh):
    return jax.shard_map(
        shards,
        mesh=mesh,
        in_specs=(P("chan", "tm"), P("chan", None), P(), P()),
        out_specs=P(None, None, "chan", "tm"),
        check_vma=False,
    )
```

```python
import functools
import math

import jax
import jax.numpy as jnp
from jax import lax
from jax.experimental import pallas as pl
from jax.experimental.pallas import tpu as pltpu
from jax.sharding import PartitionSpec as P

VS = 8
STEPS = 2
LAGS = 1024
TAPS = 32
LANES = 128
FINE = 16
SPILL = TAPS // 4
FULL = 15


def body(C, T, rows, taps_hbm, pair_hbm, blocks_hbm, rec_hbm, out_ref,
         taps_ref, pair_ref, blocks_ref, rec_ref, local_s,
         full, mate, halves, plane, own, partner, facts_w, facts_s, part_s, wp, wall, src,
         plane_s, plane_r, own_s, own_r, mate_s, mate_r, partner_s, partner_r, fw_s, fw_r, fs_s, fs_r,
         body_s, body_r, twin_s, twin_r):
    me = lax.axis_index("chan")
    t = lax.axis_index("tm")
    f32, bf16, i16, i32 = jnp.float32, jnp.bfloat16, jnp.int16, jnp.int32
    samples = rec_ref.shape[1] // 4
    width = samples + LANES
    part = samples // 2
    half = C // 2
    side = lax.rem(me, 2)
    twin = me + 1 - 2 * side
    lag_dev = LAGS // T
    P_ = max(1, lag_dev // LANES)
    A_ = min(lag_dev, LANES) // FINE
    window = samples * T

    def at_chan(d):
        return lax.rem(me + d, C)

    def at_tm(d):
        return lax.rem(t + d, T)

    def remote(src, dst, ssem, rsem, where):
        return pltpu.make_async_remote_copy(
            src_ref=src, dst_ref=dst, send_sem=ssem, recv_sem=rsem,
            device_id=where, device_id_type=pl.DeviceIdType.MESH)

    with jax.named_scope("greet"):
        loads = [pltpu.make_async_copy(src, dst, local_s.at[i]) for i, (src, dst) in enumerate((
            (taps_hbm, taps_ref), (rec_hbm, rec_ref), (pair_hbm, pair_ref), (blocks_hbm, blocks_ref)))]
        for load in loads:
            load.start()
        barrier = pltpu.get_barrier_semaphore()
        for d in range(1, C):
            pl.semaphore_signal(barrier, inc=1, device_id={"chan": at_chan(d)}, device_id_type=pl.DeviceIdType.MESH)
        for d in range(1, T):
            pl.semaphore_signal(barrier, inc=1, device_id={"tm": at_tm(d)}, device_id_type=pl.DeviceIdType.MESH)
            pl.semaphore_signal(barrier, inc=1, device_id={"chan": twin, "tm": at_tm(d)},
                                device_id_type=pl.DeviceIdType.MESH)

    with jax.named_scope("band"):
        group = 4 * LANES
        depth = LANES + group
        row = lax.broadcasted_iota(i32, (8, LANES), 0)
        n = lax.broadcasted_iota(i32, (8, LANES), 1)
        tap = 4 * n + 3 - row
        cell = jnp.zeros((8, LANES), f32)
    with jax.named_scope("load_taps"):
        loads[0].wait()
    with jax.named_scope("band_tiles"):
        for k in range(TAPS):
            cell = jnp.where(tap == k, taps_ref[k], cell)
        reach = TAPS // 4 + 1
        tiles = []
        for b in range(depth // 8):
            at = 2 * b - LANES // 4
            tile = jnp.zeros_like(cell)
            if at > -reach:
                tile = pltpu.roll(cell, at % LANES, 1) if at else cell
                if at < 0:
                    tile = jnp.where(n < reach, tile, 0.0)
                elif at + reach > LANES:
                    tile = jnp.where(n >= reach, tile, 0.0)
            tiles.append(tile)
        band = jnp.concatenate(tiles, axis=0)
        hi = band.astype(bf16)
        lo = (band - hi.astype(f32)).astype(bf16)
        band2 = jnp.concatenate([hi, lo], axis=1)
    with jax.named_scope("load_records"):
        for load in loads[1:]:
            load.wait()

    groups = samples // LANES
    lane = lax.broadcasted_iota(i32, (rows, LANES), 1)

    def encode(x):
        peak = jnp.maximum(jnp.max(jnp.abs(x), axis=1, keepdims=True), 1e-30)
        e = jnp.floor(jnp.log2(peak)) + 1.0
        return jnp.clip(jnp.round(x * jnp.exp2(FULL - e)), -32767.0, 32767.0).astype(i32), e

    def scaled(v):
        at = v.shape[1] - LANES + SPILL
        return v * jnp.exp2(v[:, at:at + 1] - (FULL + 1))

    def plain(x):
        return x.astype(i32).astype(f32)

    def permuted(onehot, x):
        v = x.astype(i32)
        pair = jnp.concatenate([(v >> 8).astype(f32).astype(bf16), (v & 255).astype(f32).astype(bf16)], axis=1)
        both = jnp.dot(onehot, pair, preferred_element_type=f32)
        return 256.0 * both[:, :x.shape[1]] + both[:, x.shape[1]:]

    with jax.named_scope("filter"):
        raw = rec_ref[...]
        parts = []
        for g in range(groups):
            if g == 0:
                first = jnp.zeros((rows, LANES), bf16)
            else:
                first = raw[:, group * g - LANES:group * g]
            parts.append(jnp.concatenate([first, raw[:, group * g:group * (g + 1)]], axis=1))
        both = jnp.dot(jnp.concatenate(parts, axis=0), band2, preferred_element_type=f32)
        both = both[:, :LANES] + both[:, LANES:]
        edge = jnp.dot(raw[:, group * groups - LANES:], band2[:LANES], preferred_element_type=f32)
        edge = edge[:, :LANES] + edge[:, LANES:]
        filtered = jnp.concatenate([both[rows * g:rows * (g + 1)] for g in range(groups)] + [edge], axis=1)
        rr = lax.broadcasted_iota(i32, (rows, LANES), 0)
        pick = jnp.zeros((rows, LANES), i32)
        for r in range(rows):
            pick = jnp.where(rr == r, pair_ref[0, r], pick)
        perm = jnp.where(pick[:, :rows] == lax.broadcasted_iota(i32, (rows, rows), 1), 1.0, 0.0).astype(bf16)
        q, e = encode(filtered)
        note = jnp.where(lane == SPILL, e.astype(i32), jnp.where(lane == SPILL + 1, pick, q[:, samples:])).astype(i16)
        q = q[:, :samples].astype(i16)
        own[t] = q
        full[...] = jnp.concatenate([q, note], axis=1)
        halves[0] = jnp.concatenate([q[:, :part], note], axis=1)
        halves[1] = jnp.concatenate([q[:, part:], note], axis=1)
        plane[me] = halves[side]

    with jax.named_scope("wait_greeting"):
        pl.semaphore_wait(barrier, C + 2 * T - 3)

    with jax.named_scope("send_filtered"):
        others = [d for d in range(1, C) if d != half]
        mate_copy = remote(full, mate, mate_s, mate_r, {"chan": at_chan(half)})
        sends = [mate_copy]
        sends += [remote(own.at[t], own.at[t], own_s.at[d], own_r.at[d], {"tm": at_tm(d)}) for d in range(1, T)]
        sends += [remote(halves.at[lax.rem(side + d, 2)], plane.at[me], plane_s.at[d], plane_r.at[d],
                         {"chan": at_chan(d)}) for d in others]
        for s in sends:
            s.start()

    with jax.named_scope("clear"):
        wp[:, window:] = jnp.zeros((rows, wp.shape[1] - window), f32)
        wall[:, window:] = jnp.zeros((wall.shape[0], LANES), bf16)
        src[:, :, samples:] = jnp.zeros((T, rows, LANES), f32)

    low = t < T // 2
    edge_dist = jnp.where(low, t, T - 1 - t)

    def near(k):
        up = jnp.where(k >= edge_dist, k + 1, k)
        slot = jnp.where(low, up, T - 1 - up)
        return slot, lax.rem(t - slot + T, T)

    relays = []

    def relay(k):
        slot, d = near(k)
        remote(own.at[slot], own.at[slot], own_s.at[d], own_r.at[d], {"tm": at_tm(d)}).wait_recv()
        s = remote(own.at[slot], partner.at[slot], partner_s.at[d], partner_r.at[d], {"chan": at_chan(half)})
        s.start()
        relays.append(s)

    def tile_of(spill, head, scale, other, power):
        x = jnp.where(lane < SPILL, spill, jnp.where(lane < 2 * SPILL, pltpu.roll(head, SPILL, 1), jnp.where(
            lane == 2 * SPILL, scale, jnp.where(lane == 2 * SPILL + 1, other, power))))
        return jnp.where(lane[:VS] < LANES // 2, x[:VS], pltpu.roll(x[VS:], LANES // 2, 1))

    def facts(ref, at):
        x = ref[at]
        return jnp.concatenate([x, pltpu.roll(x, LANES // 2, 1)], axis=0)

    def power_of(x, skip):
        sq = jnp.where((lane < SPILL) & skip, 0.0, x[:, :LANES] * x[:, :LANES])
        for g in range(1, x.shape[1] // LANES):
            y = x[:, LANES * g:LANES * (g + 1)]
            sq = sq + y * y
        return jnp.sum(sq, axis=1, keepdims=True)

    def whitening(ref, each):
        total = jnp.zeros((rows, LANES), f32)
        before = None
        for i in range(T):
            first = facts(ref, each * i)
            final = facts(ref, each * i + each - 1)
            head = pltpu.roll(first, LANES - SPILL, 1)
            if before is not None:
                head = head + before
            before = final
            total = total + jnp.where(lane < SPILL, head * head, jnp.where(
                lane == 2 * SPILL + 2, first + final if each > 1 else first, 0.0))
        return lax.rsqrt(jnp.sum(total, axis=1, keepdims=True) / window + 1e-6)

    def spilled(ref, each, slot):
        return jnp.where((slot > 0) & (lane < SPILL), facts(ref, each * jnp.maximum(slot, 1) - 1), 0.0)

    def fw_copy(d, at):
        return remote(facts_w.at[at], facts_w.at[at], fw_s.at[d], fw_r.at[d], {"tm": at_tm(d)})

    with jax.named_scope("wait_mate"):
        mate_copy.wait_recv()

    with jax.named_scope("own_facts"):
        partner[t] = mate[:, :samples]
        theirs = permuted(perm, mate[...])
        mine_scale = jnp.exp2(e - (FULL + 1))
        mate_scale = jnp.exp2(theirs[:, samples + SPILL:samples + SPILL + 1] - (FULL + 1))
        x = plain(full[...]) * mine_scale + theirs * mate_scale
        facts_w[t] = tile_of(x[:, samples:], x[:, :LANES], mine_scale, mate_scale, power_of(x[:, :samples], True))
        fw_sends = [fw_copy(d, t) for d in range(1, T)]
        for s in fw_sends:
            s.start()
        body_half = jnp.where(side == 0, plain(mate[:, :part]), plain(mate[:, part:samples]))
        plane[at_chan(half)] = jnp.concatenate([body_half.astype(i32).astype(i16), mate[:, samples:]], axis=1)

    with jax.named_scope("relay_first"):
        relay(0)

    with jax.named_scope("wait_plane"):
        for d in others:
            slot = at_chan(C - d)
            remote(halves.at[0], plane.at[slot], plane_s.at[d], plane_r.at[d], {"chan": at_chan(d)}).wait_recv()

    with jax.named_scope("relay_rest"):
        for k in range(1, max(1, T - 2)):
            relay(k)

    with jax.named_scope("pick"):
        picked = []
        per = rows // VS

        def halved(x, within):
            y = x[:VS]
            for q in range(1, per):
                y = jnp.where(within == q, x[VS * q:VS * (q + 1)], y)
            return y

        for step in range(STEPS):
            blk = blocks_ref[step]
            owner = lax.div(blk, per)
            within = lax.rem(blk, per)
            mine = halved(plain(plane[owner]), within)
            pair = mine[:, part + SPILL + 1:part + SPILL + 2]
            onehot = jnp.where(pair == lax.broadcasted_iota(i32, (VS, rows), 1).astype(f32), 1.0, 0.0).astype(bf16)
            theirs = permuted(onehot, plane[lax.rem(owner + half, C)])
            picked.append(scaled(mine) + scaled(theirs))
        x = jnp.concatenate(picked, axis=0)
        q, e = encode(x[:, :part])
        mine_at = 2 * t + side
        facts_s[mine_at] = tile_of(x[:, part:], x[:, :LANES], jnp.exp2(e - FULL), 0.0, power_of(x[:, :part], side == 0))
        part_s[mine_at] = q.astype(i16)
        away = [(d, p) for d in range(T) for p in range(2) if d or p]

        def small_copy(d, p, at):
            where = {"tm": at_tm(d)} if p == 0 else {"chan": twin, "tm": at_tm(d)}
            return remote(facts_s.at[at], facts_s.at[at], fs_s.at[2 * d + p], fs_r.at[2 * d + p], where)

        def twin_copy(d, at):
            return remote(part_s.at[at], part_s.at[at], twin_s.at[d], twin_r.at[d], {"chan": twin})

        def body_copy(d, at):
            return remote(part_s.at[at], part_s.at[at], body_s.at[d], body_r.at[d], {"tm": at_tm(d)})

        ts_sends = [small_copy(d, p, mine_at) for d, p in away if d]
        ts_sends += [body_copy(d, mine_at) for d in range(1, T)]
        ts_sends += [small_copy(0, 1, mine_at), twin_copy(0, mine_at)]
        for s in ts_sends:
            s.start()

    with jax.named_scope("relay_last"):
        for k in range(max(1, T - 2), T - 1):
            relay(k)

    lag0 = t * lag_dev
    wide = samples + LANES * P_
    span = samples + LANES
    if lag_dev % LANES == 0:
        base, rest = lag0, 0
    else:
        base = lax.div(lag0, LANES) * LANES
        rest = lax.rem(lag0, LANES)

    def at_block(slot):
        return pl.multiple_of(slot * samples, LANES)

    def white(slot):
        tile = facts(facts_w, slot)
        x = (plain(own[slot]) * tile[:, 2 * SPILL:2 * SPILL + 1]
             + permuted(perm, partner[slot]) * tile[:, 2 * SPILL + 1:2 * SPILL + 2])
        x = jnp.concatenate([x[:, :LANES] + spilled(facts_w, 1, slot), x[:, LANES:]], axis=1)
        wp[:, pl.ds(at_block(slot), samples)] = (x * scale_w).astype(bf16).astype(f32)

    def turn(slot):
        wrows = wp[:, pl.ds(pl.multiple_of(slot * samples + base, LANES), wide)]
        for a in range(A_):
            rolled = wrows
            if lag_dev % LANES:
                rolled = pltpu.roll(wrows, wide - FINE * a - rest, 1)
            elif a:
                rolled = pltpu.roll(wrows, wide - FINE * a, 1)
            for p in range(P_):
                r0 = (p * A_ + a) * rows
                wall[r0:r0 + rows, pl.ds(at_block(slot), samples)] = (
                    rolled[:, LANES * p:LANES * p + samples].astype(bf16))

    def source(slot):
        first, second = facts(facts_s, 2 * slot), facts(facts_s, 2 * slot + 1)
        x = jnp.concatenate([plain(part_s[2 * slot]) * first[:, 2 * SPILL:2 * SPILL + 1],
                             plain(part_s[2 * slot + 1]) * second[:, 2 * SPILL:2 * SPILL + 1]], axis=1)
        x = jnp.concatenate([x[:, :LANES] + spilled(facts_s, 2, slot), x[:, LANES:]], axis=1)
        src[slot, :, :samples] = (x * scale_s).astype(bf16).astype(f32)

    def term(slot):
        xs = []
        for s in range(STEPS * VS):
            one = jnp.broadcast_to(src[slot, s:s + 1, :], (FINE, span))
            xs.append(pltpu.roll(one, 0, 1, stride=1, stride_axis=0).astype(bf16))
        ws = wall[:, pl.ds(at_block(slot), span)]
        return lax.dot_general(ws, jnp.concatenate(xs, axis=0),
                               (((1,), (1,)), ((), ())), preferred_element_type=f32)

    def wait_partner(k):
        slot, d = near(k)
        remote(partner.at[slot], partner.at[slot], partner_s.at[d], partner_r.at[d],
               {"chan": at_chan(half)}).wait_recv()

    def hand_to_twin(k):
        slot, d = near(k)
        body_copy(d, 2 * slot + side).wait_recv()
        s = twin_copy(d, 2 * slot + side)
        s.start()
        relays.append(s)

    def wait_twin(k):
        slot, d = near(k)
        twin_copy(d, 2 * slot + 1 - side).wait_recv()

    with jax.named_scope("wait_own_facts"):
        for d in range(1, T):
            fw_copy(d, at_tm(T - d)).wait_recv()
        scale_w = whitening(facts_w, 1)
    with jax.named_scope("white_own"):
        white(t)
    for k in range(T - 2):
        with jax.named_scope("wait_partner"):
            wait_partner(k)
        with jax.named_scope("white"):
            white(near(k)[0])
    start = jnp.where(low, 0, 2)
    with jax.named_scope("turn"):
        for i in range(T - 2):
            turn(start + i)
    with jax.named_scope("wait_source_facts"):
        for d, p in away:
            from_side = side if p == 0 else 1 - side
            small_copy(d, p, 2 * at_tm(T - d) + from_side).wait_recv()
        scale_s = whitening(facts_s, 2)
    with jax.named_scope("hand_to_twin"):
        for k in range(T - 1):
            hand_to_twin(k)
    with jax.named_scope("wait_partner"):
        wait_partner(T - 2)
    with jax.named_scope("white"):
        white(near(T - 2)[0])
    with jax.named_scope("turn"):
        for i in range(2):
            turn(jnp.where(low, T - 2, 0) + i)
    with jax.named_scope("wait_twin"):
        twin_copy(0, 2 * t + 1 - side).wait_recv()
        for k in range(T - 2):
            wait_twin(k)
    with jax.named_scope("source"):
        source(t)
        for k in range(T - 2):
            source(near(k)[0])
    with jax.named_scope("correlate"):
        z = term(start)
        for i in range(1, T - 2):
            z = z + term(start + i)
    with jax.named_scope("wait_twin"):
        wait_twin(T - 2)
    with jax.named_scope("source"):
        source(near(T - 2)[0])
    with jax.named_scope("correlate"):
        for i in range(2):
            z = z + term(jnp.where(low, T - 2, 0) + i)
        z = z * (1.0 / math.sqrt(window))

    with jax.named_scope("result"):
        lane_group = lane // FINE
        per_tile = LANES // FINE
        span_out = min(lag_dev, LANES)
        for p in range(P_):
            for lo_s in range(0, STEPS * VS, per_tile):
                turned = []
                for a in range(A_):
                    r0 = (p * A_ + a) * rows
                    tile = z[r0:r0 + rows, lo_s * FINE:lo_s * FINE + LANES]
                    turned.append(pltpu.roll(tile, FINE * a, 1) if a else tile)
                for s in range(per_tile):
                    o = turned[0]
                    for a in range(1, A_):
                        o = jnp.where(lane_group == (s + a) % per_tile, turned[a], o)
                    if s:
                        o = pltpu.roll(o, LANES - FINE * s, 1)
                    out_ref[lo_s + s, :, LANES * p:LANES * p + span_out] = o[:, :span_out]

    with jax.named_scope("wait_sends"):
        for s in sends + fw_sends + relays + ts_sends:
            s.wait_send()


def shards(records, pair_rows, fir_taps, source_blocks):
    C = lax.axis_size("chan")
    T = lax.axis_size("tm")
    rows, raw = records.shape
    samples = raw // 4
    f32, bf16, i16 = jnp.float32, jnp.bfloat16, jnp.int16
    dma = pltpu.SemaphoreType.DMA
    hbm = pl.BlockSpec(memory_space=pltpu.HBM)
    operands = [pltpu.with_memory_space_constraint(x, pltpu.HBM)
                for x in (fir_taps, pair_rows, source_blocks, records)]
    out = pl.pallas_call(
        functools.partial(body, C, T, rows),
        out_shape=pltpu.VMEM((STEPS * VS, rows, LAGS // T), f32),
        in_specs=[hbm] * 4,
        out_specs=pl.BlockSpec(memory_space=pltpu.VMEM),
        scratch_shapes=[
            pltpu.SMEM(fir_taps.shape, f32),
            pltpu.SMEM(pair_rows.shape, jnp.int32),
            pltpu.SMEM(source_blocks.shape, jnp.int32),
            pltpu.VMEM(records.shape, bf16),
            dma((4,)),
            pltpu.VMEM((rows, samples + LANES), i16),
            pltpu.VMEM((rows, samples + LANES), i16),
            pltpu.VMEM((2, rows, samples // 2 + LANES), i16),
            pltpu.VMEM((C, rows, samples // 2 + LANES), i16),
            pltpu.VMEM((T, rows, samples), i16),
            pltpu.VMEM((T, rows, samples), i16),
            pltpu.VMEM((T, VS, LANES), f32),
            pltpu.VMEM((2 * T, VS, LANES), f32),
            pltpu.VMEM((2 * T, rows, samples // 2), i16),
            pltpu.VMEM((rows, T * samples + LAGS + LANES), f32),
            pltpu.VMEM((LAGS // T // FINE * rows, T * samples + LANES), bf16),
            pltpu.VMEM((T, rows, samples + LANES), f32),
            dma((C,)), dma((C,)), dma((T,)), dma((T,)), dma, dma, dma((T,)), dma((T,)), dma((T,)), dma((T,)),
            dma((2 * T,)), dma((2 * T,)), dma((T,)), dma((T,)), dma((T,)), dma((T,)),
        ],
        compiler_params=pltpu.CompilerParams(
            collective_id=0, has_side_effects=True,
            vmem_limit_bytes=(24 if samples * T <= 8192 else 60) * 2**20),
        cost_estimate=pl.CostEstimate(flops=600_000_000, bytes_accessed=1_000_000, transcendentals=0),
    )(*operands)
    return out.reshape(STEPS, VS, rows, LAGS // T)


def solution(mesh):
    return jax.shard_map(
        shards,
        mesh=mesh,
        in_specs=(P("chan", "tm"), P("chan", None), P(), P()),
        out_specs=P(None, None, "chan", "tm"),
        check_vma=False,
    )
```

```python
import functools
import math

import jax
import jax.numpy as jnp
from jax import lax
from jax.experimental import pallas as pl
from jax.experimental.pallas import tpu as pltpu
from jax.sharding import PartitionSpec as P

VS = 8
STEPS = 2
LAGS = 1024
TAPS = 32
LANES = 128
FINE = 16
SPILL = TAPS // 4
FULL = 15


def body(C, T, rows, taps_hbm, pair_hbm, blocks_hbm, rec_hbm, out_ref,
         taps_ref, pair_ref, blocks_ref, rec_ref, local_s,
         halves, plane, own, partner, part_s, wp, wall,
         plane_s, plane_r, own_s, own_r, partner_s, partner_r,
         body_s, body_r, twin_s, twin_r):
    me = lax.axis_index("chan")
    t = lax.axis_index("tm")
    f32, bf16, i16, i32 = jnp.float32, jnp.bfloat16, jnp.int16, jnp.int32
    samples = rec_ref.shape[1] // 4
    width = samples + LANES
    part = samples // 2
    half = C // 2
    side = lax.rem(me, 2)
    twin = me + 1 - 2 * side
    lag_dev = LAGS // T
    P_ = max(1, lag_dev // LANES)
    A_ = min(lag_dev, LANES) // FINE
    window = samples * T

    def at_chan(d):
        return lax.rem(me + d, C)

    def at_tm(d):
        return lax.rem(t + d, T)

    def remote(src, dst, ssem, rsem, where):
        return pltpu.make_async_remote_copy(
            src_ref=src, dst_ref=dst, send_sem=ssem, recv_sem=rsem,
            device_id=where, device_id_type=pl.DeviceIdType.MESH)

    with jax.named_scope("greet"):
        loads = [pltpu.make_async_copy(src, dst, local_s.at[i]) for i, (src, dst) in enumerate((
            (taps_hbm, taps_ref), (rec_hbm, rec_ref), (pair_hbm, pair_ref), (blocks_hbm, blocks_ref)))]
        for load in loads:
            load.start()
        barrier = pltpu.get_barrier_semaphore()
        for d in range(1, C):
            pl.semaphore_signal(barrier, inc=1, device_id={"chan": at_chan(d)}, device_id_type=pl.DeviceIdType.MESH)
        for d in range(1, T):
            pl.semaphore_signal(barrier, inc=1, device_id={"tm": at_tm(d)}, device_id_type=pl.DeviceIdType.MESH)

    with jax.named_scope("band"):
        group = 4 * LANES
        depth = LANES + group
        row = lax.broadcasted_iota(i32, (8, LANES), 0)
        n = lax.broadcasted_iota(i32, (8, LANES), 1)
        tap = 4 * n + 3 - row
        cell = jnp.zeros((8, LANES), f32)
    with jax.named_scope("load_taps"):
        loads[0].wait()
    with jax.named_scope("band_tiles"):
        for k in range(TAPS):
            cell = jnp.where(tap == k, taps_ref[k], cell)
        reach = TAPS // 4 + 1
        tiles = []
        for b in range(depth // 8):
            at = 2 * b - LANES // 4
            tile = jnp.zeros_like(cell)
            if at > -reach:
                tile = pltpu.roll(cell, at % LANES, 1) if at else cell
                if at < 0:
                    tile = jnp.where(n < reach, tile, 0.0)
                elif at + reach > LANES:
                    tile = jnp.where(n >= reach, tile, 0.0)
            tiles.append(tile)
        band = jnp.concatenate(tiles, axis=0)
        hi = band.astype(bf16)
        lo = (band - hi.astype(f32)).astype(bf16)
        band2 = jnp.concatenate([hi, lo], axis=1)
    with jax.named_scope("load_records"):
        for load in loads[1:]:
            load.wait()

    groups = samples // LANES
    lane = lax.broadcasted_iota(i32, (rows, LANES), 1)

    def encode(x):
        peak = jnp.maximum(jnp.max(jnp.abs(x), axis=1, keepdims=True), 1e-30)
        e = jnp.floor(jnp.log2(peak)) + 1.0
        return jnp.clip(jnp.round(x * jnp.exp2(FULL - e)), -32767.0, 32767.0).astype(i32), e

    def scaled(v):
        at = v.shape[1] - LANES + SPILL
        return v * jnp.exp2(v[:, at:at + 1] - (FULL + 1))

    def plain(x):
        return x.astype(i32).astype(f32)

    def permuted(onehot, x):
        v = x.astype(i32)
        pair = jnp.concatenate([(v >> 8).astype(f32).astype(bf16), (v & 255).astype(f32).astype(bf16)], axis=1)
        both = jnp.dot(onehot, pair, preferred_element_type=f32)
        return 256.0 * both[:, :x.shape[1]] + both[:, x.shape[1]:]

    with jax.named_scope("filter"):
        raw = rec_ref[...]
        parts = []
        for g in range(groups):
            if g == 0:
                first = jnp.zeros((rows, LANES), bf16)
            else:
                first = raw[:, group * g - LANES:group * g]
            parts.append(jnp.concatenate([first, raw[:, group * g:group * (g + 1)]], axis=1))
        both = jnp.dot(jnp.concatenate(parts, axis=0), band2, preferred_element_type=f32)
        both = both[:, :LANES] + both[:, LANES:]
        edge = jnp.dot(raw[:, group * groups - LANES:], band2[:LANES], preferred_element_type=f32)
        edge = edge[:, :LANES] + edge[:, LANES:]
        filtered = jnp.concatenate([both[rows * g:rows * (g + 1)] for g in range(groups)] + [edge], axis=1)
        rr = lax.broadcasted_iota(i32, (rows, LANES), 0)
        pick = jnp.zeros((rows, LANES), i32)
        for r in range(rows):
            pick = jnp.where(rr == r, pair_ref[0, r], pick)
        perm = jnp.where(pick[:, :rows] == lax.broadcasted_iota(i32, (rows, rows), 1), 1.0, 0.0).astype(bf16)
        q, e = encode(filtered)
        note = jnp.where(lane == SPILL, e.astype(i32), jnp.where(lane == SPILL + 1, pick, q[:, samples:])).astype(i16)
        q = q[:, :samples].astype(i16)
        own[t] = jnp.concatenate([q, note], axis=1)
        halves[0] = jnp.concatenate([q[:, :part], note], axis=1)
        halves[1] = jnp.concatenate([q[:, part:], note], axis=1)
        plane[me] = halves[side]

    with jax.named_scope("wait_greeting"):
        pl.semaphore_wait(barrier, C + T - 2)

    with jax.named_scope("send_filtered"):
        others = [d for d in range(1, C) if d != half]
        mate_copy = remote(own.at[t], partner.at[t], partner_s.at[0], partner_r.at[0], {"chan": at_chan(half)})
        sends = [mate_copy]
        sends += [remote(halves.at[lax.rem(side + d, 2)], plane.at[me], plane_s.at[d], plane_r.at[d],
                         {"chan": at_chan(d)}) for d in others]
        sends += [remote(own.at[t], own.at[t], own_s.at[d], own_r.at[d], {"tm": at_tm(d)}) for d in range(1, T)]
        for s in sends:
            s.start()

    with jax.named_scope("clear"):
        wp[:, window:] = jnp.zeros((rows, wp.shape[1] - window), f32)
        wall[:, window:] = jnp.zeros((wall.shape[0], LANES), bf16)

    low = t < T // 2
    def near(k):
        up = jnp.where(k >= t, k + 1, k)
        slot = jnp.where(low, up, lax.rem(t - 1 - k + T, T))
        return slot, lax.rem(t - slot + T, T)

    relays = []

    def relay(k):
        slot, d = near(k)
        remote(own.at[slot], own.at[slot], own_s.at[d], own_r.at[d], {"tm": at_tm(d)}).wait_recv()
        s = remote(own.at[slot], partner.at[slot], partner_s.at[d], partner_r.at[d], {"chan": at_chan(half)})
        s.start()
        relays.append(s)

    with jax.named_scope("wait_mate"):
        mate_copy.wait_recv()

    def combine(slot):
        return scaled(plain(own[slot])) + scaled(permuted(perm, partner[slot]))

    with jax.named_scope("own_block"):
        mate = partner[t]
        body_half = jnp.where(side == 0, plain(mate[:, :part]), plain(mate[:, part:samples]))
        plane[at_chan(half)] = jnp.concatenate([body_half.astype(i32).astype(i16), mate[:, samples:]], axis=1)

    with jax.named_scope("relay_first"):
        relay(0)

    with jax.named_scope("wait_plane"):
        for d in others:
            slot = at_chan(C - d)
            remote(halves.at[0], plane.at[slot], plane_s.at[d], plane_r.at[d], {"chan": at_chan(d)}).wait_recv()

    with jax.named_scope("pick"):
        picked = []
        per = rows // VS

        def halved(x, within):
            y = x[:VS]
            for q in range(1, per):
                y = jnp.where(within == q, x[VS * q:VS * (q + 1)], y)
            return y

        for step in range(STEPS):
            blk = blocks_ref[step]
            owner = lax.div(blk, per)
            within = lax.rem(blk, per)
            mine = halved(plain(plane[owner]), within)
            pair = mine[:, part + SPILL + 1:part + SPILL + 2]
            onehot = jnp.where(pair == lax.broadcasted_iota(i32, (VS, rows), 1).astype(f32), 1.0, 0.0).astype(bf16)
            theirs = permuted(onehot, plane[lax.rem(owner + half, C)])
            picked.append(scaled(mine) + scaled(theirs))
        x = jnp.concatenate(picked, axis=0)
        q, e = encode(x)
        last = jnp.where(lane == SPILL, e.astype(i32), q[:, part:])
        mine_at = 2 * t + side
        part_s[mine_at] = jnp.concatenate([q[:, :part], last], axis=1).astype(i16)

        def twin_copy(d, at):
            return remote(part_s.at[at], part_s.at[at], twin_s.at[d], twin_r.at[d], {"chan": twin})

        def body_copy(d, at):
            return remote(part_s.at[at], part_s.at[at], body_s.at[d], body_r.at[d], {"tm": at_tm(d)})

        ts_sends = [body_copy(d, mine_at) for d in range(1, T)] + [twin_copy(0, mine_at)]
        for s in ts_sends:
            s.start()

    with jax.named_scope("relay"):
        for k in range(1, T - 1):
            relay(k)

    lag0 = t * lag_dev
    wide = samples + LANES * P_
    span = samples + LANES
    if lag_dev % LANES == 0:
        base, rest = lag0, 0
    else:
        base = lax.div(lag0, LANES) * LANES
        rest = lax.rem(lag0, LANES)

    def wait_partner(k):
        slot, d = near(k)
        remote(partner.at[slot], partner.at[slot], partner_s.at[d], partner_r.at[d],
               {"chan": at_chan(half)}).wait_recv()

    def hand_to_twin(k):
        slot, d = near(k)
        body_copy(d, 2 * slot + side).wait_recv()
        s = twin_copy(d, 2 * slot + side)
        s.start()
        relays.append(s)

    def wait_twin(k):
        slot, d = near(k)
        twin_copy(d, 2 * slot + 1 - side).wait_recv()

    def assemble(blocks):
        out = []
        for i, x in enumerate(blocks):
            head = x[:, :LANES]
            if i:
                head = head + jnp.where(lane < SPILL, blocks[i - 1][:, samples:], 0.0)
            out.append(jnp.concatenate([head, x[:, LANES:samples]], axis=1))
        return out

    def whiten(blocks):
        acc = jnp.zeros((rows, LANES), f32)
        for x in blocks:
            sq = x * x
            for g in range(groups):
                acc = acc + sq[:, LANES * g:LANES * (g + 1)]
        scale = lax.rsqrt(jnp.sum(acc, axis=1, keepdims=True) / window + 1e-6)
        return [(x * scale).astype(bf16).astype(f32) for x in blocks]

    with jax.named_scope("hand_to_twin"):
        for k in range(T - 1):
            hand_to_twin(k)
    with jax.named_scope("wait_partner"):
        for k in range(T - 1):
            wait_partner(k)
    with jax.named_scope("white"):
        white = whiten(assemble([combine(i) for i in range(T)]))
        for i in range(T):
            wp[:, samples * i:samples * (i + 1)] = white[i]
    with jax.named_scope("turn"):
        for i in range(T):
            wrows = wp[:, pl.ds(pl.multiple_of(i * samples + base, LANES), wide)]
            for a in range(A_):
                rolled = wrows
                if lag_dev % LANES:
                    rolled = pltpu.roll(wrows, wide - FINE * a - rest, 1)
                elif a:
                    rolled = pltpu.roll(wrows, wide - FINE * a, 1)
                for p in range(P_):
                    r0 = (p * A_ + a) * rows
                    wall[r0:r0 + rows, samples * i:samples * (i + 1)] = (
                        rolled[:, LANES * p:LANES * p + samples].astype(bf16))
    with jax.named_scope("wait_twin"):
        twin_copy(0, 2 * t + 1 - side).wait_recv()
        for k in range(T - 1):
            wait_twin(k)
    with jax.named_scope("sources"):
        blocks = []
        for i in range(T):
            first, second = 2.0 * scaled(plain(part_s[2 * i])), 2.0 * scaled(plain(part_s[2 * i + 1]))
            blocks.append(jnp.concatenate([first[:, :part], second], axis=1))
        sources = whiten(assemble(blocks))
    with jax.named_scope("correlate"):
        z = None
        for i in range(T):
            srows = jnp.concatenate([sources[i], jnp.zeros((rows, LANES), f32)], axis=1)
            xs = []
            for s in range(STEPS * VS):
                one = jnp.broadcast_to(srows[s:s + 1], (FINE, span))
                xs.append(pltpu.roll(one, 0, 1, stride=1, stride_axis=0).astype(bf16))
            term = lax.dot_general(wall[:, samples * i:samples * i + span], jnp.concatenate(xs, axis=0),
                                   (((1,), (1,)), ((), ())), preferred_element_type=f32)
            z = term if z is None else z + term
        z = z * (1.0 / math.sqrt(window))

    with jax.named_scope("result"):
        lane_group = lane // FINE
        per_tile = LANES // FINE
        span_out = min(lag_dev, LANES)
        for p in range(P_):
            for lo_s in range(0, STEPS * VS, per_tile):
                turned = []
                for a in range(A_):
                    r0 = (p * A_ + a) * rows
                    tile = z[r0:r0 + rows, lo_s * FINE:lo_s * FINE + LANES]
                    turned.append(pltpu.roll(tile, FINE * a, 1) if a else tile)
                for s in range(per_tile):
                    o = turned[0]
                    for a in range(1, A_):
                        o = jnp.where(lane_group == (s + a) % per_tile, turned[a], o)
                    if s:
                        o = pltpu.roll(o, LANES - FINE * s, 1)
                    out_ref[lo_s + s, :, LANES * p:LANES * p + span_out] = o[:, :span_out]

    with jax.named_scope("wait_sends"):
        for s in sends + relays + ts_sends:
            s.wait_send()


def shards(records, pair_rows, fir_taps, source_blocks):
    C = lax.axis_size("chan")
    T = lax.axis_size("tm")
    rows, raw = records.shape
    samples = raw // 4
    f32, bf16, i16 = jnp.float32, jnp.bfloat16, jnp.int16
    dma = pltpu.SemaphoreType.DMA
    hbm = pl.BlockSpec(memory_space=pltpu.HBM)
    operands = [pltpu.with_memory_space_constraint(x, pltpu.HBM)
                for x in (fir_taps, pair_rows, source_blocks, records)]
    out = pl.pallas_call(
        functools.partial(body, C, T, rows),
        out_shape=pltpu.VMEM((STEPS * VS, rows, LAGS // T), f32),
        in_specs=[hbm] * 4,
        out_specs=pl.BlockSpec(memory_space=pltpu.VMEM),
        scratch_shapes=[
            pltpu.SMEM(fir_taps.shape, f32),
            pltpu.SMEM(pair_rows.shape, jnp.int32),
            pltpu.SMEM(source_blocks.shape, jnp.int32),
            pltpu.VMEM(records.shape, bf16),
            dma((4,)),
            pltpu.VMEM((2, rows, samples // 2 + LANES), i16),
            pltpu.VMEM((C, rows, samples // 2 + LANES), i16),
            pltpu.VMEM((T, rows, samples + LANES), i16),
            pltpu.VMEM((T, rows, samples + LANES), i16),
            pltpu.VMEM((2 * T, rows, samples // 2 + LANES), i16),
            pltpu.VMEM((rows, T * samples + LAGS + LANES), f32),
            pltpu.VMEM((LAGS // T // FINE * rows, T * samples + LANES), bf16),
            dma((C,)), dma((C,)), dma((T,)), dma((T,)), dma((T,)), dma((T,)), dma((T,)), dma((T,)), dma((T,)), dma((T,)),
        ],
        compiler_params=pltpu.CompilerParams(
            collective_id=0, has_side_effects=True,
            vmem_limit_bytes=(24 if samples * T <= 8192 else 60) * 2**20),
        cost_estimate=pl.CostEstimate(flops=600_000_000, bytes_accessed=1_000_000, transcendentals=0),
    )(*operands)
    return out.reshape(STEPS, VS, rows, LAGS // T)


def solution(mesh):
    return jax.shard_map(
        shards,
        mesh=mesh,
        in_specs=(P("chan", "tm"), P("chan", None), P(), P()),
        out_specs=P(None, None, "chan", "tm"),
        check_vma=False,
    )
```

```python
import functools
import math

import jax
import jax.numpy as jnp
from jax import lax
from jax.experimental import pallas as pl
from jax.experimental.pallas import tpu as pltpu
from jax.sharding import PartitionSpec as P

VS = 8
STEPS = 2
LAGS = 1024
TAPS = 32
LANES = 128
FINE = 16
SPILL = TAPS // 4
FULL = 15


def body(C, T, rows, taps_hbm, pair_hbm, blocks_hbm, rec_hbm, out_ref,
         taps_ref, pair_ref, blocks_ref, rec_ref, local_s,
         halves, plane, mate_rest, own, partner, part_s, wp, wall,
         plane_s, plane_r, own_s, own_r, mate_s, mate_r, partner_s, partner_r,
         body_s, body_r, twin_s, twin_r):
    me = lax.axis_index("chan")
    t = lax.axis_index("tm")
    f32, bf16, i16, i32 = jnp.float32, jnp.bfloat16, jnp.int16, jnp.int32
    samples = rec_ref.shape[1] // 4
    width = samples + LANES
    part = samples // 2
    half = C // 2
    side = lax.rem(me, 2)
    twin = me + 1 - 2 * side
    lag_dev = LAGS // T
    P_ = max(1, lag_dev // LANES)
    A_ = min(lag_dev, LANES) // FINE
    window = samples * T

    def at_chan(d):
        return lax.rem(me + d, C)

    def at_tm(d):
        return lax.rem(t + d, T)

    def remote(src, dst, ssem, rsem, where):
        return pltpu.make_async_remote_copy(
            src_ref=src, dst_ref=dst, send_sem=ssem, recv_sem=rsem,
            device_id=where, device_id_type=pl.DeviceIdType.MESH)

    def arrived(buf, count, sem):
        blocks = buf.at[pl.ds(0, count)]
        pltpu.make_async_copy(blocks, blocks, sem).wait()

    gone = arrived

    with jax.named_scope("greet"):
        loads = [pltpu.make_async_copy(src, dst, local_s.at[i]) for i, (src, dst) in enumerate((
            (taps_hbm, taps_ref), (rec_hbm, rec_ref), (pair_hbm, pair_ref), (blocks_hbm, blocks_ref)))]
        for load in loads:
            load.start()
        barrier = pltpu.get_barrier_semaphore()
        for d in range(1, C):
            pl.semaphore_signal(barrier, inc=1, device_id={"chan": at_chan(d)}, device_id_type=pl.DeviceIdType.MESH)
        for d in range(1, T):
            pl.semaphore_signal(barrier, inc=1, device_id={"tm": at_tm(d)}, device_id_type=pl.DeviceIdType.MESH)

    with jax.named_scope("band"):
        group = 4 * LANES
        depth = LANES + group
        row = lax.broadcasted_iota(i32, (8, LANES), 0)
        n = lax.broadcasted_iota(i32, (8, LANES), 1)
        tap = 4 * n + 3 - row
        cell = jnp.zeros((8, LANES), f32)
    with jax.named_scope("load_taps"):
        loads[0].wait()
    with jax.named_scope("band_tiles"):
        for k in range(TAPS):
            cell = jnp.where(tap == k, taps_ref[k], cell)
        reach = TAPS // 4 + 1
        tiles = []
        for b in range(depth // 8):
            at = 2 * b - LANES // 4
            tile = jnp.zeros_like(cell)
            if at > -reach:
                tile = pltpu.roll(cell, at % LANES, 1) if at else cell
                if at < 0:
                    tile = jnp.where(n < reach, tile, 0.0)
                elif at + reach > LANES:
                    tile = jnp.where(n >= reach, tile, 0.0)
            tiles.append(tile)
        band = jnp.concatenate(tiles, axis=0)
        hi = band.astype(bf16)
        lo = (band - hi.astype(f32)).astype(bf16)
        band2 = jnp.concatenate([hi, lo], axis=1)
    with jax.named_scope("load_records"):
        for load in loads[1:]:
            load.wait()

    groups = samples // LANES
    lane = lax.broadcasted_iota(i32, (rows, LANES), 1)

    def encode(x):
        peak = jnp.maximum(jnp.max(jnp.abs(x), axis=1, keepdims=True), 1e-30)
        e = jnp.floor(jnp.log2(peak)) + 1.0
        return jnp.clip(jnp.round(x * jnp.exp2(FULL - e)), -32767.0, 32767.0).astype(i32), e

    def scaled(v):
        at = v.shape[1] - LANES + SPILL
        return v * jnp.exp2(v[:, at:at + 1] - (FULL + 1))

    def plain(x):
        return x.astype(i32).astype(f32)

    def permuted(at, x):
        out = []
        for h in range(at.shape[0] // 8):
            want = at[8 * h:8 * h + 8]
            cols = []
            for g in range(x.shape[1] // LANES):
                tile = x[:, LANES * g:LANES * (g + 1)]
                got = jnp.take_along_axis(tile[:8], want & 7, axis=0)
                for v in range(1, rows // 8):
                    more = jnp.take_along_axis(tile[8 * v:8 * v + 8], want & 7, axis=0)
                    got = jnp.where((want >> 3) == v, more, got)
                cols.append(got)
            out.append(jnp.concatenate(cols, axis=1))
        return jnp.concatenate(out, axis=0)

    with jax.named_scope("filter"):
        raw = rec_ref[...]
        parts = []
        for g in range(groups):
            if g == 0:
                first = jnp.zeros((rows, LANES), bf16)
            else:
                first = raw[:, group * g - LANES:group * g]
            parts.append(jnp.concatenate([first, raw[:, group * g:group * (g + 1)]], axis=1))
        both = jnp.dot(jnp.concatenate(parts, axis=0), band2, preferred_element_type=f32)
        both = both[:, :LANES] + both[:, LANES:]
        edge = jnp.dot(raw[:, group * groups - LANES:], band2[:LANES], preferred_element_type=f32)
        edge = edge[:, :LANES] + edge[:, LANES:]
        filtered = jnp.concatenate([both[rows * g:rows * (g + 1)] for g in range(groups)] + [edge], axis=1)
        rr = lax.broadcasted_iota(i32, (rows, LANES), 0)
        pick = jnp.zeros((rows, LANES), i32)
        for r in range(rows):
            pick = jnp.where(rr == r, pair_ref[0, r], pick)
        q, e = encode(filtered)
        note = jnp.where(lane == SPILL, e.astype(i32), jnp.where(lane == SPILL + 1, pick, q[:, samples:])).astype(i16)
        q = q[:, :samples].astype(i16)
        own[t] = jnp.concatenate([q, note], axis=1)
        halves[0] = jnp.concatenate([q[:, :part], note], axis=1)
        halves[1] = jnp.concatenate([q[:, part:], note], axis=1)
        plane[me] = halves[side]

    with jax.named_scope("wait_greeting"):
        pl.semaphore_wait(barrier, C + T - 2)

    with jax.named_scope("send_filtered"):
        others = [d for d in range(1, C) if d != half]
        mate_copy = remote(halves.at[lax.rem(side + half + 1, 2)], mate_rest, mate_s, mate_r, {"chan": at_chan(half)})
        others = [half] + others
        sends = [remote(halves.at[lax.rem(side + d, 2)], plane.at[me], plane_s, plane_r,
                         {"chan": at_chan(d)}) for d in others]
        sends += [remote(own.at[t], own.at[t], own_s, own_r.at[d], {"tm": at_tm(d)}) for d in range(1, T)]
        sends = sends[:C - 1] + [mate_copy] + sends[C - 1:]
        for s in sends:
            s.start()

    with jax.named_scope("clear"):
        wp[:, window:] = jnp.zeros((rows, wp.shape[1] - window), f32)
        wall[:, window:] = jnp.zeros((wall.shape[0], LANES), bf16)

    low = t < T // 2
    def near(k):
        up = jnp.where(k >= t, k + 1, k)
        slot = jnp.where(low, up, lax.rem(t - 1 - k + T, T))
        return slot, lax.rem(t - slot + T, T)

    def relay(k):
        slot, d = near(k)
        remote(own.at[slot], own.at[slot], own_s, own_r.at[d], {"tm": at_tm(d)}).wait_recv()
        s = remote(own.at[slot], partner.at[slot], partner_s, partner_r, {"chan": at_chan(half)})
        s.start()

    def combine(slot):
        return scaled(plain(own[slot])) + scaled(permuted(pick, plain(partner[slot])))

    with jax.named_scope("relay_first"):
        relay(0)

    with jax.named_scope("wait_plane"):
        arrived(plane, C - 1, plane_r)

    early = range(1, min(2, T - 1))
    with jax.named_scope("relay_early"):
        @pl.when(low)
        def _():
            for k in early:
                relay(k)

    with jax.named_scope("pick"):
        picked = []
        per = rows // VS

        def halved(x, within):
            y = x[:VS]
            for q in range(1, per):
                y = jnp.where(within == q, x[VS * q:VS * (q + 1)], y)
            return y

        for step in range(STEPS):
            blk = blocks_ref[step]
            owner = lax.div(blk, per)
            within = lax.rem(blk, per)
            mine = halved(plain(plane[owner]), within)
            pair = mine[:, part + SPILL + 1:part + SPILL + 2].astype(i32)
            theirs = permuted(jnp.broadcast_to(pair, (VS, LANES)), plain(plane[lax.rem(owner + half, C)]))
            first, second = (x[:, part + SPILL:part + SPILL + 1] for x in (mine, theirs))
            top = jnp.maximum(first, second)
            q = jnp.round(mine * jnp.exp2(first - top - 1.0) + theirs * jnp.exp2(second - top - 1.0))
            last = jnp.where(lane[:VS] == SPILL, top, q[:, part:])
            picked.append(jnp.concatenate([q[:, :part], last], axis=1))
        x = jnp.concatenate(picked, axis=0).astype(i32).astype(i16)
        mine_at = 2 * t + side
        part_s[mine_at] = x

        def twin_copy(d, at):
            return remote(part_s.at[at], part_s.at[at], twin_s, twin_r, {"chan": twin})

        def body_copy(d, at):
            return remote(part_s.at[at], part_s.at[at], body_s, body_r.at[d], {"tm": at_tm(d)})

        ts_sends = [body_copy(d, mine_at) for d in range(1, T)] + [twin_copy(0, mine_at)]
        for s in ts_sends:
            s.start()

    with jax.named_scope("relay"):
        @pl.when(jnp.logical_not(low))
        def _():
            for k in early:
                relay(k)
        for k in range(early.stop, T - 1):
            relay(k)

    lag0 = t * lag_dev
    wide = samples + LANES * P_
    span = samples + LANES
    if lag_dev % LANES == 0:
        base, rest = lag0, 0
    else:
        base = lax.div(lag0, LANES) * LANES
        rest = lax.rem(lag0, LANES)

    def hand_to_twin(k):
        slot, d = near(k)
        body_copy(d, 2 * slot + side).wait_recv()
        s = twin_copy(d, 2 * slot + side)
        s.start()

    def assemble(blocks):
        out = []
        for i, x in enumerate(blocks):
            head = x[:, :LANES]
            if i:
                head = head + jnp.where(lane < SPILL, blocks[i - 1][:, samples:], 0.0)
            out.append(jnp.concatenate([head, x[:, LANES:samples]], axis=1))
        return out

    def whiten(blocks):
        acc = jnp.zeros((rows, LANES), f32)
        for x in blocks:
            sq = x * x
            for g in range(groups):
                acc = acc + sq[:, LANES * g:LANES * (g + 1)]
        scale = lax.rsqrt(jnp.sum(acc, axis=1, keepdims=True) / window + 1e-6)
        return [(x * scale).astype(bf16).astype(f32) for x in blocks]

    with jax.named_scope("hand_to_twin"):
        for k in range(T - 1):
            hand_to_twin(k)
    with jax.named_scope("own_block"):
        mate_copy.wait_recv()
        near_half, far_half = plain(plane[at_chan(half)]), plain(mate_rest[...])
        mate = jnp.concatenate([jnp.where(side == 0, near_half[:, :part], far_half[:, :part]),
                                jnp.where(side == 0, far_half[:, :part], near_half[:, :part]),
                                near_half[:, part:]], axis=1)
        partner[t] = mate.astype(i32).astype(i16)

    with jax.named_scope("wait_partner"):
        arrived(partner, T - 1, partner_r)
    with jax.named_scope("white"):
        white = whiten(assemble([combine(i) for i in range(T)]))
        for i in range(T):
            wp[:, samples * i:samples * (i + 1)] = white[i]
    with jax.named_scope("turn"):
        for i in range(T):
            wrows = wp[:, pl.ds(pl.multiple_of(i * samples + base, LANES), wide)]
            for a in range(A_):
                rolled = wrows
                if lag_dev % LANES:
                    rolled = pltpu.roll(wrows, wide - FINE * a - rest, 1)
                elif a:
                    rolled = pltpu.roll(wrows, wide - FINE * a, 1)
                for p in range(P_):
                    r0 = (p * A_ + a) * rows
                    wall[r0:r0 + rows, samples * i:samples * (i + 1)] = (
                        rolled[:, LANES * p:LANES * p + samples].astype(bf16))
    with jax.named_scope("wait_twin"):
        arrived(part_s, T, twin_r)
    with jax.named_scope("sources"):
        blocks = []
        for i in range(T):
            first, second = 2.0 * scaled(plain(part_s[2 * i])), 2.0 * scaled(plain(part_s[2 * i + 1]))
            blocks.append(jnp.concatenate([first[:, :part], second], axis=1))
        sources = whiten(assemble(blocks))
    with jax.named_scope("correlate"):
        z = None
        for i in range(T):
            srows = jnp.concatenate([sources[i], jnp.zeros((rows, LANES), f32)], axis=1)
            xs = []
            for s in range(STEPS * VS):
                one = jnp.broadcast_to(srows[s:s + 1], (FINE, span))
                xs.append(pltpu.roll(one, 0, 1, stride=1, stride_axis=0).astype(bf16))
            term = lax.dot_general(wall[:, samples * i:samples * i + span], jnp.concatenate(xs, axis=0),
                                   (((1,), (1,)), ((), ())), preferred_element_type=f32)
            z = term if z is None else z + term
        z = z * (1.0 / math.sqrt(window))

    with jax.named_scope("result"):
        lane_group = lane // FINE
        per_tile = LANES // FINE
        span_out = min(lag_dev, LANES)
        for p in range(P_):
            for lo_s in range(0, STEPS * VS, per_tile):
                turned = []
                for a in range(A_):
                    r0 = (p * A_ + a) * rows
                    tile = z[r0:r0 + rows, lo_s * FINE:lo_s * FINE + LANES]
                    turned.append(pltpu.roll(tile, FINE * a, 1) if a else tile)
                for s in range(per_tile):
                    o = turned[0]
                    for a in range(1, A_):
                        o = jnp.where(lane_group == (s + a) % per_tile, turned[a], o)
                    if s:
                        o = pltpu.roll(o, LANES - FINE * s, 1)
                    out_ref[lo_s + s, :, LANES * p:LANES * p + span_out] = o[:, :span_out]

    with jax.named_scope("wait_sends"):
        mate_copy.wait_send()
        for buf, count, sem in ((plane, C - 1, plane_s), (own, T - 1, own_s), (partner, T - 1, partner_s),
                                (part_s, T - 1, body_s), (part_s, T, twin_s)):
            gone(buf, count, sem)


def shards(records, pair_rows, fir_taps, source_blocks):
    C = lax.axis_size("chan")
    T = lax.axis_size("tm")
    rows, raw = records.shape
    samples = raw // 4
    f32, bf16, i16 = jnp.float32, jnp.bfloat16, jnp.int16
    dma = pltpu.SemaphoreType.DMA
    hbm = pl.BlockSpec(memory_space=pltpu.HBM)
    operands = [pltpu.with_memory_space_constraint(x, pltpu.HBM)
                for x in (fir_taps, pair_rows, source_blocks, records)]
    out = pl.pallas_call(
        functools.partial(body, C, T, rows),
        out_shape=pltpu.VMEM((STEPS * VS, rows, LAGS // T), f32),
        in_specs=[hbm] * 4,
        out_specs=pl.BlockSpec(memory_space=pltpu.VMEM),
        scratch_shapes=[
            pltpu.SMEM(fir_taps.shape, f32),
            pltpu.SMEM(pair_rows.shape, jnp.int32),
            pltpu.SMEM(source_blocks.shape, jnp.int32),
            pltpu.VMEM(records.shape, bf16),
            dma((4,)),
            pltpu.VMEM((2, rows, samples // 2 + LANES), i16),
            pltpu.VMEM((C, rows, samples // 2 + LANES), i16),
            pltpu.VMEM((rows, samples // 2 + LANES), i16),
            pltpu.VMEM((T, rows, samples + LANES), i16),
            pltpu.VMEM((T, rows, samples + LANES), i16),
            pltpu.VMEM((2 * T, rows, samples // 2 + LANES), i16),
            pltpu.VMEM((rows, T * samples + LAGS + LANES), f32),
            pltpu.VMEM((LAGS // T // FINE * rows, T * samples + LANES), bf16),
            dma, dma, dma, dma((T,)), dma, dma, dma, dma, dma, dma((T,)), dma, dma,
        ],
        compiler_params=pltpu.CompilerParams(
            collective_id=0, has_side_effects=True,
            vmem_limit_bytes=(24 if samples * T <= 8192 else 60) * 2**20),
        cost_estimate=pl.CostEstimate(flops=600_000_000, bytes_accessed=1_000_000, transcendentals=0),
    )(*operands)
    return out.reshape(STEPS, VS, rows, LAGS // T)


def solution(mesh):
    return jax.shard_map(
        shards,
        mesh=mesh,
        in_specs=(P("chan", "tm"), P("chan", None), P(), P()),
        out_specs=P(None, None, "chan", "tm"),
        check_vma=False,
    )
```

```python
import functools
import math

import jax
import jax.numpy as jnp
from jax import lax
from jax.experimental import pallas as pl
from jax.experimental.pallas import tpu as pltpu
from jax.sharding import PartitionSpec as P

VS = 8
STEPS = 2
LAGS = 1024
TAPS = 32
LANES = 128
FINE = 16
SPILL = TAPS // 4
FULL = 15


def body(C, T, rows, taps_hbm, pair_hbm, blocks_hbm, rec_hbm, out_ref,
         taps_ref, pair_ref, blocks_ref, rec_ref, local_s,
         halves, plane, mate_rest, own, partner, part_s, wp, wall,
         plane_s, plane_r, own_s, own_r, mate_s, mate_r, partner_s, partner_r,
         body_s, body_r, twin_s, twin_r):
    me = lax.axis_index("chan")
    t = lax.axis_index("tm")
    f32, bf16, i16, i32 = jnp.float32, jnp.bfloat16, jnp.int16, jnp.int32
    samples = rec_ref.shape[1] // 4
    width = samples + LANES
    part = samples // 2
    half = C // 2
    side = lax.rem(me, 2)
    twin = me + 1 - 2 * side
    lag_dev = LAGS // T
    P_ = max(1, lag_dev // LANES)
    A_ = min(lag_dev, LANES) // FINE
    window = samples * T

    def at_chan(d):
        return lax.rem(me + d, C)

    def at_tm(d):
        return lax.rem(t + d, T)

    def remote(src, dst, ssem, rsem, where):
        return pltpu.make_async_remote_copy(
            src_ref=src, dst_ref=dst, send_sem=ssem, recv_sem=rsem,
            device_id=where, device_id_type=pl.DeviceIdType.MESH)

    def arrived(buf, count, sem):
        blocks = buf.at[pl.ds(0, count)]
        pltpu.make_async_copy(blocks, blocks, sem).wait()

    gone = arrived

    with jax.named_scope("greet"):
        loads = [pltpu.make_async_copy(src, dst, local_s.at[i]) for i, (src, dst) in enumerate((
            (taps_hbm, taps_ref), (rec_hbm, rec_ref), (pair_hbm, pair_ref), (blocks_hbm, blocks_ref)))]
        for load in loads:
            load.start()
        barrier = pltpu.get_barrier_semaphore()
        for d in range(1, C):
            pl.semaphore_signal(barrier, inc=1, device_id={"chan": at_chan(d)}, device_id_type=pl.DeviceIdType.MESH)
        for d in range(1, T):
            pl.semaphore_signal(barrier, inc=1, device_id={"tm": at_tm(d)}, device_id_type=pl.DeviceIdType.MESH)

    with jax.named_scope("band"):
        group = 4 * LANES
        depth = LANES + group
        row = lax.broadcasted_iota(i32, (8, LANES), 0)
        n = lax.broadcasted_iota(i32, (8, LANES), 1)
        tap = 4 * n + 3 - row
        cell = jnp.zeros((8, LANES), f32)
    with jax.named_scope("load_taps"):
        loads[0].wait()
    with jax.named_scope("band_tiles"):
        for k in range(TAPS):
            cell = jnp.where(tap == k, taps_ref[k], cell)
        reach = TAPS // 4 + 1
        tiles = []
        for b in range(depth // 8):
            at = 2 * b - LANES // 4
            tile = jnp.zeros_like(cell)
            if at > -reach:
                tile = pltpu.roll(cell, at % LANES, 1) if at else cell
                if at < 0:
                    tile = jnp.where(n < reach, tile, 0.0)
                elif at + reach > LANES:
                    tile = jnp.where(n >= reach, tile, 0.0)
            tiles.append(tile)
        band = jnp.concatenate(tiles, axis=0)
        hi = band.astype(bf16)
        lo = (band - hi.astype(f32)).astype(bf16)
        band2 = jnp.concatenate([hi, lo], axis=1)
    with jax.named_scope("load_records"):
        for load in loads[1:]:
            load.wait()

    groups = samples // LANES
    lane = lax.broadcasted_iota(i32, (rows, LANES), 1)

    def encode(x):
        peak = jnp.maximum(jnp.max(jnp.abs(x), axis=1, keepdims=True), 1e-30)
        e = jnp.floor(jnp.log2(peak)) + 1.0
        return jnp.clip(jnp.round(x * jnp.exp2(FULL - e)), -32767.0, 32767.0).astype(i32), e

    def scaled(v):
        at = v.shape[1] - LANES + SPILL
        return v * jnp.exp2(v[:, at:at + 1] - (FULL + 1))

    def plain(x):
        return x.astype(i32).astype(f32)

    def permuted(at, x):
        out = []
        for h in range(at.shape[0] // 8):
            want = at[8 * h:8 * h + 8]
            cols = []
            for g in range(x.shape[1] // LANES):
                tile = x[:, LANES * g:LANES * (g + 1)]
                got = jnp.take_along_axis(tile[:8], want & 7, axis=0)
                for v in range(1, rows // 8):
                    more = jnp.take_along_axis(tile[8 * v:8 * v + 8], want & 7, axis=0)
                    got = jnp.where((want >> 3) == v, more, got)
                cols.append(got)
            out.append(jnp.concatenate(cols, axis=1))
        return jnp.concatenate(out, axis=0)

    with jax.named_scope("filter"):
        raw = rec_ref[...]
        parts = []
        for g in range(groups):
            if g == 0:
                first = jnp.zeros((rows, LANES), bf16)
            else:
                first = raw[:, group * g - LANES:group * g]
            parts.append(jnp.concatenate([first, raw[:, group * g:group * (g + 1)]], axis=1))
        both = jnp.dot(jnp.concatenate(parts, axis=0), band2, preferred_element_type=f32)
        both = both[:, :LANES] + both[:, LANES:]
        edge = jnp.dot(raw[:, group * groups - LANES:], band2[:LANES], preferred_element_type=f32)
        edge = edge[:, :LANES] + edge[:, LANES:]
        filtered = jnp.concatenate([both[rows * g:rows * (g + 1)] for g in range(groups)] + [edge], axis=1)
        rr = lax.broadcasted_iota(i32, (rows, LANES), 0)
        pick = jnp.zeros((rows, LANES), i32)
        for r in range(rows):
            pick = jnp.where(rr == r, pair_ref[0, r], pick)
        q, e = encode(filtered)
        note = jnp.where(lane == SPILL, e.astype(i32), jnp.where(lane == SPILL + 1, pick, q[:, samples:])).astype(i16)
        q = q[:, :samples].astype(i16)
        own[t] = jnp.concatenate([q, note], axis=1)
        halves[0] = jnp.concatenate([q[:, :part], note], axis=1)
        halves[1] = jnp.concatenate([q[:, part:], note], axis=1)
        plane[me] = halves[side]

    with jax.named_scope("wait_greeting"):
        pl.semaphore_wait(barrier, C + T - 2)

    with jax.named_scope("send_filtered"):
        others = [d for d in range(1, C) if d != half]
        mate_copy = remote(halves.at[lax.rem(side + half + 1, 2)], mate_rest, mate_s, mate_r, {"chan": at_chan(half)})
        others = [half] + others
        sends = [remote(halves.at[lax.rem(side + d, 2)], plane.at[me], plane_s, plane_r,
                         {"chan": at_chan(d)}) for d in others]
        sends += [remote(own.at[t], own.at[t], own_s, own_r.at[d], {"tm": at_tm(d)}) for d in range(1, T)]
        sends = sends[:C - 1] + [mate_copy] + sends[C - 1:]
        for s in sends:
            s.start()

    with jax.named_scope("clear"):
        wp[:, window:] = jnp.zeros((rows, wp.shape[1] - window), bf16)
        wall[:, window:] = jnp.zeros((wall.shape[0], LANES * P_), bf16)

    low = t < T // 2
    def near(k):
        up = jnp.where(k >= t, k + 1, k)
        slot = jnp.where(low, up, lax.rem(t - 1 - k + T, T))
        return slot, lax.rem(t - slot + T, T)

    def relay(k):
        slot, d = near(k)
        remote(own.at[slot], own.at[slot], own_s, own_r.at[d], {"tm": at_tm(d)}).wait_recv()
        s = remote(own.at[slot], partner.at[slot], partner_s, partner_r, {"chan": at_chan(half)})
        s.start()

    def combine(slot):
        return scaled(plain(own[slot])) + scaled(permuted(pick, plain(partner[slot])))

    with jax.named_scope("relay_first"):
        relay(0)

    with jax.named_scope("wait_plane"):
        arrived(plane, C - 1, plane_r)

    early = range(1, min(2, T - 1))
    with jax.named_scope("relay_early"):
        @pl.when(low)
        def _():
            for k in early:
                relay(k)

    with jax.named_scope("pick"):
        picked = []
        per = rows // VS

        def halved(x, within):
            y = x[:VS]
            for q in range(1, per):
                y = jnp.where(within == q, x[VS * q:VS * (q + 1)], y)
            return y

        for step in range(STEPS):
            blk = blocks_ref[step]
            owner = lax.div(blk, per)
            within = lax.rem(blk, per)
            mine = halved(plain(plane[owner]), within)
            pair = mine[:, part + SPILL + 1:part + SPILL + 2].astype(i32)
            theirs = permuted(jnp.broadcast_to(pair, (VS, LANES)), plain(plane[lax.rem(owner + half, C)]))
            first, second = (x[:, part + SPILL:part + SPILL + 1] for x in (mine, theirs))
            top = jnp.maximum(first, second)
            q = jnp.round(mine * jnp.exp2(first - top - 1.0) + theirs * jnp.exp2(second - top - 1.0))
            last = jnp.where(lane[:VS] == SPILL, top, q[:, part:])
            picked.append(jnp.concatenate([q[:, :part], last], axis=1))
        x = jnp.concatenate(picked, axis=0).astype(i32).astype(i16)
        mine_at = 2 * t + side
        part_s[mine_at] = x

        def twin_copy(d, at):
            return remote(part_s.at[at], part_s.at[at], twin_s, twin_r, {"chan": twin})

        def body_copy(d, at):
            return remote(part_s.at[at], part_s.at[at], body_s, body_r.at[d], {"tm": at_tm(d)})

        ts_sends = [body_copy(d, mine_at) for d in range(1, T)] + [twin_copy(0, mine_at)]
        for s in ts_sends:
            s.start()

    with jax.named_scope("relay"):
        @pl.when(jnp.logical_not(low))
        def _():
            for k in early:
                relay(k)
        for k in range(early.stop, T - 1):
            relay(k)

    lag0 = t * lag_dev
    wide = samples + LANES
    span = samples + LANES
    if lag_dev % LANES == 0:
        base, rest = lag0, 0
    else:
        base = lax.div(lag0, LANES) * LANES
        rest = lax.rem(lag0, LANES)

    def hand_to_twin(k):
        slot, d = near(k)
        body_copy(d, 2 * slot + side).wait_recv()
        s = twin_copy(d, 2 * slot + side)
        s.start()

    def assemble(blocks):
        out = []
        for i, x in enumerate(blocks):
            head = x[:, :LANES]
            if i:
                head = head + jnp.where(lane < SPILL, blocks[i - 1][:, samples:], 0.0)
            out.append(jnp.concatenate([head, x[:, LANES:samples]], axis=1))
        return out

    def whiten(blocks):
        acc = jnp.zeros((rows, LANES), f32)
        for x in blocks:
            sq = x * x
            for g in range(groups):
                acc = acc + sq[:, LANES * g:LANES * (g + 1)]
        scale = lax.rsqrt(jnp.sum(acc, axis=1, keepdims=True) / window + 1e-6)
        return [(x * scale).astype(bf16) for x in blocks]

    with jax.named_scope("hand_to_twin"):
        for k in range(T - 1):
            hand_to_twin(k)
    with jax.named_scope("own_block"):
        mate_copy.wait_recv()
        near_half, far_half = plain(plane[at_chan(half)]), plain(mate_rest[...])
        mate = jnp.concatenate([jnp.where(side == 0, near_half[:, :part], far_half[:, :part]),
                                jnp.where(side == 0, far_half[:, :part], near_half[:, :part]),
                                near_half[:, part:]], axis=1)
        partner[t] = mate.astype(i32).astype(i16)

    with jax.named_scope("wait_partner"):
        arrived(partner, T - 1, partner_r)
    with jax.named_scope("white"):
        white = whiten(assemble([combine(i) for i in range(T)]))
        for i in range(T):
            wp[:, samples * i:samples * (i + 1)] = white[i]
    with jax.named_scope("turn"):
        for i in range(T):
            wrows = wp[:, pl.ds(pl.multiple_of(i * samples + base, LANES), wide)]
            for a in range(A_):
                rolled = wrows
                if lag_dev % LANES:
                    rolled = pltpu.roll(wrows, wide - FINE * a - rest, 1)
                elif a:
                    rolled = pltpu.roll(wrows, wide - FINE * a, 1)
                wall[a * rows:(a + 1) * rows, samples * i:samples * (i + 1)] = rolled[:, :samples]
    with jax.named_scope("wait_twin"):
        arrived(part_s, T, twin_r)
    with jax.named_scope("sources"):
        blocks = []
        for i in range(T):
            first, second = 2.0 * scaled(plain(part_s[2 * i])), 2.0 * scaled(plain(part_s[2 * i + 1]))
            blocks.append(jnp.concatenate([first[:, :part], second], axis=1))
        sources = whiten(assemble(blocks))
    with jax.named_scope("correlate"):
        z = None
        for i in range(T):
            srows = jnp.concatenate([sources[i], jnp.zeros((rows, LANES), bf16)], axis=1)
            xs = []
            for s in range(STEPS * VS):
                one = jnp.broadcast_to(srows[s:s + 1], (FINE, span))
                xs.append(pltpu.roll(one, 0, 1, stride=1, stride_axis=0))
            ws = jnp.concatenate([wall[:, samples * i + LANES * p:samples * i + LANES * p + span] for p in range(P_)],
                                 axis=0)
            term = lax.dot_general(ws, jnp.concatenate(xs, axis=0),
                                   (((1,), (1,)), ((), ())), preferred_element_type=f32)
            z = term if z is None else z + term
        z = z * (1.0 / math.sqrt(window))

    with jax.named_scope("result"):
        lane_group = lane // FINE
        per_tile = LANES // FINE
        span_out = min(lag_dev, LANES)
        for p in range(P_):
            for lo_s in range(0, STEPS * VS, per_tile):
                turned = []
                for a in range(A_):
                    r0 = (p * A_ + a) * rows
                    tile = z[r0:r0 + rows, lo_s * FINE:lo_s * FINE + LANES]
                    turned.append(pltpu.roll(tile, FINE * a, 1) if a else tile)
                for s in range(per_tile):
                    o = turned[0]
                    for a in range(1, A_):
                        o = jnp.where(lane_group == (s + a) % per_tile, turned[a], o)
                    if s:
                        o = pltpu.roll(o, LANES - FINE * s, 1)
                    out_ref[lo_s + s, :, LANES * p:LANES * p + span_out] = o[:, :span_out]

    with jax.named_scope("wait_sends"):
        mate_copy.wait_send()
        for buf, count, sem in ((plane, C - 1, plane_s), (own, T - 1, own_s), (partner, T - 1, partner_s),
                                (part_s, T - 1, body_s), (part_s, T, twin_s)):
            gone(buf, count, sem)


def shards(records, pair_rows, fir_taps, source_blocks):
    C = lax.axis_size("chan")
    T = lax.axis_size("tm")
    rows, raw = records.shape
    samples = raw // 4
    f32, bf16, i16 = jnp.float32, jnp.bfloat16, jnp.int16
    dma = pltpu.SemaphoreType.DMA
    hbm = pl.BlockSpec(memory_space=pltpu.HBM)
    operands = [pltpu.with_memory_space_constraint(x, pltpu.HBM)
                for x in (fir_taps, pair_rows, source_blocks, records)]
    out = pl.pallas_call(
        functools.partial(body, C, T, rows),
        out_shape=pltpu.VMEM((STEPS * VS, rows, LAGS // T), f32),
        in_specs=[hbm] * 4,
        out_specs=pl.BlockSpec(memory_space=pltpu.VMEM),
        scratch_shapes=[
            pltpu.SMEM(fir_taps.shape, f32),
            pltpu.SMEM(pair_rows.shape, jnp.int32),
            pltpu.SMEM(source_blocks.shape, jnp.int32),
            pltpu.VMEM(records.shape, bf16),
            dma((4,)),
            pltpu.VMEM((2, rows, samples // 2 + LANES), i16),
            pltpu.VMEM((C, rows, samples // 2 + LANES), i16),
            pltpu.VMEM((rows, samples // 2 + LANES), i16),
            pltpu.VMEM((T, rows, samples + LANES), i16),
            pltpu.VMEM((T, rows, samples + LANES), i16),
            pltpu.VMEM((2 * T, rows, samples // 2 + LANES), i16),
            pltpu.VMEM((rows, T * samples + LAGS + LANES), bf16),
            pltpu.VMEM((min(LAGS // T, LANES) // FINE * rows, T * samples + LANES * max(1, LAGS // T // LANES)), bf16),
            dma, dma, dma, dma((T,)), dma, dma, dma, dma, dma, dma((T,)), dma, dma,
        ],
        compiler_params=pltpu.CompilerParams(
            collective_id=0, has_side_effects=True,
            vmem_limit_bytes=(24 if samples * T <= 8192 else 60) * 2**20),
        cost_estimate=pl.CostEstimate(flops=600_000_000, bytes_accessed=1_000_000, transcendentals=0),
    )(*operands)
    return out.reshape(STEPS, VS, rows, LAGS // T)


def solution(mesh):
    return jax.shard_map(
        shards,
        mesh=mesh,
        in_specs=(P("chan", "tm"), P("chan", None), P(), P()),
        out_specs=P(None, None, "chan", "tm"),
        check_vma=False,
    )
```

```python
import functools
import math

import jax
import jax.numpy as jnp
from jax import lax
from jax.experimental import pallas as pl
from jax.experimental.pallas import tpu as pltpu
from jax.sharding import PartitionSpec as P

VS = 8
STEPS = 2
LAGS = 1024
TAPS = 32
LANES = 128
FINE = 16
SPILL = TAPS // 4
FULL = 15


def body(C, T, rows, taps_hbm, pair_hbm, blocks_hbm, rec_hbm, out_ref,
         taps_ref, pair_ref, blocks_ref, rec_ref, local_s,
         halves, plane, mate_rest, own, partner, part_s, src, wp, wall,
         plane_s, plane_r, own_s, own_r, mate_r, partner_s, partner_r,
         body_r, twin_s, twin_r):
    me = lax.axis_index("chan")
    t = lax.axis_index("tm")
    f32, bf16, i16, i32 = jnp.float32, jnp.bfloat16, jnp.int16, jnp.int32
    samples = rec_ref.shape[1] // 4
    width = samples + LANES
    part = samples // 2
    half = C // 2
    side = lax.rem(me, 2)
    twin = me + 1 - 2 * side
    lag_dev = LAGS // T
    P_ = max(1, lag_dev // LANES)
    A_ = min(lag_dev, LANES) // FINE
    window = samples * T

    def at_chan(d):
        return lax.rem(me + d, C)

    def at_tm(d):
        return lax.rem(t + d, T)

    def remote(src, dst, ssem, rsem, where):
        return pltpu.make_async_remote_copy(
            src_ref=src, dst_ref=dst, send_sem=ssem, recv_sem=rsem,
            device_id=where, device_id_type=pl.DeviceIdType.MESH)

    def arrived(buf, count, sem):
        blocks = buf.at[pl.ds(0, count)]
        pltpu.make_async_copy(blocks, blocks, sem).wait()

    gone = arrived

    with jax.named_scope("greet"):
        loads = [pltpu.make_async_copy(src, dst, local_s.at[i]) for i, (src, dst) in enumerate((
            (taps_hbm, taps_ref), (rec_hbm, rec_ref), (pair_hbm, pair_ref), (blocks_hbm, blocks_ref)))]
        loads[0].start()
        for g in range(4):
            cut = pl.ds(samples * g, samples)
            pltpu.make_async_copy(rec_hbm.at[:, cut], rec_ref.at[:, cut], local_s.at[1]).start()
        loads[2].start()
        loads[3].start()
        barrier = pltpu.get_barrier_semaphore()
        for d in range(1, C):
            pl.semaphore_signal(barrier, inc=1, device_id={"chan": at_chan(d)}, device_id_type=pl.DeviceIdType.MESH)
        for d in range(1, T):
            pl.semaphore_signal(barrier, inc=1, device_id={"tm": at_tm(d)}, device_id_type=pl.DeviceIdType.MESH)

    with jax.named_scope("band"):
        group = 4 * LANES
        depth = LANES + group
        row = lax.broadcasted_iota(i32, (8, LANES), 0)
        n = lax.broadcasted_iota(i32, (8, LANES), 1)
        tap = 4 * n + 3 - row
        cell = jnp.zeros((8, LANES), f32)
    with jax.named_scope("load_taps"):
        loads[0].wait()
    with jax.named_scope("band_tiles"):
        for k in range(TAPS):
            cell = jnp.where(tap == k, taps_ref[k], cell)
        reach = TAPS // 4 + 1
        tiles = []
        for b in range(depth // 8):
            at = 2 * b - LANES // 4
            tile = jnp.zeros_like(cell)
            if at > -reach:
                tile = pltpu.roll(cell, at % LANES, 1) if at else cell
                if at < 0:
                    tile = jnp.where(n < reach, tile, 0.0)
                elif at + reach > LANES:
                    tile = jnp.where(n >= reach, tile, 0.0)
            tiles.append(tile)
        band = jnp.concatenate(tiles, axis=0)
        hi = band.astype(bf16)
        lo = (band - hi.astype(f32)).astype(bf16)
        band2 = jnp.concatenate([hi, lo], axis=1)
    with jax.named_scope("load_records"):
        for load in loads[1:]:
            load.wait()

    groups = samples // LANES
    lane = lax.broadcasted_iota(i32, (rows, LANES), 1)

    def encode(x):
        peak = jnp.maximum(jnp.max(jnp.abs(x), axis=1, keepdims=True), 1e-30)
        e = jnp.floor(jnp.log2(peak)) + 1.0
        return jnp.clip(jnp.round(x * jnp.exp2(FULL - e)), -32767.0, 32767.0).astype(i32), e

    def scaled(v):
        at = v.shape[1] - LANES + SPILL
        return v * jnp.exp2(v[:, at:at + 1] - (FULL + 1))

    def plain(x):
        return x.astype(i32).astype(f32)

    def permuted(at, x):
        out = []
        for h in range(at.shape[0] // 8):
            want = at[8 * h:8 * h + 8]
            cols = []
            for g in range(x.shape[1] // LANES):
                tile = x[:, LANES * g:LANES * (g + 1)]
                got = jnp.take_along_axis(tile[:8], want & 7, axis=0)
                for v in range(1, rows // 8):
                    more = jnp.take_along_axis(tile[8 * v:8 * v + 8], want & 7, axis=0)
                    got = jnp.where((want >> 3) == v, more, got)
                cols.append(got)
            out.append(jnp.concatenate(cols, axis=1))
        return jnp.concatenate(out, axis=0)

    with jax.named_scope("filter"):
        raw = rec_ref[...]
        parts = []
        for g in range(groups):
            if g == 0:
                first = jnp.zeros((rows, LANES), bf16)
            else:
                first = raw[:, group * g - LANES:group * g]
            parts.append(jnp.concatenate([first, raw[:, group * g:group * (g + 1)]], axis=1))
        both = jnp.dot(jnp.concatenate(parts, axis=0), band2, preferred_element_type=f32)
        both = both[:, :LANES] + both[:, LANES:]
        edge = jnp.dot(raw[:, group * groups - LANES:], band2[:LANES], preferred_element_type=f32)
        edge = edge[:, :LANES] + edge[:, LANES:]
        filtered = jnp.concatenate([both[rows * g:rows * (g + 1)] for g in range(groups)] + [edge], axis=1)
        rr = lax.broadcasted_iota(i32, (rows, LANES), 0)
        pick = jnp.zeros((rows, LANES), i32)
        for r in range(rows):
            pick = jnp.where(rr == r, pair_ref[0, r], pick)
        q, e = encode(filtered)
        note = jnp.where(lane == SPILL, e.astype(i32), jnp.where(lane == SPILL + 1, pick, q[:, samples:])).astype(i16)
        q = q[:, :samples].astype(i16)
        own[t] = jnp.concatenate([q, note], axis=1)
        halves[0] = jnp.concatenate([q[:, :part], note], axis=1)
        halves[1] = jnp.concatenate([q[:, part:], note], axis=1)
        plane[me] = halves[side]

    with jax.named_scope("wait_greeting"):
        pl.semaphore_wait(barrier, C + T - 2)

    with jax.named_scope("send_filtered"):
        others = [d for d in range(1, C) if d != half]
        mate_copy = remote(halves.at[lax.rem(side + half + 1, 2)], mate_rest, plane_s, mate_r, {"chan": at_chan(half)})
        others = [half] + others
        sends = [remote(halves.at[lax.rem(side + d, 2)], plane.at[me], plane_s, plane_r,
                         {"chan": at_chan(d)}) for d in others]
        sends += [remote(own.at[t], own.at[t], own_s, own_r.at[d - 1], {"tm": at_tm(d)}) for d in range(1, T)]
        sends = sends[:C - 1] + [mate_copy] + sends[C - 1:]
        for s in sends:
            s.start()

    with jax.named_scope("clear"):
        wp[:, window:] = jnp.zeros((rows, wp.shape[1] - window), bf16)
        wall[:, window:] = jnp.zeros((wall.shape[0], LANES * P_), bf16)

    low = t < T // 2
    def near(k):
        up = jnp.where(k >= t, k + 1, k)
        slot = jnp.where(low, up, lax.rem(t - 1 - k + T, T))
        return slot, lax.rem(t - slot + T, T)

    def relay(k):
        slot, d = near(k)
        remote(own.at[slot], own.at[slot], own_s, own_r.at[d - 1], {"tm": at_tm(d)}).wait_recv()
        s = remote(own.at[slot], partner.at[slot], partner_s, partner_r, {"chan": at_chan(half)})
        s.start()

    def combine(slot):
        return scaled(plain(own[slot])) + scaled(permuted(pick, plain(partner[slot])))

    with jax.named_scope("relay_first"):
        relay(0)

    with jax.named_scope("wait_plane"):
        arrived(plane, C - 1, plane_r)

    early = range(1, min(2, T - 1))
    with jax.named_scope("relay_early"):
        @pl.when(low)
        def _():
            for k in early:
                relay(k)

    with jax.named_scope("pick"):
        picked = []
        per = rows // VS

        def halved(x, within):
            y = x[:VS]
            for q in range(1, per):
                y = jnp.where(within == q, x[VS * q:VS * (q + 1)], y)
            return y

        for step in range(STEPS):
            blk = blocks_ref[step]
            owner = lax.div(blk, per)
            within = lax.rem(blk, per)
            mine = halved(plain(plane[owner]), within)
            pair = mine[:, part + SPILL + 1:part + SPILL + 2].astype(i32)
            theirs = permuted(jnp.broadcast_to(pair, (VS, LANES)), plain(plane[lax.rem(owner + half, C)]))
            first, second = (x[:, part + SPILL:part + SPILL + 1] for x in (mine, theirs))
            top = jnp.maximum(first, second)
            q = jnp.round(mine * jnp.exp2(first - top - 1.0) + theirs * jnp.exp2(second - top - 1.0))
            last = jnp.where(lane[:VS] == SPILL, top, q[:, part:])
            picked.append(jnp.concatenate([q[:, :part], last], axis=1))
        x = jnp.concatenate(picked, axis=0).astype(i32).astype(i16)
        mine_at = 2 * t + side
        part_s[mine_at] = x

        def twin_copy(d, at):
            return remote(part_s.at[at], part_s.at[at], twin_s, twin_r, {"chan": twin})

        def body_copy(d, at):
            return remote(part_s.at[at], part_s.at[at], twin_s, body_r.at[d - 1], {"tm": at_tm(d)})

        ts_sends = [body_copy(d, mine_at) for d in range(1, T)] + [twin_copy(0, mine_at)]
        for s in ts_sends:
            s.start()

    with jax.named_scope("relay"):
        @pl.when(jnp.logical_not(low))
        def _():
            for k in early:
                relay(k)
        for k in range(early.stop, T - 1):
            relay(k)

    lag0 = t * lag_dev
    wide = samples + LANES
    span = samples + LANES
    if lag_dev % LANES == 0:
        base, rest = lag0, 0
    else:
        base = lax.div(lag0, LANES) * LANES
        rest = lax.rem(lag0, LANES)

    def hand_to_twin(k):
        slot, d = near(k)
        body_copy(d, 2 * slot + side).wait_recv()
        twin_copy(d, 2 * slot + side).start()

    def assemble(blocks):
        out = []
        for i, x in enumerate(blocks):
            head = x[:, :LANES]
            if i:
                head = head + jnp.where(lane < SPILL, blocks[i - 1][:, samples:], 0.0)
            out.append(jnp.concatenate([head, x[:, LANES:samples]], axis=1))
        return out

    def whiten(blocks):
        acc = jnp.zeros((rows, LANES), f32)
        for x in blocks:
            sq = x * x
            for g in range(groups):
                acc = acc + sq[:, LANES * g:LANES * (g + 1)]
        scale = lax.rsqrt(jnp.sum(acc, axis=1, keepdims=True) / window + 1e-6)
        return [(x * scale).astype(bf16) for x in blocks]

    with jax.named_scope("hand_to_twin"):
        for k in range(T - 1):
            hand_to_twin(k)
    with jax.named_scope("own_block"):
        mate_copy.wait_recv()
        near_half, far_half = plain(plane[at_chan(half)]), plain(mate_rest[...])
        mate = jnp.concatenate([jnp.where(side == 0, near_half[:, :part], far_half[:, :part]),
                                jnp.where(side == 0, far_half[:, :part], near_half[:, :part]),
                                near_half[:, part:]], axis=1)
        partner[t] = mate.astype(i32).astype(i16)

    def whiten_own():
        white = whiten(assemble([combine(i) for i in range(T)]))
        for i in range(T):
            wp[:, samples * i:samples * (i + 1)] = white[i]

    def turn_own():
        for i in range(T):
            wrows = wp[:, pl.ds(pl.multiple_of(i * samples + base, LANES), wide)]
            for a in range(A_):
                rolled = wrows
                if lag_dev % LANES:
                    rolled = pltpu.roll(wrows, wide - FINE * a - rest, 1)
                elif a:
                    rolled = pltpu.roll(wrows, wide - FINE * a, 1)
                wall[a * rows:(a + 1) * rows, samples * i:samples * (i + 1)] = rolled[:, :samples]

    def whiten_sources():
        blocks = []
        for i in range(T):
            first, second = 2.0 * scaled(plain(part_s[2 * i])), 2.0 * scaled(plain(part_s[2 * i + 1]))
            blocks.append(jnp.concatenate([first[:, :part], second], axis=1))
        for i, x in enumerate(whiten(assemble(blocks))):
            src[i] = x

    @pl.when(side == 0)
    def _():
        with jax.named_scope("wait_both"):
            arrived(partner, T - 1, partner_r)
            arrived(part_s, T, twin_r)
        with jax.named_scope("prepare_both"):
            whiten_own()
            whiten_sources()
            turn_own()

    @pl.when(side == 1)
    def _():
        with jax.named_scope("wait_partner"):
            arrived(partner, T - 1, partner_r)
        with jax.named_scope("prepare_own"):
            whiten_own()
            turn_own()
        with jax.named_scope("wait_twin"):
            arrived(part_s, T, twin_r)
        with jax.named_scope("prepare_sources"):
            whiten_sources()

    with jax.named_scope("correlate"):
        z = None
        for i in range(T):
            before = src[i - 1][:, samples - LANES:] if i else jnp.zeros((rows, LANES), bf16)
            srows = jnp.concatenate([src[i], before], axis=1)
            xs = []
            for s in range(STEPS * VS):
                one = jnp.broadcast_to(srows[s:s + 1], (FINE, span))
                xs.append(pltpu.roll(one, 0, 1, stride=1, stride_axis=0)[:, :samples])
            ws = jnp.concatenate([wall[:, samples * i + LANES * p:samples * i + LANES * p + samples] for p in range(P_)],
                                 axis=0)
            term = lax.dot_general(ws, jnp.concatenate(xs, axis=0),
                                   (((1,), (1,)), ((), ())), preferred_element_type=f32)
            z = term if z is None else z + term
        z = z * (1.0 / math.sqrt(window))

    with jax.named_scope("result"):
        lane_group = lane // FINE
        per_tile = LANES // FINE
        span_out = min(lag_dev, LANES)
        for p in range(P_):
            for lo_s in range(0, STEPS * VS, per_tile):
                turned = []
                for a in range(A_):
                    r0 = (p * A_ + a) * rows
                    tile = z[r0:r0 + rows, lo_s * FINE:lo_s * FINE + LANES]
                    turned.append(pltpu.roll(tile, FINE * a, 1) if a else tile)
                for s in range(per_tile):
                    o = turned[0]
                    for a in range(1, A_):
                        o = jnp.where(lane_group == (s + a) % per_tile, turned[a], o)
                    if s:
                        o = pltpu.roll(o, LANES - FINE * s, 1)
                    out_ref[lo_s + s, :, LANES * p:LANES * p + span_out] = o[:, :span_out]

    with jax.named_scope("wait_sends"):
        for buf, count, sem in ((plane, C, plane_s), (own, T - 1, own_s), (partner, T - 1, partner_s),
                                (part_s, 2 * T - 1, twin_s)):
            gone(buf, count, sem)


def shards(records, pair_rows, fir_taps, source_blocks):
    C = lax.axis_size("chan")
    T = lax.axis_size("tm")
    rows, raw = records.shape
    samples = raw // 4
    f32, bf16, i16 = jnp.float32, jnp.bfloat16, jnp.int16
    dma = pltpu.SemaphoreType.DMA
    hbm = pl.BlockSpec(memory_space=pltpu.HBM)
    operands = [pltpu.with_memory_space_constraint(x, pltpu.HBM)
                for x in (fir_taps, pair_rows, source_blocks, records)]
    out = pl.pallas_call(
        functools.partial(body, C, T, rows),
        out_shape=pltpu.VMEM((STEPS * VS, rows, LAGS // T), f32),
        in_specs=[hbm] * 4,
        out_specs=pl.BlockSpec(memory_space=pltpu.VMEM),
        scratch_shapes=[
            pltpu.SMEM(fir_taps.shape, f32),
            pltpu.SMEM(pair_rows.shape, jnp.int32),
            pltpu.SMEM(source_blocks.shape, jnp.int32),
            pltpu.VMEM(records.shape, bf16),
            dma((4,)),
            pltpu.VMEM((2, rows, samples // 2 + LANES), i16),
            pltpu.VMEM((C, rows, samples // 2 + LANES), i16),
            pltpu.VMEM((rows, samples // 2 + LANES), i16),
            pltpu.VMEM((T, rows, samples + LANES), i16),
            pltpu.VMEM((T, rows, samples + LANES), i16),
            pltpu.VMEM((2 * T, rows, samples // 2 + LANES), i16),
            pltpu.VMEM((T, rows, samples), bf16),
            pltpu.VMEM((rows, T * samples + LAGS + LANES), bf16),
            pltpu.VMEM((min(LAGS // T, LANES) // FINE * rows, T * samples + LANES * max(1, LAGS // T // LANES)), bf16),
            dma, dma, dma, dma((T - 1,)), dma, dma, dma, dma((T - 1,)), dma, dma,
        ],
        compiler_params=pltpu.CompilerParams(
            collective_id=0, has_side_effects=True,
            vmem_limit_bytes=(24 if samples * T <= 8192 else 60) * 2**20),
        cost_estimate=pl.CostEstimate(flops=600_000_000, bytes_accessed=1_000_000, transcendentals=0),
    )(*operands)
    return out.reshape(STEPS, VS, rows, LAGS // T)


def solution(mesh):
    return jax.shard_map(
        shards,
        mesh=mesh,
        in_specs=(P("chan", "tm"), P("chan", None), P(), P()),
        out_specs=P(None, None, "chan", "tm"),
        check_vma=False,
    )
```

```python
import functools
import math

import jax
import jax.numpy as jnp
from jax import lax
from jax.experimental import pallas as pl
from jax.experimental.pallas import tpu as pltpu
from jax.sharding import PartitionSpec as P

VS = 8
STEPS = 2
LAGS = 1024
TAPS = 32
LANES = 128
FINE = 16
SPILL = TAPS // 4
FULL = 15
NOTE = 16


def body(C, T, rows, taps_hbm, pair_hbm, blocks_hbm, rec_hbm, out_ref,
         taps_ref, pair_ref, blocks_ref, rec_ref, local_s,
         halves, plane, mate_rest, own, partner, part_s, src, wp, wall,
         plane_s, plane_r, own_s, own_r, mate_r, partner_s, partner_r,
         body_r, twin_s, twin_r):
    me = lax.axis_index("chan")
    t = lax.axis_index("tm")
    f32, bf16, i16, i32 = jnp.float32, jnp.bfloat16, jnp.int16, jnp.int32
    samples = rec_ref.shape[1] // 4
    width = samples + LANES
    part = samples // 2
    half = C // 2
    side = lax.rem(me, 2)
    twin = me + 1 - 2 * side
    lag_dev = LAGS // T
    P_ = max(1, lag_dev // LANES)
    A_ = min(lag_dev, LANES) // FINE
    window = samples * T

    def at_chan(d):
        return lax.rem(me + d, C)

    def at_tm(d):
        return lax.rem(t + d, T)

    def remote(src, dst, ssem, rsem, where):
        return pltpu.make_async_remote_copy(
            src_ref=src, dst_ref=dst, send_sem=ssem, recv_sem=rsem,
            device_id=where, device_id_type=pl.DeviceIdType.MESH)

    def arrived(buf, count, sem):
        blocks = buf.at[pl.ds(0, count)]
        pltpu.make_async_copy(blocks, blocks, sem).wait()

    gone = arrived

    with jax.named_scope("greet"):
        loads = [pltpu.make_async_copy(src, dst, local_s.at[i]) for i, (src, dst) in enumerate((
            (taps_hbm, taps_ref), (rec_hbm, rec_ref), (pair_hbm, pair_ref), (blocks_hbm, blocks_ref)))]
        loads[0].start()
        for g in range(4):
            cut = pl.ds(samples * g, samples)
            pltpu.make_async_copy(rec_hbm.at[:, cut], rec_ref.at[:, cut], local_s.at[1]).start()
        loads[2].start()
        loads[3].start()
        barrier = pltpu.get_barrier_semaphore()
        for d in range(1, C):
            pl.semaphore_signal(barrier, inc=1, device_id={"chan": at_chan(d)}, device_id_type=pl.DeviceIdType.MESH)
        for d in range(1, T):
            pl.semaphore_signal(barrier, inc=1, device_id={"tm": at_tm(d)}, device_id_type=pl.DeviceIdType.MESH)

    with jax.named_scope("band"):
        group = 4 * LANES
        depth = LANES + group
        row = lax.broadcasted_iota(i32, (8, LANES), 0)
        n = lax.broadcasted_iota(i32, (8, LANES), 1)
        tap = 4 * n + 3 - row
        cell = jnp.zeros((8, LANES), f32)
    with jax.named_scope("load_taps"):
        loads[0].wait()
    with jax.named_scope("band_tiles"):
        for k in range(TAPS):
            cell = jnp.where(tap == k, taps_ref[k], cell)
        reach = TAPS // 4 + 1
        tiles = []
        for b in range(depth // 8):
            at = 2 * b - LANES // 4
            tile = jnp.zeros_like(cell)
            if at > -reach:
                tile = pltpu.roll(cell, at % LANES, 1) if at else cell
                if at < 0:
                    tile = jnp.where(n < reach, tile, 0.0)
                elif at + reach > LANES:
                    tile = jnp.where(n >= reach, tile, 0.0)
            tiles.append(tile)
        band = jnp.concatenate(tiles, axis=0)
        hi = band.astype(bf16)
        lo = (band - hi.astype(f32)).astype(bf16)
        band2 = jnp.concatenate([hi, lo], axis=1)
    with jax.named_scope("load_records"):
        for load in loads[1:]:
            load.wait()

    groups = samples // LANES
    lane = lax.broadcasted_iota(i32, (rows, LANES), 1)

    def encode(x):
        peak = jnp.maximum(jnp.max(jnp.abs(x), axis=1, keepdims=True), 1e-30)
        e = jnp.floor(jnp.log2(peak)) + 1.0
        return jnp.clip(jnp.round(x * jnp.exp2(FULL - e)), -32767.0, 32767.0).astype(i32), e

    def scaled(v):
        at = v.shape[1] - LANES + SPILL
        return v * jnp.exp2(v[:, at:at + 1] - (FULL + 1))

    def plain(x):
        return x.astype(i32).astype(f32)

    def permuted(at, x):
        out = []
        for h in range(at.shape[0] // 8):
            want = at[8 * h:8 * h + 8]
            cols = []
            for g in range(x.shape[1] // LANES):
                tile = x[:, LANES * g:LANES * (g + 1)]
                got = jnp.take_along_axis(tile[:8], want & 7, axis=0)
                for v in range(1, rows // 8):
                    more = jnp.take_along_axis(tile[8 * v:8 * v + 8], want & 7, axis=0)
                    got = jnp.where((want >> 3) == v, more, got)
                cols.append(got)
            out.append(jnp.concatenate(cols, axis=1))
        return jnp.concatenate(out, axis=0)

    with jax.named_scope("filter"):
        raw = rec_ref[...]
        parts = []
        for g in range(groups):
            if g == 0:
                first = jnp.zeros((rows, LANES), bf16)
            else:
                first = raw[:, group * g - LANES:group * g]
            parts.append(jnp.concatenate([first, raw[:, group * g:group * (g + 1)]], axis=1))
        both = jnp.dot(jnp.concatenate(parts, axis=0), band2, preferred_element_type=f32)
        both = both[:, :LANES] + both[:, LANES:]
        edge = jnp.dot(raw[:, group * groups - LANES:], band2[:LANES], preferred_element_type=f32)
        edge = edge[:, :LANES] + edge[:, LANES:]
        filtered = jnp.concatenate([both[rows * g:rows * (g + 1)] for g in range(groups)] + [edge], axis=1)
        rr = lax.broadcasted_iota(i32, (rows, LANES), 0)
        pick = jnp.zeros((rows, LANES), i32)
        for r in range(rows):
            pick = jnp.where(rr == r, pair_ref[0, r], pick)
        q, e = encode(filtered)
        note = jnp.where(lane == SPILL, e.astype(i32), jnp.where(lane == SPILL + 1, pick, q[:, samples:])).astype(i16)
        q = q[:, :samples].astype(i16)
        own[t] = q
        halves[0] = jnp.concatenate([q[:, :part], note], axis=1)
        halves[1] = jnp.concatenate([q[:, part:], note], axis=1)
        plane[me] = halves[side]

    with jax.named_scope("wait_greeting"):
        pl.semaphore_wait(barrier, C + T - 2)

    with jax.named_scope("send_filtered"):
        others = [d for d in range(1, C) if d != half]
        mate_copy = remote(halves.at[lax.rem(side + half + 1, 2)], mate_rest, plane_s, mate_r, {"chan": at_chan(half)})
        others = [half] + others
        sends = [remote(halves.at[lax.rem(side + d, 2)], plane.at[me], plane_s, plane_r,
                         {"chan": at_chan(d)}) for d in others]
        sends += [remote(own.at[t], own.at[t], own_s, own_r.at[d - 1], {"tm": at_tm(d)}) for d in range(1, T)]
        sends = sends[:C - 1] + [mate_copy] + sends[C - 1:]
        for s in sends:
            s.start()

    with jax.named_scope("clear"):
        wp[:, window:] = jnp.zeros((rows, wp.shape[1] - window), bf16)
        wall[:, window:] = jnp.zeros((wall.shape[0], LANES * P_), bf16)

    low = t < T // 2
    def near(k):
        up = jnp.where(k >= t, k + 1, k)
        slot = jnp.where(low, up, lax.rem(t - 1 - k + T, T))
        return slot, lax.rem(t - slot + T, T)

    def relay(k):
        slot, d = near(k)
        remote(own.at[slot], own.at[slot], own_s, own_r.at[d - 1], {"tm": at_tm(d)}).wait_recv()
        s = remote(own.at[slot], partner.at[slot], partner_s, partner_r, {"chan": at_chan(half)})
        s.start()

    def combine(slot):
        note = plain(part_s[2 * slot + side][:, part:])
        mine, theirs = (jnp.concatenate([plain(buf[slot]), pltpu.roll(note, LANES - NOTE * g, 1)], axis=1)
                        for g, buf in ((1, own), (2, partner)))
        return scaled(mine) + scaled(permuted(pick, theirs))

    with jax.named_scope("relay_first"):
        relay(0)

    with jax.named_scope("wait_plane"):
        arrived(plane, C - 1, plane_r)

    early = range(1, min(2, T - 1))
    with jax.named_scope("relay_early"):
        @pl.when(low)
        def _():
            for k in early:
                relay(k)

    with jax.named_scope("pick"):
        picked = []
        per = rows // VS

        def halved(x, within):
            y = x[:VS]
            for q in range(1, per):
                y = jnp.where(within == q, x[VS * q:VS * (q + 1)], y)
            return y

        for step in range(STEPS):
            blk = blocks_ref[step]
            owner = lax.div(blk, per)
            within = lax.rem(blk, per)
            mine = halved(plain(plane[owner]), within)
            pair = mine[:, part + SPILL + 1:part + SPILL + 2].astype(i32)
            theirs = permuted(jnp.broadcast_to(pair, (VS, LANES)), plain(plane[lax.rem(owner + half, C)]))
            first, second = (x[:, part + SPILL:part + SPILL + 1] for x in (mine, theirs))
            top = jnp.maximum(first, second)
            q = jnp.round(mine * jnp.exp2(first - top - 1.0) + theirs * jnp.exp2(second - top - 1.0))
            last = jnp.where(lane[:VS] == SPILL, top, q[:, part:])
            picked.append(jnp.concatenate([q[:, :part], last], axis=1))
        x = jnp.concatenate(picked, axis=0)
        notes = [pltpu.roll(plain(plane[at][:, part:]), NOTE * g, 1) for g, at in ((1, me), (2, at_chan(half)))]
        last = jnp.where(lane < NOTE, x[:, part:], jnp.where(lane < 2 * NOTE, *notes))
        x = jnp.concatenate([x[:, :part], last], axis=1).astype(i32).astype(i16)
        mine_at = 2 * t + side
        part_s[mine_at] = x

        def twin_copy(d, at):
            return remote(part_s.at[at], part_s.at[at], twin_s, twin_r, {"chan": twin})

        def body_copy(d, at):
            return remote(part_s.at[at], part_s.at[at], twin_s, body_r.at[d - 1], {"tm": at_tm(d)})

        ts_sends = [body_copy(d, mine_at) for d in range(1, T)] + [twin_copy(0, mine_at)]
        for s in ts_sends:
            s.start()

    with jax.named_scope("relay"):
        @pl.when(jnp.logical_not(low))
        def _():
            for k in early:
                relay(k)
        for k in range(early.stop, T - 1):
            relay(k)

    lag0 = t * lag_dev
    wide = samples + LANES
    span = samples + LANES
    if lag_dev % LANES == 0:
        base, rest = lag0, 0
    else:
        base = lax.div(lag0, LANES) * LANES
        rest = lax.rem(lag0, LANES)

    def hand_to_twin(k):
        slot, d = near(k)
        body_copy(d, 2 * slot + side).wait_recv()
        twin_copy(d, 2 * slot + side).start()

    def assemble(blocks):
        out = []
        for i, x in enumerate(blocks):
            head = x[:, :LANES]
            if i:
                head = head + jnp.where(lane < SPILL, blocks[i - 1][:, samples:], 0.0)
            out.append(jnp.concatenate([head, x[:, LANES:samples]], axis=1))
        return out

    def whiten(blocks):
        acc = jnp.zeros((rows, LANES), f32)
        for x in blocks:
            sq = x * x
            for g in range(groups):
                acc = acc + sq[:, LANES * g:LANES * (g + 1)]
        scale = lax.rsqrt(jnp.sum(acc, axis=1, keepdims=True) / window + 1e-6)
        return [(x * scale).astype(bf16) for x in blocks]

    with jax.named_scope("hand_to_twin"):
        for k in range(T - 1):
            hand_to_twin(k)
    with jax.named_scope("own_block"):
        mate_copy.wait_recv()
        near_half, far_half = plain(plane[at_chan(half)]), plain(mate_rest[...])
        mate = jnp.concatenate([jnp.where(side == 0, near_half[:, :part], far_half[:, :part]),
                                jnp.where(side == 0, far_half[:, :part], near_half[:, :part])], axis=1)
        partner[t] = mate.astype(i32).astype(i16)

    def whiten_own():
        white = whiten(assemble([combine(i) for i in range(T)]))
        for i in range(T):
            wp[:, samples * i:samples * (i + 1)] = white[i]

    def turn_own():
        for i in range(T):
            wrows = wp[:, pl.ds(pl.multiple_of(i * samples + base, LANES), wide)]
            for a in range(A_):
                rolled = wrows
                if lag_dev % LANES:
                    rolled = pltpu.roll(wrows, wide - FINE * a - rest, 1)
                elif a:
                    rolled = pltpu.roll(wrows, wide - FINE * a, 1)
                wall[a * rows:(a + 1) * rows, samples * i:samples * (i + 1)] = rolled[:, :samples]

    def whiten_sources():
        blocks = []
        for i in range(T):
            first, second = 2.0 * scaled(plain(part_s[2 * i])), 2.0 * scaled(plain(part_s[2 * i + 1]))
            blocks.append(jnp.concatenate([first[:, :part], second], axis=1))
        for i, x in enumerate(whiten(assemble(blocks))):
            src[i] = x

    with jax.named_scope("wait_partner"):
        arrived(partner, T - 1, partner_r)
    with jax.named_scope("prepare_own"):
        whiten_own()
        turn_own()
    with jax.named_scope("wait_twin"):
        arrived(part_s, T, twin_r)
    with jax.named_scope("prepare_sources"):
        whiten_sources()

    with jax.named_scope("correlate"):
        z = None
        for i in range(T):
            before = src[i - 1][:, samples - LANES:] if i else jnp.zeros((rows, LANES), bf16)
            srows = jnp.concatenate([src[i], before], axis=1)
            xs = []
            for s in range(STEPS * VS):
                one = jnp.broadcast_to(srows[s:s + 1], (FINE, span))
                xs.append(pltpu.roll(one, 0, 1, stride=1, stride_axis=0)[:, :samples])
            ws = jnp.concatenate([wall[:, samples * i + LANES * p:samples * i + LANES * p + samples] for p in range(P_)],
                                 axis=0)
            term = lax.dot_general(ws, jnp.concatenate(xs, axis=0),
                                   (((1,), (1,)), ((), ())), preferred_element_type=f32)
            z = term if z is None else z + term
        z = z * (1.0 / math.sqrt(window))

    with jax.named_scope("result"):
        lane_group = lane // FINE
        per_tile = LANES // FINE
        span_out = min(lag_dev, LANES)
        for p in range(P_):
            for lo_s in range(0, STEPS * VS, per_tile):
                turned = []
                for a in range(A_):
                    r0 = (p * A_ + a) * rows
                    tile = z[r0:r0 + rows, lo_s * FINE:lo_s * FINE + LANES]
                    turned.append(pltpu.roll(tile, FINE * a, 1) if a else tile)
                for s in range(per_tile):
                    o = turned[0]
                    for a in range(1, A_):
                        o = jnp.where(lane_group == (s + a) % per_tile, turned[a], o)
                    if s:
                        o = pltpu.roll(o, LANES - FINE * s, 1)
                    out_ref[lo_s + s, :, LANES * p:LANES * p + span_out] = o[:, :span_out]

    with jax.named_scope("wait_sends"):
        for buf, count, sem in ((plane, C, plane_s), (own, T - 1, own_s), (partner, T - 1, partner_s),
                                (part_s, 2 * T - 1, twin_s)):
            gone(buf, count, sem)


def shards(records, pair_rows, fir_taps, source_blocks):
    C = lax.axis_size("chan")
    T = lax.axis_size("tm")
    rows, raw = records.shape
    samples = raw // 4
    f32, bf16, i16 = jnp.float32, jnp.bfloat16, jnp.int16
    dma = pltpu.SemaphoreType.DMA
    hbm = pl.BlockSpec(memory_space=pltpu.HBM)
    operands = [pltpu.with_memory_space_constraint(x, pltpu.HBM)
                for x in (fir_taps, pair_rows, source_blocks, records)]
    out = pl.pallas_call(
        functools.partial(body, C, T, rows),
        out_shape=pltpu.VMEM((STEPS * VS, rows, LAGS // T), f32),
        in_specs=[hbm] * 4,
        out_specs=pl.BlockSpec(memory_space=pltpu.VMEM),
        scratch_shapes=[
            pltpu.SMEM(fir_taps.shape, f32),
            pltpu.SMEM(pair_rows.shape, jnp.int32),
            pltpu.SMEM(source_blocks.shape, jnp.int32),
            pltpu.VMEM(records.shape, bf16),
            dma((4,)),
            pltpu.VMEM((2, rows, samples // 2 + LANES), i16),
            pltpu.VMEM((C, rows, samples // 2 + LANES), i16),
            pltpu.VMEM((rows, samples // 2 + LANES), i16),
            pltpu.VMEM((T, rows, samples), i16),
            pltpu.VMEM((T, rows, samples), i16),
            pltpu.VMEM((2 * T, rows, samples // 2 + LANES), i16),
            pltpu.VMEM((T, rows, samples), bf16),
            pltpu.VMEM((rows, T * samples + LAGS + LANES), bf16),
            pltpu.VMEM((min(LAGS // T, LANES) // FINE * rows, T * samples + LANES * max(1, LAGS // T // LANES)), bf16),
            dma, dma, dma, dma((T - 1,)), dma, dma, dma, dma((T - 1,)), dma, dma,
        ],
        compiler_params=pltpu.CompilerParams(
            collective_id=0, has_side_effects=True,
            vmem_limit_bytes=(24 if samples * T <= 8192 else 60) * 2**20),
        cost_estimate=pl.CostEstimate(flops=600_000_000, bytes_accessed=1_000_000, transcendentals=0),
    )(*operands)
    return out.reshape(STEPS, VS, rows, LAGS // T)


def solution(mesh):
    return jax.shard_map(
        shards,
        mesh=mesh,
        in_specs=(P("chan", "tm"), P("chan", None), P(), P()),
        out_specs=P(None, None, "chan", "tm"),
        check_vma=False,
    )
```

```python
import functools
import math

import jax
import jax.numpy as jnp
from jax import lax
from jax.experimental import pallas as pl
from jax.experimental.pallas import tpu as pltpu
from jax.sharding import PartitionSpec as P

VS = 8
STEPS = 2
LAGS = 1024
TAPS = 32
LANES = 128
FINE = 16
SPILL = TAPS // 4
FULL = 15
NOTE = 16


def body(C, T, rows, taps_hbm, pair_hbm, blocks_hbm, rec_hbm, out_ref,
         taps_ref, pair_ref, blocks_ref, rec_ref, local_s,
         halves, plane, mate_rest, own, partner, part_s, src, wp, wall,
         plane_s, plane_r, own_s, own_r, mate_r, partner_s, partner_r,
         body_r, twin_s, twin_r):
    me = lax.axis_index("chan")
    t = lax.axis_index("tm")
    f32, bf16, i16, i32 = jnp.float32, jnp.bfloat16, jnp.int16, jnp.int32
    samples = rec_ref.shape[1] // 4
    width = samples + LANES
    part = samples // 2
    half = C // 2
    side = lax.rem(me, 2)
    twin = me + 1 - 2 * side
    lag_dev = LAGS // T
    P_ = max(1, lag_dev // LANES)
    A_ = min(lag_dev, LANES) // FINE
    window = samples * T

    def at_chan(d):
        return lax.rem(me + d, C)

    def at_tm(d):
        return lax.rem(t + d, T)

    def remote(src, dst, ssem, rsem, where):
        return pltpu.make_async_remote_copy(
            src_ref=src, dst_ref=dst, send_sem=ssem, recv_sem=rsem,
            device_id=where, device_id_type=pl.DeviceIdType.MESH)

    def arrived(buf, count, sem):
        blocks = buf.at[pl.ds(0, count)]
        pltpu.make_async_copy(blocks, blocks, sem).wait()

    gone = arrived

    with jax.named_scope("greet"):
        loads = [pltpu.make_async_copy(src, dst, local_s.at[i]) for i, (src, dst) in enumerate((
            (taps_hbm, taps_ref), (rec_hbm, rec_ref), (pair_hbm, pair_ref), (blocks_hbm, blocks_ref)))]
        loads[0].start()
        for g in range(4):
            cut = pl.ds(samples * g, samples)
            pltpu.make_async_copy(rec_hbm.at[:, cut], rec_ref.at[:, cut], local_s.at[1]).start()
        loads[2].start()
        loads[3].start()
        barrier = pltpu.get_barrier_semaphore()
        for d in range(1, C):
            pl.semaphore_signal(barrier, inc=1, device_id={"chan": at_chan(d)}, device_id_type=pl.DeviceIdType.MESH)
        for d in range(1, T):
            pl.semaphore_signal(barrier, inc=1, device_id={"tm": at_tm(d)}, device_id_type=pl.DeviceIdType.MESH)

    with jax.named_scope("band"):
        group = 4 * LANES
        depth = LANES + group
        row = lax.broadcasted_iota(i32, (8, LANES), 0)
        n = lax.broadcasted_iota(i32, (8, LANES), 1)
        tap = 4 * n + 3 - row
        cell = jnp.zeros((8, LANES), f32)
    with jax.named_scope("load_taps"):
        loads[0].wait()
    with jax.named_scope("band_tiles"):
        for k in range(TAPS):
            cell = jnp.where(tap == k, taps_ref[k], cell)
        reach = TAPS // 4 + 1
        tiles = []
        for b in range(depth // 8):
            at = 2 * b - LANES // 4
            tile = jnp.zeros_like(cell)
            if at > -reach:
                tile = pltpu.roll(cell, at % LANES, 1) if at else cell
                if at < 0:
                    tile = jnp.where(n < reach, tile, 0.0)
                elif at + reach > LANES:
                    tile = jnp.where(n >= reach, tile, 0.0)
            tiles.append(tile)
        band = jnp.concatenate(tiles, axis=0)
        hi = band.astype(bf16)
        lo = (band - hi.astype(f32)).astype(bf16)
        band2 = jnp.concatenate([hi, lo], axis=1)
    with jax.named_scope("load_records"):
        for load in loads[1:]:
            load.wait()

    groups = samples // LANES
    lane = lax.broadcasted_iota(i32, (rows, LANES), 1)

    def encode(x):
        peak = jnp.maximum(jnp.max(jnp.abs(x), axis=1, keepdims=True), 1e-30)
        e = jnp.floor(jnp.log2(peak)) + 1.0
        return jnp.clip(jnp.round(x * jnp.exp2(FULL - e)), -32767.0, 32767.0).astype(i32), e

    def scaled(v):
        at = v.shape[1] - LANES + SPILL
        return v * jnp.exp2(v[:, at:at + 1] - (FULL + 1))

    def plain(x):
        return x.astype(i32).astype(f32)

    def permuted(at, x):
        out = []
        for h in range(at.shape[0] // 8):
            want = at[8 * h:8 * h + 8]
            cols = []
            for g in range(x.shape[1] // LANES):
                tile = x[:, LANES * g:LANES * (g + 1)]
                got = jnp.take_along_axis(tile[:8], want & 7, axis=0)
                for v in range(1, rows // 8):
                    more = jnp.take_along_axis(tile[8 * v:8 * v + 8], want & 7, axis=0)
                    got = jnp.where((want >> 3) == v, more, got)
                cols.append(got)
            out.append(jnp.concatenate(cols, axis=1))
        return jnp.concatenate(out, axis=0)

    with jax.named_scope("filter"):
        raw = rec_ref[...]
        parts = []
        for g in range(groups):
            if g == 0:
                first = jnp.zeros((rows, LANES), bf16)
            else:
                first = raw[:, group * g - LANES:group * g]
            parts.append(jnp.concatenate([first, raw[:, group * g:group * (g + 1)]], axis=1))
        both = jnp.dot(jnp.concatenate(parts, axis=0), band2, preferred_element_type=f32)
        both = both[:, :LANES] + both[:, LANES:]
        edge = jnp.dot(raw[:, group * groups - LANES:], band2[:LANES], preferred_element_type=f32)
        edge = edge[:, :LANES] + edge[:, LANES:]
        filtered = jnp.concatenate([both[rows * g:rows * (g + 1)] for g in range(groups)] + [edge], axis=1)
        rr = lax.broadcasted_iota(i32, (rows, LANES), 0)
        pick = jnp.zeros((rows, LANES), i32)
        for r in range(rows):
            pick = jnp.where(rr == r, pair_ref[0, r], pick)
        q, e = encode(filtered)
        note = jnp.where(lane == SPILL, e.astype(i32), jnp.where(lane == SPILL + 1, pick, q[:, samples:])).astype(i16)
        q = q[:, :samples].astype(i16)
        own[t] = q
        halves[0] = jnp.concatenate([q[:, :part], note], axis=1)
        halves[1] = jnp.concatenate([q[:, part:], note], axis=1)
        plane[me] = halves[side]

    with jax.named_scope("wait_greeting"):
        pl.semaphore_wait(barrier, C + T - 2)

    with jax.named_scope("send_filtered"):
        others = [d for d in range(1, C) if d != half]
        mate_copy = remote(halves.at[lax.rem(side + half + 1, 2)], mate_rest, plane_s, mate_r, {"chan": at_chan(half)})
        others = [half] + others
        sends = [remote(halves.at[lax.rem(side + d, 2)], plane.at[me], plane_s, plane_r,
                         {"chan": at_chan(d)}) for d in others]
        sends += [remote(own.at[t], own.at[t], own_s, own_r.at[d - 1], {"tm": at_tm(d)}) for d in range(1, T)]
        sends = sends[:C - 1] + [mate_copy] + sends[C - 1:]
        for s in sends:
            s.start()

    with jax.named_scope("clear"):
        wp[:, window:] = jnp.zeros((rows, wp.shape[1] - window), bf16)
        wall[:, window:] = jnp.zeros((wall.shape[0], LANES * P_), bf16)

    low = t < T // 2
    def near(k):
        up = jnp.where(k >= t, k + 1, k)
        slot = jnp.where(low, up, lax.rem(t - 1 - k + T, T))
        return slot, lax.rem(t - slot + T, T)

    def relay(k):
        slot, d = near(k)
        remote(own.at[slot], own.at[slot], own_s, own_r.at[d - 1], {"tm": at_tm(d)}).wait_recv()
        s = remote(own.at[slot], partner.at[slot], partner_s, partner_r, {"chan": at_chan(half)})
        s.start()

    def combine(slot):
        note = plain(part_s[2 * slot + side][:, part:])
        mine, theirs = (jnp.concatenate([plain(buf[slot]), pltpu.roll(note, LANES - NOTE * g, 1)], axis=1)
                        for g, buf in ((1, own), (2, partner)))
        return scaled(mine) + scaled(permuted(pick, theirs))

    @pl.when(t == 0)
    def _():
        with jax.named_scope("relay_all"):
            for k in (1, 0, *range(2, T - 1)) if T > 2 else range(T - 1):
                relay(k)

    @pl.when(t > 0)
    def _():
        with jax.named_scope("relay_first"):
            relay(0)

    with jax.named_scope("wait_plane"):
        arrived(plane, C - 1, plane_r)

    with jax.named_scope("pick"):
        picked = []
        per = rows // VS

        def halved(x, within):
            y = x[:VS]
            for q in range(1, per):
                y = jnp.where(within == q, x[VS * q:VS * (q + 1)], y)
            return y

        for step in range(STEPS):
            blk = blocks_ref[step]
            owner = lax.div(blk, per)
            within = lax.rem(blk, per)
            mine = halved(plain(plane[owner]), within)
            pair = mine[:, part + SPILL + 1:part + SPILL + 2].astype(i32)
            theirs = permuted(jnp.broadcast_to(pair, (VS, LANES)), plain(plane[lax.rem(owner + half, C)]))
            first, second = (x[:, part + SPILL:part + SPILL + 1] for x in (mine, theirs))
            top = jnp.maximum(first, second)
            q = jnp.round(mine * jnp.exp2(first - top - 1.0) + theirs * jnp.exp2(second - top - 1.0))
            last = jnp.where(lane[:VS] == SPILL, top, q[:, part:])
            picked.append(jnp.concatenate([q[:, :part], last], axis=1))
        x = jnp.concatenate(picked, axis=0)
        notes = [pltpu.roll(plain(plane[at][:, part:]), NOTE * g, 1) for g, at in ((1, me), (2, at_chan(half)))]
        last = jnp.where(lane < NOTE, x[:, part:], jnp.where(lane < 2 * NOTE, *notes))
        x = jnp.concatenate([x[:, :part], last], axis=1).astype(i32).astype(i16)
        mine_at = 2 * t + side
        part_s[mine_at] = x

        def twin_copy(d, at):
            return remote(part_s.at[at], part_s.at[at], twin_s, twin_r, {"chan": twin})

        def body_copy(d, at):
            return remote(part_s.at[at], part_s.at[at], twin_s, body_r.at[d - 1], {"tm": at_tm(d)})

        ts_sends = [body_copy(d, mine_at) for d in range(1, T)] + [twin_copy(0, mine_at)]
        for s in ts_sends:
            s.start()

    with jax.named_scope("relay"):
        @pl.when(t > 0)
        def _():
            for k in range(1, T - 1):
                relay(k)

    lag0 = t * lag_dev
    wide = samples + LANES
    span = samples + LANES
    if lag_dev % LANES == 0:
        base, rest = lag0, 0
    else:
        base = lax.div(lag0, LANES) * LANES
        rest = lax.rem(lag0, LANES)

    def hand_to_twin(k):
        slot, d = near(k)
        body_copy(d, 2 * slot + side).wait_recv()
        twin_copy(d, 2 * slot + side).start()

    def assemble(blocks):
        out = []
        for i, x in enumerate(blocks):
            head = x[:, :LANES]
            if i:
                head = head + jnp.where(lane < SPILL, blocks[i - 1][:, samples:], 0.0)
            out.append(jnp.concatenate([head, x[:, LANES:samples]], axis=1))
        return out

    def whiten(blocks):
        acc = jnp.zeros((rows, LANES), f32)
        for x in blocks:
            sq = x * x
            for g in range(groups):
                acc = acc + sq[:, LANES * g:LANES * (g + 1)]
        scale = lax.rsqrt(jnp.sum(acc, axis=1, keepdims=True) / window + 1e-6)
        return [(x * scale).astype(bf16) for x in blocks]

    with jax.named_scope("hand_to_twin"):
        for k in range(T - 1):
            hand_to_twin(k)
    with jax.named_scope("own_block"):
        mate_copy.wait_recv()
        near_half, far_half = plain(plane[at_chan(half)]), plain(mate_rest[...])
        mate = jnp.concatenate([jnp.where(side == 0, near_half[:, :part], far_half[:, :part]),
                                jnp.where(side == 0, far_half[:, :part], near_half[:, :part])], axis=1)
        partner[t] = mate.astype(i32).astype(i16)

    def whiten_own():
        white = whiten(assemble([combine(i) for i in range(T)]))
        for i in range(T):
            wp[:, samples * i:samples * (i + 1)] = white[i]

    def turn_own():
        for i in range(T):
            wrows = wp[:, pl.ds(pl.multiple_of(i * samples + base, LANES), wide)]
            for a in range(A_):
                rolled = wrows
                if lag_dev % LANES:
                    rolled = pltpu.roll(wrows, wide - FINE * a - rest, 1)
                elif a:
                    rolled = pltpu.roll(wrows, wide - FINE * a, 1)
                wall[a * rows:(a + 1) * rows, samples * i:samples * (i + 1)] = rolled[:, :samples]

    def whiten_sources():
        blocks = []
        for i in range(T):
            first, second = 2.0 * scaled(plain(part_s[2 * i])), 2.0 * scaled(plain(part_s[2 * i + 1]))
            blocks.append(jnp.concatenate([first[:, :part], second], axis=1))
        for i, x in enumerate(whiten(assemble(blocks))):
            src[i] = x

    with jax.named_scope("wait_partner"):
        arrived(partner, T - 1, partner_r)
    with jax.named_scope("prepare_own"):
        whiten_own()
        turn_own()
    with jax.named_scope("wait_twin"):
        arrived(part_s, T, twin_r)
    with jax.named_scope("prepare_sources"):
        whiten_sources()

    with jax.named_scope("correlate"):
        z = None
        for i in range(T):
            before = src[i - 1][:, samples - LANES:] if i else jnp.zeros((rows, LANES), bf16)
            srows = jnp.concatenate([src[i], before], axis=1)
            xs = []
            for s in range(STEPS * VS):
                one = jnp.broadcast_to(srows[s:s + 1], (FINE, span))
                xs.append(pltpu.roll(one, 0, 1, stride=1, stride_axis=0)[:, :samples])
            ws = jnp.concatenate([wall[:, samples * i + LANES * p:samples * i + LANES * p + samples] for p in range(P_)],
                                 axis=0)
            term = lax.dot_general(ws, jnp.concatenate(xs, axis=0),
                                   (((1,), (1,)), ((), ())), preferred_element_type=f32)
            z = term if z is None else z + term
        z = z * (1.0 / math.sqrt(window))

    with jax.named_scope("result"):
        lane_group = lane // FINE
        per_tile = LANES // FINE
        span_out = min(lag_dev, LANES)
        for p in range(P_):
            for lo_s in range(0, STEPS * VS, per_tile):
                turned = []
                for a in range(A_):
                    r0 = (p * A_ + a) * rows
                    tile = z[r0:r0 + rows, lo_s * FINE:lo_s * FINE + LANES]
                    turned.append(pltpu.roll(tile, FINE * a, 1) if a else tile)
                for s in range(per_tile):
                    o = turned[0]
                    for a in range(1, A_):
                        o = jnp.where(lane_group == (s + a) % per_tile, turned[a], o)
                    if s:
                        o = pltpu.roll(o, LANES - FINE * s, 1)
                    out_ref[lo_s + s, :, LANES * p:LANES * p + span_out] = o[:, :span_out]

    with jax.named_scope("wait_sends"):
        for buf, count, sem in ((plane, C, plane_s), (own, T - 1, own_s), (partner, T - 1, partner_s),
                                (part_s, 2 * T - 1, twin_s)):
            gone(buf, count, sem)


def shards(records, pair_rows, fir_taps, source_blocks):
    C = lax.axis_size("chan")
    T = lax.axis_size("tm")
    rows, raw = records.shape
    samples = raw // 4
    f32, bf16, i16 = jnp.float32, jnp.bfloat16, jnp.int16
    dma = pltpu.SemaphoreType.DMA
    hbm = pl.BlockSpec(memory_space=pltpu.HBM)
    operands = [pltpu.with_memory_space_constraint(x, pltpu.HBM)
                for x in (fir_taps, pair_rows, source_blocks, records)]
    out = pl.pallas_call(
        functools.partial(body, C, T, rows),
        out_shape=pltpu.VMEM((STEPS * VS, rows, LAGS // T), f32),
        in_specs=[hbm] * 4,
        out_specs=pl.BlockSpec(memory_space=pltpu.VMEM),
        scratch_shapes=[
            pltpu.SMEM(fir_taps.shape, f32),
            pltpu.SMEM(pair_rows.shape, jnp.int32),
            pltpu.SMEM(source_blocks.shape, jnp.int32),
            pltpu.VMEM(records.shape, bf16),
            dma((4,)),
            pltpu.VMEM((2, rows, samples // 2 + LANES), i16),
            pltpu.VMEM((C, rows, samples // 2 + LANES), i16),
            pltpu.VMEM((rows, samples // 2 + LANES), i16),
            pltpu.VMEM((T, rows, samples), i16),
            pltpu.VMEM((T, rows, samples), i16),
            pltpu.VMEM((2 * T, rows, samples // 2 + LANES), i16),
            pltpu.VMEM((T, rows, samples), bf16),
            pltpu.VMEM((rows, T * samples + LAGS + LANES), bf16),
            pltpu.VMEM((min(LAGS // T, LANES) // FINE * rows, T * samples + LANES * max(1, LAGS // T // LANES)), bf16),
            dma, dma, dma, dma((T - 1,)), dma, dma, dma, dma((T - 1,)), dma, dma,
        ],
        compiler_params=pltpu.CompilerParams(
            collective_id=0, has_side_effects=True,
            vmem_limit_bytes=(24 if samples * T <= 8192 else 60) * 2**20),
        cost_estimate=pl.CostEstimate(flops=600_000_000, bytes_accessed=1_000_000, transcendentals=0),
    )(*operands)
    return out.reshape(STEPS, VS, rows, LAGS // T)


def solution(mesh):
    return jax.shard_map(
        shards,
        mesh=mesh,
        in_specs=(P("chan", "tm"), P("chan", None), P(), P()),
        out_specs=P(None, None, "chan", "tm"),
        check_vma=False,
    )
```

```python
import functools
import math

import jax
import jax.numpy as jnp
from jax import lax
from jax.experimental import pallas as pl
from jax.experimental.pallas import tpu as pltpu
from jax.sharding import PartitionSpec as P

VS = 8
STEPS = 2
LAGS = 1024
TAPS = 32
LANES = 128
FINE = 16
SPILL = TAPS // 4
FULL = 15
NOTE = 16


def body(C, T, rows, taps_hbm, pair_hbm, blocks_hbm, rec_hbm, out_ref,
         taps_ref, pair_ref, blocks_ref, rec_ref, local_s,
         halves, plane, mate_rest, own, partner, gathered, part_s, src, wp, wall,
         plane_s, plane_r, own_s, own_r, mate_r, partner_s, partner_r,
         body_r, twin_s, twin_r):
    me = lax.axis_index("chan")
    t = lax.axis_index("tm")
    f32, bf16, i16, i32 = jnp.float32, jnp.bfloat16, jnp.int16, jnp.int32
    samples = rec_ref.shape[1] // 4
    width = samples + LANES
    part = samples // 2
    half = C // 2
    side = lax.rem(me, 2)
    twin = me + 1 - 2 * side
    lag_dev = LAGS // T
    P_ = max(1, lag_dev // LANES)
    A_ = min(lag_dev, LANES) // FINE
    window = samples * T

    def at_chan(d):
        return lax.rem(me + d, C)

    def at_tm(d):
        return lax.rem(t + d, T)

    def remote(src, dst, ssem, rsem, where):
        return pltpu.make_async_remote_copy(
            src_ref=src, dst_ref=dst, send_sem=ssem, recv_sem=rsem,
            device_id=where, device_id_type=pl.DeviceIdType.MESH)

    def arrived(buf, count, sem):
        blocks = buf.at[pl.ds(0, count)]
        pltpu.make_async_copy(blocks, blocks, sem).wait()

    gone = arrived

    with jax.named_scope("greet"):
        loads = [pltpu.make_async_copy(src, dst, local_s.at[i]) for i, (src, dst) in enumerate((
            (taps_hbm, taps_ref), (rec_hbm, rec_ref), (pair_hbm, pair_ref), (blocks_hbm, blocks_ref)))]
        loads[0].start()
        for g in range(4):
            cut = pl.ds(samples * g, samples)
            pltpu.make_async_copy(rec_hbm.at[:, cut], rec_ref.at[:, cut], local_s.at[1]).start()
        loads[2].start()
        loads[3].start()
        barrier = pltpu.get_barrier_semaphore()
        for d in range(1, C):
            pl.semaphore_signal(barrier, inc=1, device_id={"chan": at_chan(d)}, device_id_type=pl.DeviceIdType.MESH)
        for d in range(1, T):
            pl.semaphore_signal(barrier, inc=1, device_id={"tm": at_tm(d)}, device_id_type=pl.DeviceIdType.MESH)

    with jax.named_scope("band"):
        group = 4 * LANES
        depth = LANES + group
        row = lax.broadcasted_iota(i32, (8, LANES), 0)
        n = lax.broadcasted_iota(i32, (8, LANES), 1)
        tap = 4 * n + 3 - row
        cell = jnp.zeros((8, LANES), f32)
    with jax.named_scope("load_taps"):
        loads[0].wait()
    with jax.named_scope("band_tiles"):
        for k in range(TAPS):
            cell = jnp.where(tap == k, taps_ref[k], cell)
        reach = TAPS // 4 + 1
        tiles = []
        for b in range(depth // 8):
            at = 2 * b - LANES // 4
            tile = jnp.zeros_like(cell)
            if at > -reach:
                tile = pltpu.roll(cell, at % LANES, 1) if at else cell
                if at < 0:
                    tile = jnp.where(n < reach, tile, 0.0)
                elif at + reach > LANES:
                    tile = jnp.where(n >= reach, tile, 0.0)
            tiles.append(tile)
        band = jnp.concatenate(tiles, axis=0)
        hi = band.astype(bf16)
        lo = (band - hi.astype(f32)).astype(bf16)
        band2 = jnp.concatenate([hi, lo], axis=1)
    with jax.named_scope("load_records"):
        for load in loads[1:]:
            load.wait()

    groups = samples // LANES
    lane = lax.broadcasted_iota(i32, (rows, LANES), 1)

    def encode(x):
        peak = jnp.maximum(jnp.max(jnp.abs(x), axis=1, keepdims=True), 1e-30)
        e = jnp.floor(jnp.log2(peak)) + 1.0
        return jnp.clip(jnp.round(x * jnp.exp2(FULL - e)), -32767.0, 32767.0).astype(i32), e

    def scaled(v):
        at = v.shape[1] - LANES + SPILL
        return v * jnp.exp2(v[:, at:at + 1] - (FULL + 1))

    def plain(x):
        return x.astype(i32).astype(f32)

    def permuted(at, x):
        out = []
        for h in range(at.shape[0] // 8):
            want = at[8 * h:8 * h + 8]
            cols = []
            for g in range(x.shape[1] // LANES):
                tile = x[:, LANES * g:LANES * (g + 1)]
                got = jnp.take_along_axis(tile[:8], want & 7, axis=0)
                for v in range(1, rows // 8):
                    more = jnp.take_along_axis(tile[8 * v:8 * v + 8], want & 7, axis=0)
                    got = jnp.where((want >> 3) == v, more, got)
                cols.append(got)
            out.append(jnp.concatenate(cols, axis=1))
        return jnp.concatenate(out, axis=0)

    with jax.named_scope("filter"):
        raw = rec_ref[...]
        parts = []
        for g in range(groups):
            if g == 0:
                first = jnp.zeros((rows, LANES), bf16)
            else:
                first = raw[:, group * g - LANES:group * g]
            parts.append(jnp.concatenate([first, raw[:, group * g:group * (g + 1)]], axis=1))
        both = jnp.dot(jnp.concatenate(parts, axis=0), band2, preferred_element_type=f32)
        both = both[:, :LANES] + both[:, LANES:]
        edge = jnp.dot(raw[:, group * groups - LANES:], band2[:LANES], preferred_element_type=f32)
        edge = edge[:, :LANES] + edge[:, LANES:]
        filtered = jnp.concatenate([both[rows * g:rows * (g + 1)] for g in range(groups)] + [edge], axis=1)
        rr = lax.broadcasted_iota(i32, (rows, LANES), 0)
        pick = jnp.zeros((rows, LANES), i32)
        for r in range(rows):
            pick = jnp.where(rr == r, pair_ref[0, r], pick)
        q, e = encode(filtered)
        note = jnp.where(lane == SPILL, e.astype(i32), jnp.where(lane == SPILL + 1, pick, q[:, samples:])).astype(i16)
        q = q[:, :samples].astype(i16)
        own[t] = q
        halves[0] = jnp.concatenate([q[:, :part], note], axis=1)
        halves[1] = jnp.concatenate([q[:, part:], note], axis=1)
        plane[me] = halves[side]

    with jax.named_scope("wait_greeting"):
        pl.semaphore_wait(barrier, C + T - 2)

    with jax.named_scope("send_filtered"):
        others = [d for d in range(1, C) if d != half]
        mate_copy = remote(halves.at[lax.rem(side + half + 1, 2)], mate_rest, plane_s, mate_r, {"chan": at_chan(half)})
        others = [half] + others
        sends = [remote(halves.at[lax.rem(side + d, 2)], plane.at[me], plane_s, plane_r,
                         {"chan": at_chan(d)}) for d in others]
        sends += [remote(own.at[t], own.at[t], own_s, own_r.at[d - 1], {"tm": at_tm(d)}) for d in range(1, T)]
        sends = sends[:C - 1] + [mate_copy] + sends[C - 1:]
        for s in sends:
            s.start()

    with jax.named_scope("clear"):
        wp[:, window:] = jnp.zeros((rows, wp.shape[1] - window), bf16)
        wall[:, window:] = jnp.zeros((wall.shape[0], LANES * P_), bf16)

    low = t < T // 2
    def near(k):
        up = jnp.where(k >= t, k + 1, k)
        slot = jnp.where(low, up, lax.rem(t - 1 - k + T, T))
        return slot, lax.rem(t - slot + T, T)

    def relay(k):
        slot, d = near(k)
        remote(own.at[slot], own.at[slot], own_s, own_r.at[d - 1], {"tm": at_tm(d)}).wait_recv()
        s = remote(own.at[slot], partner.at[slot], partner_s, partner_r, {"chan": at_chan(half)})
        s.start()

    def combine(slot):
        note = plain(part_s[2 * slot + side][:, part:])
        mine = jnp.concatenate([plain(own[slot]), pltpu.roll(note, LANES - NOTE, 1)], axis=1)
        there = permuted(pick, pltpu.roll(note, LANES - 2 * NOTE, 1))
        return scaled(mine) + scaled(jnp.concatenate([gathered[slot], there], axis=1))

    @pl.when(t == 0)
    def _():
        with jax.named_scope("relay_all"):
            for k in (1, 0, *range(2, T - 1)) if T > 2 else range(T - 1):
                relay(k)

    @pl.when(t > 0)
    def _():
        with jax.named_scope("relay_first"):
            relay(0)

    with jax.named_scope("wait_plane"):
        arrived(plane, C - 1, plane_r)

    with jax.named_scope("pick"):
        picked = []
        per = rows // VS

        def halved(x, within):
            y = x[:VS]
            for q in range(1, per):
                y = jnp.where(within == q, x[VS * q:VS * (q + 1)], y)
            return y

        for step in range(STEPS):
            blk = blocks_ref[step]
            owner = lax.div(blk, per)
            within = lax.rem(blk, per)
            mine = halved(plain(plane[owner]), within)
            pair = mine[:, part + SPILL + 1:part + SPILL + 2].astype(i32)
            theirs = permuted(jnp.broadcast_to(pair, (VS, LANES)), plain(plane[lax.rem(owner + half, C)]))
            first, second = (x[:, part + SPILL:part + SPILL + 1] for x in (mine, theirs))
            top = jnp.maximum(first, second)
            q = jnp.round(mine * jnp.exp2(first - top - 1.0) + theirs * jnp.exp2(second - top - 1.0))
            last = jnp.where(lane[:VS] == SPILL, top, q[:, part:])
            picked.append(jnp.concatenate([q[:, :part], last], axis=1))
        x = jnp.concatenate(picked, axis=0)
        notes = [pltpu.roll(plain(plane[at][:, part:]), NOTE * g, 1) for g, at in ((1, me), (2, at_chan(half)))]
        last = jnp.where(lane < NOTE, x[:, part:], jnp.where(lane < 2 * NOTE, *notes))
        x = jnp.concatenate([x[:, :part], last], axis=1).astype(i32).astype(i16)
        mine_at = 2 * t + side
        part_s[mine_at] = x

        def twin_copy(d, at):
            return remote(part_s.at[at], part_s.at[at], twin_s, twin_r, {"chan": twin})

        def body_copy(d, at):
            return remote(part_s.at[at], part_s.at[at], twin_s, body_r.at[d - 1], {"tm": at_tm(d)})

        ts_sends = [body_copy(d, mine_at) for d in range(1, T)] + [twin_copy(0, mine_at)]
        for s in ts_sends:
            s.start()

    with jax.named_scope("relay"):
        @pl.when(t > 0)
        def _():
            for k in range(1, T - 1):
                relay(k)

    lag0 = t * lag_dev
    wide = samples + LANES
    span = samples + LANES
    if lag_dev % LANES == 0:
        base, rest = lag0, 0
    else:
        base = lax.div(lag0, LANES) * LANES
        rest = lax.rem(lag0, LANES)

    def hand_to_twin(k):
        slot, d = near(k)
        body_copy(d, 2 * slot + side).wait_recv()
        twin_copy(d, 2 * slot + side).start()

    def assemble(blocks):
        out = []
        for i, x in enumerate(blocks):
            head = x[:, :LANES]
            if i:
                head = head + jnp.where(lane < SPILL, blocks[i - 1][:, samples:], 0.0)
            out.append(jnp.concatenate([head, x[:, LANES:samples]], axis=1))
        return out

    def whiten(blocks):
        acc = jnp.zeros((rows, LANES), f32)
        for x in blocks:
            sq = x * x
            for g in range(groups):
                acc = acc + sq[:, LANES * g:LANES * (g + 1)]
        scale = lax.rsqrt(jnp.sum(acc, axis=1, keepdims=True) / window + 1e-6)
        return [(x * scale).astype(bf16) for x in blocks]

    with jax.named_scope("own_block"):
        mate_copy.wait_recv()
        near_half, far_half = plain(plane[at_chan(half)]), plain(mate_rest[...])
        mate = jnp.concatenate([jnp.where(side == 0, near_half[:, :part], far_half[:, :part]),
                                jnp.where(side == 0, far_half[:, :part], near_half[:, :part])], axis=1)
        partner[t] = mate.astype(i32).astype(i16)

    with jax.named_scope("wait_partner"):
        arrived(partner, T - 1, partner_r)
    with jax.named_scope("gather"):
        for i in range(T):
            gathered[i] = permuted(pick, plain(partner[i]))
    with jax.named_scope("hand_to_twin"):
        for k in range(T - 1):
            hand_to_twin(k)

    def whiten_own():
        white = whiten(assemble([combine(i) for i in range(T)]))
        for i in range(T):
            wp[:, samples * i:samples * (i + 1)] = white[i]

    def turn_own():
        for i in range(T):
            wrows = wp[:, pl.ds(pl.multiple_of(i * samples + base, LANES), wide)]
            for a in range(A_):
                rolled = wrows
                if lag_dev % LANES:
                    rolled = pltpu.roll(wrows, wide - FINE * a - rest, 1)
                elif a:
                    rolled = pltpu.roll(wrows, wide - FINE * a, 1)
                wall[a * rows:(a + 1) * rows, samples * i:samples * (i + 1)] = rolled[:, :samples]

    def whiten_sources():
        blocks = []
        for i in range(T):
            first, second = 2.0 * scaled(plain(part_s[2 * i])), 2.0 * scaled(plain(part_s[2 * i + 1]))
            blocks.append(jnp.concatenate([first[:, :part], second], axis=1))
        for i, x in enumerate(whiten(assemble(blocks))):
            src[i] = x

    with jax.named_scope("prepare_own"):
        whiten_own()
        turn_own()
    with jax.named_scope("wait_twin"):
        arrived(part_s, T, twin_r)
    with jax.named_scope("prepare_sources"):
        whiten_sources()

    with jax.named_scope("correlate"):
        z = None
        for i in range(T):
            before = src[i - 1][:, samples - LANES:] if i else jnp.zeros((rows, LANES), bf16)
            srows = jnp.concatenate([src[i], before], axis=1)
            xs = []
            for s in range(STEPS * VS):
                one = jnp.broadcast_to(srows[s:s + 1], (FINE, span))
                xs.append(pltpu.roll(one, 0, 1, stride=1, stride_axis=0)[:, :samples])
            ws = jnp.concatenate([wall[:, samples * i + LANES * p:samples * i + LANES * p + samples] for p in range(P_)],
                                 axis=0)
            term = lax.dot_general(ws, jnp.concatenate(xs, axis=0),
                                   (((1,), (1,)), ((), ())), preferred_element_type=f32)
            z = term if z is None else z + term
        z = z * (1.0 / math.sqrt(window))

    with jax.named_scope("result"):
        lane_group = lane // FINE
        per_tile = LANES // FINE
        span_out = min(lag_dev, LANES)
        for p in range(P_):
            for lo_s in range(0, STEPS * VS, per_tile):
                turned = []
                for a in range(A_):
                    r0 = (p * A_ + a) * rows
                    tile = z[r0:r0 + rows, lo_s * FINE:lo_s * FINE + LANES]
                    turned.append(pltpu.roll(tile, FINE * a, 1) if a else tile)
                for s in range(per_tile):
                    o = turned[0]
                    for a in range(1, A_):
                        o = jnp.where(lane_group == (s + a) % per_tile, turned[a], o)
                    if s:
                        o = pltpu.roll(o, LANES - FINE * s, 1)
                    out_ref[lo_s + s, :, LANES * p:LANES * p + span_out] = o[:, :span_out]

    with jax.named_scope("wait_sends"):
        for buf, count, sem in ((plane, C, plane_s), (own, T - 1, own_s), (partner, T - 1, partner_s),
                                (part_s, 2 * T - 1, twin_s)):
            gone(buf, count, sem)


def shards(records, pair_rows, fir_taps, source_blocks):
    C = lax.axis_size("chan")
    T = lax.axis_size("tm")
    rows, raw = records.shape
    samples = raw // 4
    f32, bf16, i16 = jnp.float32, jnp.bfloat16, jnp.int16
    dma = pltpu.SemaphoreType.DMA
    hbm = pl.BlockSpec(memory_space=pltpu.HBM)
    operands = [pltpu.with_memory_space_constraint(x, pltpu.HBM)
                for x in (fir_taps, pair_rows, source_blocks, records)]
    out = pl.pallas_call(
        functools.partial(body, C, T, rows),
        out_shape=pltpu.VMEM((STEPS * VS, rows, LAGS // T), f32),
        in_specs=[hbm] * 4,
        out_specs=pl.BlockSpec(memory_space=pltpu.VMEM),
        scratch_shapes=[
            pltpu.SMEM(fir_taps.shape, f32),
            pltpu.SMEM(pair_rows.shape, jnp.int32),
            pltpu.SMEM(source_blocks.shape, jnp.int32),
            pltpu.VMEM(records.shape, bf16),
            dma((4,)),
            pltpu.VMEM((2, rows, samples // 2 + LANES), i16),
            pltpu.VMEM((C, rows, samples // 2 + LANES), i16),
            pltpu.VMEM((rows, samples // 2 + LANES), i16),
            pltpu.VMEM((T, rows, samples), i16),
            pltpu.VMEM((T, rows, samples), i16),
            pltpu.VMEM((T, rows, samples), f32),
            pltpu.VMEM((2 * T, rows, samples // 2 + LANES), i16),
            pltpu.VMEM((T, rows, samples), bf16),
            pltpu.VMEM((rows, T * samples + LAGS + LANES), bf16),
            pltpu.VMEM((min(LAGS // T, LANES) // FINE * rows, T * samples + LANES * max(1, LAGS // T // LANES)), bf16),
            dma, dma, dma, dma((T - 1,)), dma, dma, dma, dma((T - 1,)), dma, dma,
        ],
        compiler_params=pltpu.CompilerParams(
            collective_id=0, has_side_effects=True,
            vmem_limit_bytes=(24 if samples * T <= 8192 else 60) * 2**20),
        cost_estimate=pl.CostEstimate(flops=600_000_000, bytes_accessed=1_000_000, transcendentals=0),
    )(*operands)
    return out.reshape(STEPS, VS, rows, LAGS // T)


def solution(mesh):
    return jax.shard_map(
        shards,
        mesh=mesh,
        in_specs=(P("chan", "tm"), P("chan", None), P(), P()),
        out_specs=P(None, None, "chan", "tm"),
        check_vma=False,
    )
```

```python
import functools
import math

import jax
import jax.numpy as jnp
from jax import lax
from jax.experimental import pallas as pl
from jax.experimental.pallas import tpu as pltpu
from jax.sharding import PartitionSpec as P

VS = 8
STEPS = 2
LAGS = 1024
TAPS = 32
LANES = 128
FINE = 16
SPILL = TAPS // 4
FULL = 15
NOTE = 16


def body(C, T, rows, taps_hbm, pair_hbm, blocks_hbm, rec_hbm, out_ref,
         taps_ref, pair_ref, blocks_ref, rec_ref, local_s,
         halves, plane, mate_rest, own, partner, gathered, part_s, src, wp, wall,
         plane_s, plane_r, own_s, own_r, mate_r, partner_s, partner_r,
         body_r, twin_s, twin_r):
    me = lax.axis_index("chan")
    t = lax.axis_index("tm")
    f32, bf16, i16, i32 = jnp.float32, jnp.bfloat16, jnp.int16, jnp.int32
    samples = rec_ref.shape[1] // 4
    width = samples + LANES
    part = samples // 2
    half = C // 2
    side = lax.rem(me, 2)
    twin = me + 1 - 2 * side
    lag_dev = LAGS // T
    P_ = max(1, lag_dev // LANES)
    A_ = min(lag_dev, LANES) // FINE
    window = samples * T

    def at_chan(d):
        return lax.rem(me + d, C)

    def at_tm(d):
        return lax.rem(t + d, T)

    def remote(src, dst, ssem, rsem, where):
        return pltpu.make_async_remote_copy(
            src_ref=src, dst_ref=dst, send_sem=ssem, recv_sem=rsem,
            device_id=where, device_id_type=pl.DeviceIdType.MESH)

    def arrived(buf, count, sem):
        blocks = buf.at[pl.ds(0, count)]
        pltpu.make_async_copy(blocks, blocks, sem).wait()

    gone = arrived

    with jax.named_scope("greet"):
        loads = [pltpu.make_async_copy(src, dst, local_s.at[i]) for i, (src, dst) in enumerate((
            (taps_hbm, taps_ref), (rec_hbm, rec_ref), (pair_hbm, pair_ref), (blocks_hbm, blocks_ref)))]
        loads[0].start()
        for g in range(4):
            cut = pl.ds(samples * g, samples)
            pltpu.make_async_copy(rec_hbm.at[:, cut], rec_ref.at[:, cut], local_s.at[1]).start()
        loads[2].start()
        loads[3].start()
        barrier = pltpu.get_barrier_semaphore()
        for d in range(1, C):
            pl.semaphore_signal(barrier, inc=1, device_id={"chan": at_chan(d)}, device_id_type=pl.DeviceIdType.MESH)
        for d in range(1, T):
            pl.semaphore_signal(barrier, inc=1, device_id={"tm": at_tm(d)}, device_id_type=pl.DeviceIdType.MESH)

    with jax.named_scope("band"):
        group = 4 * LANES
        depth = LANES + group
        row = lax.broadcasted_iota(i32, (8, LANES), 0)
        n = lax.broadcasted_iota(i32, (8, LANES), 1)
        tap = 4 * n + 3 - row
        cell = jnp.zeros((8, LANES), f32)
    with jax.named_scope("load_taps"):
        loads[0].wait()
    with jax.named_scope("band_tiles"):
        for k in range(TAPS):
            cell = jnp.where(tap == k, taps_ref[k], cell)
        reach = TAPS // 4 + 1
        tiles = []
        for b in range(depth // 8):
            at = 2 * b - LANES // 4
            tile = jnp.zeros_like(cell)
            if at > -reach:
                tile = pltpu.roll(cell, at % LANES, 1) if at else cell
                if at < 0:
                    tile = jnp.where(n < reach, tile, 0.0)
                elif at + reach > LANES:
                    tile = jnp.where(n >= reach, tile, 0.0)
            tiles.append(tile)
        band = jnp.concatenate(tiles, axis=0)
        hi = band.astype(bf16)
        lo = (band - hi.astype(f32)).astype(bf16)
        band2 = jnp.concatenate([hi, lo], axis=1)
    with jax.named_scope("load_records"):
        for load in loads[1:]:
            load.wait()

    groups = samples // LANES
    lane = lax.broadcasted_iota(i32, (rows, LANES), 1)

    def encode(x):
        peak = jnp.maximum(jnp.max(jnp.abs(x), axis=1, keepdims=True), 1e-30)
        e = jnp.floor(jnp.log2(peak)) + 1.0
        return jnp.clip(jnp.round(x * jnp.exp2(FULL - e)), -32767.0, 32767.0).astype(i32), e

    def scaled(v):
        at = v.shape[1] - LANES + SPILL
        return v * jnp.exp2(v[:, at:at + 1] - (FULL + 1))

    def plain(x):
        return x.astype(i32).astype(f32)

    def permuted(at, x):
        out = []
        for h in range(at.shape[0] // 8):
            want = at[8 * h:8 * h + 8]
            cols = []
            for g in range(x.shape[1] // LANES):
                tile = x[:, LANES * g:LANES * (g + 1)]
                got = jnp.take_along_axis(tile[:8], want & 7, axis=0)
                for v in range(1, rows // 8):
                    more = jnp.take_along_axis(tile[8 * v:8 * v + 8], want & 7, axis=0)
                    got = jnp.where((want >> 3) == v, more, got)
                cols.append(got)
            out.append(jnp.concatenate(cols, axis=1))
        return jnp.concatenate(out, axis=0)

    with jax.named_scope("filter"):
        raw = rec_ref[...]
        parts = []
        for g in range(groups):
            if g == 0:
                first = jnp.zeros((rows, LANES), bf16)
            else:
                first = raw[:, group * g - LANES:group * g]
            parts.append(jnp.concatenate([first, raw[:, group * g:group * (g + 1)]], axis=1))
        both = jnp.dot(jnp.concatenate(parts, axis=0), band2, preferred_element_type=f32)
        both = both[:, :LANES] + both[:, LANES:]
        edge = jnp.dot(raw[:, group * groups - LANES:], band2[:LANES], preferred_element_type=f32)
        edge = edge[:, :LANES] + edge[:, LANES:]
        filtered = jnp.concatenate([both[rows * g:rows * (g + 1)] for g in range(groups)] + [edge], axis=1)
        rr = lax.broadcasted_iota(i32, (rows, LANES), 0)
        pick = jnp.zeros((rows, LANES), i32)
        for r in range(rows):
            pick = jnp.where(rr == r, pair_ref[0, r], pick)
        q, e = encode(filtered)
        note = jnp.where(lane == SPILL, e.astype(i32), jnp.where(lane == SPILL + 1, pick, q[:, samples:])).astype(i16)
        q = q[:, :samples].astype(i16)
        own[t] = q
        halves[0] = jnp.concatenate([q[:, :part], note], axis=1)
        halves[1] = jnp.concatenate([q[:, part:], note], axis=1)
        plane[me] = halves[side]

    with jax.named_scope("wait_greeting"):
        pl.semaphore_wait(barrier, C + T - 2)

    with jax.named_scope("send_filtered"):
        others = [d for d in range(1, C) if d != half]
        mate_copy = remote(halves.at[lax.rem(side + half + 1, 2)], mate_rest, plane_s, mate_r, {"chan": at_chan(half)})
        others = [half] + others
        sends = [remote(halves.at[lax.rem(side + d, 2)], plane.at[me], plane_s, plane_r,
                         {"chan": at_chan(d)}) for d in others]
        sends += [remote(own.at[t], own.at[t], own_s, own_r.at[d - 1], {"tm": at_tm(d)}) for d in range(1, T)]
        sends = sends[:C - 1] + [mate_copy] + sends[C - 1:]
        for s in sends:
            s.start()

    with jax.named_scope("clear"):
        wp[:, window:] = jnp.zeros((rows, wp.shape[1] - window), bf16)
        wall[:, window:] = jnp.zeros((wall.shape[0], LANES * P_), bf16)

    low = t < T // 2
    def near(k):
        up = jnp.where(k >= t, k + 1, k)
        slot = jnp.where(low, up, lax.rem(t - 1 - k + T, T))
        return slot, lax.rem(t - slot + T, T)

    def relay(k):
        slot, d = near(k)
        remote(own.at[slot], own.at[slot], own_s, own_r.at[d - 1], {"tm": at_tm(d)}).wait_recv()
        s = remote(own.at[slot], partner.at[slot], partner_s, partner_r, {"chan": at_chan(half)})
        s.start()

    def combine(slot):
        note = plain(part_s[2 * slot + side][:, part:])
        mine = jnp.concatenate([plain(own[slot]), pltpu.roll(note, LANES - NOTE, 1)], axis=1)
        there = permuted(pick, pltpu.roll(note, LANES - 2 * NOTE, 1))
        return scaled(mine) + scaled(jnp.concatenate([gathered[slot], there], axis=1))

    @pl.when(t == 0)
    def _():
        with jax.named_scope("relay_all"):
            for k in (1, 0, *range(2, T - 1)) if T > 2 else range(T - 1):
                relay(k)

    with jax.named_scope("wait_plane"):
        arrived(plane, C - 1, plane_r)

    with jax.named_scope("pick"):
        picked = []
        per = rows // VS

        def halved(x, within):
            y = x[:VS]
            for q in range(1, per):
                y = jnp.where(within == q, x[VS * q:VS * (q + 1)], y)
            return y

        for step in range(STEPS):
            blk = blocks_ref[step]
            owner = lax.div(blk, per)
            within = lax.rem(blk, per)
            mine = halved(plain(plane[owner]), within)
            pair = mine[:, part + SPILL + 1:part + SPILL + 2].astype(i32)
            theirs = permuted(jnp.broadcast_to(pair, (VS, LANES)), plain(plane[lax.rem(owner + half, C)]))
            first, second = (x[:, part + SPILL:part + SPILL + 1] for x in (mine, theirs))
            top = jnp.maximum(first, second)
            q = jnp.round(mine * jnp.exp2(first - top - 1.0) + theirs * jnp.exp2(second - top - 1.0))
            last = jnp.where(lane[:VS] == SPILL, top, q[:, part:])
            picked.append(jnp.concatenate([q[:, :part], last], axis=1))
        x = jnp.concatenate(picked, axis=0)
        notes = [pltpu.roll(plain(plane[at][:, part:]), NOTE * g, 1) for g, at in ((1, me), (2, at_chan(half)))]
        last = jnp.where(lane < NOTE, x[:, part:], jnp.where(lane < 2 * NOTE, *notes))
        x = jnp.concatenate([x[:, :part], last], axis=1).astype(i32).astype(i16)
        mine_at = 2 * t + side
        part_s[mine_at] = x

        def twin_copy(d, at):
            return remote(part_s.at[at], part_s.at[at], twin_s, twin_r, {"chan": twin})

        def body_copy(d, at):
            return remote(part_s.at[at], part_s.at[at], twin_s, body_r.at[d - 1], {"tm": at_tm(d)})

        ts_sends = [body_copy(d, mine_at) for d in range(1, T)] + [twin_copy(0, mine_at)]
        for s in ts_sends:
            s.start()

    with jax.named_scope("relay"):
        @pl.when(t > 0)
        def _():
            for k in range(T - 1):
                relay(k)

    lag0 = t * lag_dev
    wide = samples + LANES
    span = samples + LANES
    if lag_dev % LANES == 0:
        base, rest = lag0, 0
    else:
        base = lax.div(lag0, LANES) * LANES
        rest = lax.rem(lag0, LANES)

    def hand_to_twin(k):
        slot, d = near(k)
        body_copy(d, 2 * slot + side).wait_recv()
        twin_copy(d, 2 * slot + side).start()

    def assemble(blocks):
        out = []
        for i, x in enumerate(blocks):
            head = x[:, :LANES]
            if i:
                head = head + jnp.where(lane < SPILL, blocks[i - 1][:, samples:], 0.0)
            out.append(jnp.concatenate([head, x[:, LANES:samples]], axis=1))
        return out

    def whiten(blocks):
        acc = jnp.zeros((rows, LANES), f32)
        for x in blocks:
            sq = x * x
            for g in range(groups):
                acc = acc + sq[:, LANES * g:LANES * (g + 1)]
        scale = lax.rsqrt(jnp.sum(acc, axis=1, keepdims=True) / window + 1e-6)
        return [(x * scale).astype(bf16) for x in blocks]

    with jax.named_scope("own_block"):
        mate_copy.wait_recv()
        near_half, far_half = plain(plane[at_chan(half)]), plain(mate_rest[...])
        mate = jnp.concatenate([jnp.where(side == 0, near_half[:, :part], far_half[:, :part]),
                                jnp.where(side == 0, far_half[:, :part], near_half[:, :part])], axis=1)
        partner[t] = mate.astype(i32).astype(i16)

    with jax.named_scope("wait_partner"):
        arrived(partner, T - 1, partner_r)
    with jax.named_scope("gather"):
        for i in range(T):
            gathered[i] = permuted(pick, plain(partner[i]))
    with jax.named_scope("hand_to_twin"):
        for k in range(T - 1):
            hand_to_twin(k)

    def whiten_own():
        white = whiten(assemble([combine(i) for i in range(T)]))
        for i in range(T):
            wp[:, samples * i:samples * (i + 1)] = white[i]

    def turn_own():
        for i in range(T):
            wrows = wp[:, pl.ds(pl.multiple_of(i * samples + base, LANES), wide)]
            for a in range(A_):
                rolled = wrows
                if lag_dev % LANES:
                    rolled = pltpu.roll(wrows, wide - FINE * a - rest, 1)
                elif a:
                    rolled = pltpu.roll(wrows, wide - FINE * a, 1)
                wall[a * rows:(a + 1) * rows, samples * i:samples * (i + 1)] = rolled[:, :samples]

    def whiten_sources():
        blocks = []
        for i in range(T):
            first, second = 2.0 * scaled(plain(part_s[2 * i])), 2.0 * scaled(plain(part_s[2 * i + 1]))
            blocks.append(jnp.concatenate([first[:, :part], second], axis=1))
        for i, x in enumerate(whiten(assemble(blocks))):
            src[i] = x

    with jax.named_scope("prepare_own"):
        whiten_own()
        turn_own()
    with jax.named_scope("wait_twin"):
        arrived(part_s, T, twin_r)
    with jax.named_scope("prepare_sources"):
        whiten_sources()

    with jax.named_scope("correlate"):
        z = None
        for i in range(T):
            before = src[i - 1][:, samples - LANES:] if i else jnp.zeros((rows, LANES), bf16)
            srows = jnp.concatenate([src[i], before], axis=1)
            xs = []
            for s in range(STEPS * VS):
                one = jnp.broadcast_to(srows[s:s + 1], (FINE, span))
                xs.append(pltpu.roll(one, 0, 1, stride=1, stride_axis=0)[:, :samples])
            ws = jnp.concatenate([wall[:, samples * i + LANES * p:samples * i + LANES * p + samples] for p in range(P_)],
                                 axis=0)
            term = lax.dot_general(ws, jnp.concatenate(xs, axis=0),
                                   (((1,), (1,)), ((), ())), preferred_element_type=f32)
            z = term if z is None else z + term
        z = z * (1.0 / math.sqrt(window))

    with jax.named_scope("result"):
        lane_group = lane // FINE
        per_tile = LANES // FINE
        span_out = min(lag_dev, LANES)
        for p in range(P_):
            for lo_s in range(0, STEPS * VS, per_tile):
                turned = []
                for a in range(A_):
                    r0 = (p * A_ + a) * rows
                    tile = z[r0:r0 + rows, lo_s * FINE:lo_s * FINE + LANES]
                    turned.append(pltpu.roll(tile, FINE * a, 1) if a else tile)
                for s in range(per_tile):
                    o = turned[0]
                    for a in range(1, A_):
                        o = jnp.where(lane_group == (s + a) % per_tile, turned[a], o)
                    if s:
                        o = pltpu.roll(o, LANES - FINE * s, 1)
                    out_ref[lo_s + s, :, LANES * p:LANES * p + span_out] = o[:, :span_out]

    with jax.named_scope("wait_sends"):
        for buf, count, sem in ((plane, C, plane_s), (own, T - 1, own_s), (partner, T - 1, partner_s),
                                (part_s, 2 * T - 1, twin_s)):
            gone(buf, count, sem)


def shards(records, pair_rows, fir_taps, source_blocks):
    C = lax.axis_size("chan")
    T = lax.axis_size("tm")
    rows, raw = records.shape
    samples = raw // 4
    f32, bf16, i16 = jnp.float32, jnp.bfloat16, jnp.int16
    dma = pltpu.SemaphoreType.DMA
    hbm = pl.BlockSpec(memory_space=pltpu.HBM)
    operands = [pltpu.with_memory_space_constraint(x, pltpu.HBM)
                for x in (fir_taps, pair_rows, source_blocks, records)]
    out = pl.pallas_call(
        functools.partial(body, C, T, rows),
        out_shape=pltpu.VMEM((STEPS * VS, rows, LAGS // T), f32),
        in_specs=[hbm] * 4,
        out_specs=pl.BlockSpec(memory_space=pltpu.VMEM),
        scratch_shapes=[
            pltpu.SMEM(fir_taps.shape, f32),
            pltpu.SMEM(pair_rows.shape, jnp.int32),
            pltpu.SMEM(source_blocks.shape, jnp.int32),
            pltpu.VMEM(records.shape, bf16),
            dma((4,)),
            pltpu.VMEM((2, rows, samples // 2 + LANES), i16),
            pltpu.VMEM((C, rows, samples // 2 + LANES), i16),
            pltpu.VMEM((rows, samples // 2 + LANES), i16),
            pltpu.VMEM((T, rows, samples), i16),
            pltpu.VMEM((T, rows, samples), i16),
            pltpu.VMEM((T, rows, samples), f32),
            pltpu.VMEM((2 * T, rows, samples // 2 + LANES), i16),
            pltpu.VMEM((T, rows, samples), bf16),
            pltpu.VMEM((rows, T * samples + LAGS + LANES), bf16),
            pltpu.VMEM((min(LAGS // T, LANES) // FINE * rows, T * samples + LANES * max(1, LAGS // T // LANES)), bf16),
            dma, dma, dma, dma((T - 1,)), dma, dma, dma, dma((T - 1,)), dma, dma,
        ],
        compiler_params=pltpu.CompilerParams(
            collective_id=0, has_side_effects=True,
            vmem_limit_bytes=(24 if samples * T <= 8192 else 60) * 2**20),
        cost_estimate=pl.CostEstimate(flops=600_000_000, bytes_accessed=1_000_000, transcendentals=0),
    )(*operands)
    return out.reshape(STEPS, VS, rows, LAGS // T)


def solution(mesh):
    return jax.shard_map(
        shards,
        mesh=mesh,
        in_specs=(P("chan", "tm"), P("chan", None), P(), P()),
        out_specs=P(None, None, "chan", "tm"),
        check_vma=False,
    )
```

```python
import functools
import math

import jax
import jax.numpy as jnp
from jax import lax
from jax.experimental import pallas as pl
from jax.experimental.pallas import tpu as pltpu
from jax.sharding import PartitionSpec as P

VS = 8
STEPS = 2
LAGS = 1024
TAPS = 32
LANES = 128
FINE = 16
SPILL = TAPS // 4
FULL = 15
NOTE = 16


def body(C, T, rows, taps_hbm, pair_hbm, blocks_hbm, rec_hbm, out_ref,
         taps_ref, pair_ref, blocks_ref, rec_ref, local_s,
         halves, plane, mate_rest, own, partner, gathered, part_s, src, wp, wall,
         plane_s, plane_r, own_s, own_r, mate_s, mate_r, partner_s, partner_r,
         body_r, twin_s, twin_r):
    me = lax.axis_index("chan")
    t = lax.axis_index("tm")
    f32, bf16, i16, i32 = jnp.float32, jnp.bfloat16, jnp.int16, jnp.int32
    samples = rec_ref.shape[1] // 4
    width = samples + LANES
    part = samples // 2
    half = C // 2
    side = lax.rem(me, 2)
    twin = me + 1 - 2 * side
    lag_dev = LAGS // T
    P_ = max(1, lag_dev // LANES)
    A_ = min(lag_dev, LANES) // FINE
    window = samples * T

    def at_chan(d):
        return lax.rem(me + d, C)

    def at_tm(d):
        return lax.rem(t + d, T)

    def remote(src, dst, ssem, rsem, where):
        return pltpu.make_async_remote_copy(
            src_ref=src, dst_ref=dst, send_sem=ssem, recv_sem=rsem,
            device_id=where, device_id_type=pl.DeviceIdType.MESH)

    def arrived(buf, count, sem):
        blocks = buf.at[pl.ds(0, count)]
        pltpu.make_async_copy(blocks, blocks, sem).wait()

    gone = arrived

    with jax.named_scope("greet"):
        loads = [pltpu.make_async_copy(src, dst, local_s.at[i]) for i, (src, dst) in enumerate((
            (taps_hbm, taps_ref), (rec_hbm, rec_ref), (pair_hbm, pair_ref), (blocks_hbm, blocks_ref)))]
        loads[0].start()
        for g in range(4):
            cut = pl.ds(samples * g, samples)
            pltpu.make_async_copy(rec_hbm.at[:, cut], rec_ref.at[:, cut], local_s.at[1]).start()
        loads[2].start()
        loads[3].start()
        barrier = pltpu.get_barrier_semaphore()
        for d in range(1, C):
            pl.semaphore_signal(barrier, inc=1, device_id={"chan": at_chan(d)}, device_id_type=pl.DeviceIdType.MESH)
        for d in range(1, T):
            pl.semaphore_signal(barrier, inc=1, device_id={"tm": at_tm(d)}, device_id_type=pl.DeviceIdType.MESH)

    with jax.named_scope("band"):
        group = 4 * LANES
        depth = LANES + group
        row = lax.broadcasted_iota(i32, (8, LANES), 0)
        n = lax.broadcasted_iota(i32, (8, LANES), 1)
        tap = 4 * n + 3 - row
        cell = jnp.zeros((8, LANES), f32)
    with jax.named_scope("load_taps"):
        loads[0].wait()
    with jax.named_scope("band_tiles"):
        for k in range(TAPS):
            cell = jnp.where(tap == k, taps_ref[k], cell)
        reach = TAPS // 4 + 1
        tiles = []
        for b in range(depth // 8):
            at = 2 * b - LANES // 4
            tile = jnp.zeros_like(cell)
            if at > -reach:
                tile = pltpu.roll(cell, at % LANES, 1) if at else cell
                if at < 0:
                    tile = jnp.where(n < reach, tile, 0.0)
                elif at + reach > LANES:
                    tile = jnp.where(n >= reach, tile, 0.0)
            tiles.append(tile)
        band = jnp.concatenate(tiles, axis=0)
        hi = band.astype(bf16)
        lo = (band - hi.astype(f32)).astype(bf16)
        band2 = jnp.concatenate([hi, lo], axis=1)
    with jax.named_scope("load_records"):
        for load in loads[1:]:
            load.wait()

    groups = samples // LANES
    lane = lax.broadcasted_iota(i32, (rows, LANES), 1)

    def encode(x):
        peak = jnp.maximum(jnp.max(jnp.abs(x), axis=1, keepdims=True), 1e-30)
        e = jnp.floor(jnp.log2(peak)) + 1.0
        return jnp.clip(jnp.round(x * jnp.exp2(FULL - e)), -32767.0, 32767.0).astype(i32), e

    def scaled(v):
        at = v.shape[1] - LANES + SPILL
        return v * jnp.exp2(v[:, at:at + 1] - (FULL + 1))

    def plain(x):
        return x.astype(i32).astype(f32)

    def permuted(at, x):
        out = []
        for h in range(at.shape[0] // 8):
            want = at[8 * h:8 * h + 8]
            cols = []
            for g in range(x.shape[1] // LANES):
                tile = x[:, LANES * g:LANES * (g + 1)]
                got = jnp.take_along_axis(tile[:8], want & 7, axis=0)
                for v in range(1, rows // 8):
                    more = jnp.take_along_axis(tile[8 * v:8 * v + 8], want & 7, axis=0)
                    got = jnp.where((want >> 3) == v, more, got)
                cols.append(got)
            out.append(jnp.concatenate(cols, axis=1))
        return jnp.concatenate(out, axis=0)

    with jax.named_scope("filter"):
        raw = rec_ref[...]
        parts = []
        for g in range(groups):
            if g == 0:
                first = jnp.zeros((rows, LANES), bf16)
            else:
                first = raw[:, group * g - LANES:group * g]
            parts.append(jnp.concatenate([first, raw[:, group * g:group * (g + 1)]], axis=1))
        both = jnp.dot(jnp.concatenate(parts, axis=0), band2, preferred_element_type=f32)
        both = both[:, :LANES] + both[:, LANES:]
        edge = jnp.dot(raw[:, group * groups - LANES:], band2[:LANES], preferred_element_type=f32)
        edge = edge[:, :LANES] + edge[:, LANES:]
        filtered = jnp.concatenate([both[rows * g:rows * (g + 1)] for g in range(groups)] + [edge], axis=1)
        rr = lax.broadcasted_iota(i32, (rows, LANES), 0)
        pick = jnp.zeros((rows, LANES), i32)
        for r in range(rows):
            pick = jnp.where(rr == r, pair_ref[0, r], pick)
        q, e = encode(filtered)
        note = jnp.where(lane == SPILL, e.astype(i32), jnp.where(lane == SPILL + 1, pick, q[:, samples:])).astype(i16)
        q = q[:, :samples].astype(i16)
        own[t] = q
        halves[0] = jnp.concatenate([q[:, :part], note], axis=1)
        halves[1] = jnp.concatenate([q[:, part:], note], axis=1)
        plane[me] = halves[side]

    with jax.named_scope("wait_greeting"):
        pl.semaphore_wait(barrier, C + T - 2)

    with jax.named_scope("send_filtered"):
        others = [d for d in range(1, C) if d != half]
        mate_copy = remote(halves.at[lax.rem(side + half + 1, 2), :, pl.ds(0, part)], mate_rest, mate_s, mate_r,
                           {"chan": at_chan(half)})
        others = [half] + others
        sends = [remote(halves.at[lax.rem(side + d, 2)], plane.at[me], plane_s, plane_r,
                         {"chan": at_chan(d)}) for d in others]
        sends += [remote(own.at[t], own.at[t], own_s, own_r.at[d - 1], {"tm": at_tm(d)}) for d in range(1, T)]
        sends = sends[:C - 1] + [mate_copy] + sends[C - 1:]
        for s in sends:
            s.start()

    with jax.named_scope("clear"):
        wp[:, window:] = jnp.zeros((rows, wp.shape[1] - window), bf16)
        wall[:, window:] = jnp.zeros((wall.shape[0], LANES * P_), bf16)

    low = t < T // 2
    def near(k):
        up = jnp.where(k >= t, k + 1, k)
        slot = jnp.where(low, up, lax.rem(t - 1 - k + T, T))
        return slot, lax.rem(t - slot + T, T)

    def relay(k):
        slot, d = near(k)
        remote(own.at[slot], own.at[slot], own_s, own_r.at[d - 1], {"tm": at_tm(d)}).wait_recv()
        s = remote(own.at[slot], partner.at[slot], partner_s, partner_r, {"chan": at_chan(half)})
        s.start()

    def combine(slot):
        note = plain(part_s[2 * slot + side][:, part:])
        mine = jnp.concatenate([plain(own[slot]), pltpu.roll(note, LANES - NOTE, 1)], axis=1)
        there = permuted(pick, pltpu.roll(note, LANES - 2 * NOTE, 1))
        return scaled(mine) + scaled(jnp.concatenate([gathered[slot], there], axis=1))

    @pl.when(t == 0)
    def _():
        with jax.named_scope("relay_all"):
            for k in (1, 0, *range(2, T - 1)) if T > 2 else range(T - 1):
                relay(k)

    @pl.when(t > 0)
    def _():
        with jax.named_scope("relay_first"):
            relay(0)

    with jax.named_scope("wait_plane"):
        arrived(plane, C - 1, plane_r)

    with jax.named_scope("pick"):
        picked = []
        per = rows // VS

        def halved(x, within):
            y = x[:VS]
            for q in range(1, per):
                y = jnp.where(within == q, x[VS * q:VS * (q + 1)], y)
            return y

        for step in range(STEPS):
            blk = blocks_ref[step]
            owner = lax.div(blk, per)
            within = lax.rem(blk, per)
            mine = halved(plain(plane[owner]), within)
            pair = mine[:, part + SPILL + 1:part + SPILL + 2].astype(i32)
            theirs = permuted(jnp.broadcast_to(pair, (VS, LANES)), plain(plane[lax.rem(owner + half, C)]))
            first, second = (x[:, part + SPILL:part + SPILL + 1] for x in (mine, theirs))
            top = jnp.maximum(first, second)
            q = jnp.round(mine * jnp.exp2(first - top - 1.0) + theirs * jnp.exp2(second - top - 1.0))
            last = jnp.where(lane[:VS] == SPILL, top, q[:, part:])
            picked.append(jnp.concatenate([q[:, :part], last], axis=1))
        x = jnp.concatenate(picked, axis=0)
        notes = [pltpu.roll(plain(plane[at][:, part:]), NOTE * g, 1) for g, at in ((1, me), (2, at_chan(half)))]
        last = jnp.where(lane < NOTE, x[:, part:], jnp.where(lane < 2 * NOTE, *notes))
        x = jnp.concatenate([x[:, :part], last], axis=1).astype(i32).astype(i16)
        mine_at = 2 * t + side
        part_s[mine_at] = x

        def twin_copy(d, at):
            return remote(part_s.at[at], part_s.at[at], twin_s, twin_r, {"chan": twin})

        def body_copy(d, at):
            return remote(part_s.at[at], part_s.at[at], twin_s, body_r.at[d - 1], {"tm": at_tm(d)})

        ts_sends = [body_copy(d, mine_at) for d in range(1, T)] + [twin_copy(0, mine_at)]
        for s in ts_sends:
            s.start()

    with jax.named_scope("relay"):
        @pl.when(t > 0)
        def _():
            for k in range(1, T - 1):
                relay(k)

    lag0 = t * lag_dev
    wide = samples + LANES
    span = samples + LANES
    if lag_dev % LANES == 0:
        base, rest = lag0, 0
    else:
        base = lax.div(lag0, LANES) * LANES
        rest = lax.rem(lag0, LANES)

    def hand_to_twin(k):
        slot, d = near(k)
        body_copy(d, 2 * slot + side).wait_recv()
        twin_copy(d, 2 * slot + side).start()

    def assemble(blocks):
        out = []
        for i, x in enumerate(blocks):
            head = x[:, :LANES]
            if i:
                head = head + jnp.where(lane < SPILL, blocks[i - 1][:, samples:], 0.0)
            out.append(jnp.concatenate([head, x[:, LANES:samples]], axis=1))
        return out

    def whiten(blocks):
        acc = jnp.zeros((rows, LANES), f32)
        for x in blocks:
            sq = x * x
            for g in range(groups):
                acc = acc + sq[:, LANES * g:LANES * (g + 1)]
        scale = lax.rsqrt(jnp.sum(acc, axis=1, keepdims=True) / window + 1e-6)
        return [(x * scale).astype(bf16) for x in blocks]

    with jax.named_scope("own_block"):
        mate_copy.wait_recv()
        near_half, far_half = plain(plane[at_chan(half)])[:, :part], plain(mate_rest[...])
        mate = jnp.concatenate([jnp.where(side == 0, near_half, far_half),
                                jnp.where(side == 0, far_half, near_half)], axis=1)
        partner[t] = mate.astype(i32).astype(i16)

    with jax.named_scope("wait_partner"):
        arrived(partner, T - 1, partner_r)
    with jax.named_scope("gather"):
        for i in range(T):
            gathered[i] = permuted(pick, plain(partner[i]))
    with jax.named_scope("hand_to_twin"):
        for k in range(T - 1):
            hand_to_twin(k)

    def whiten_own():
        white = whiten(assemble([combine(i) for i in range(T)]))
        for i in range(T):
            wp[:, samples * i:samples * (i + 1)] = white[i]

    def turn_own():
        for i in range(T):
            wrows = wp[:, pl.ds(pl.multiple_of(i * samples + base, LANES), wide)]
            for a in range(A_):
                rolled = wrows
                if lag_dev % LANES:
                    rolled = pltpu.roll(wrows, wide - FINE * a - rest, 1)
                elif a:
                    rolled = pltpu.roll(wrows, wide - FINE * a, 1)
                wall[a * rows:(a + 1) * rows, samples * i:samples * (i + 1)] = rolled[:, :samples]

    def whiten_sources():
        blocks = []
        for i in range(T):
            first, second = 2.0 * scaled(plain(part_s[2 * i])), 2.0 * scaled(plain(part_s[2 * i + 1]))
            blocks.append(jnp.concatenate([first[:, :part], second], axis=1))
        for i, x in enumerate(whiten(assemble(blocks))):
            src[i] = x

    with jax.named_scope("prepare_own"):
        whiten_own()
        turn_own()
    with jax.named_scope("wait_twin"):
        arrived(part_s, T, twin_r)
    with jax.named_scope("prepare_sources"):
        whiten_sources()

    with jax.named_scope("correlate"):
        z = None
        for i in range(T):
            before = src[i - 1][:, samples - LANES:] if i else jnp.zeros((rows, LANES), bf16)
            srows = jnp.concatenate([src[i], before], axis=1)
            xs = []
            for s in range(STEPS * VS):
                one = jnp.broadcast_to(srows[s:s + 1], (FINE, span))
                xs.append(pltpu.roll(one, 0, 1, stride=1, stride_axis=0)[:, :samples])
            ws = jnp.concatenate([wall[:, samples * i + LANES * p:samples * i + LANES * p + samples] for p in range(P_)],
                                 axis=0)
            term = lax.dot_general(ws, jnp.concatenate(xs, axis=0),
                                   (((1,), (1,)), ((), ())), preferred_element_type=f32)
            z = term if z is None else z + term
        z = z * (1.0 / math.sqrt(window))

    with jax.named_scope("result"):
        lane_group = lane // FINE
        per_tile = LANES // FINE
        span_out = min(lag_dev, LANES)
        for p in range(P_):
            for lo_s in range(0, STEPS * VS, per_tile):
                turned = []
                for a in range(A_):
                    r0 = (p * A_ + a) * rows
                    tile = z[r0:r0 + rows, lo_s * FINE:lo_s * FINE + LANES]
                    turned.append(pltpu.roll(tile, FINE * a, 1) if a else tile)
                for s in range(per_tile):
                    o = turned[0]
                    for a in range(1, A_):
                        o = jnp.where(lane_group == (s + a) % per_tile, turned[a], o)
                    if s:
                        o = pltpu.roll(o, LANES - FINE * s, 1)
                    out_ref[lo_s + s, :, LANES * p:LANES * p + span_out] = o[:, :span_out]

    with jax.named_scope("wait_sends"):
        for buf, count, sem in ((plane, C - 1, plane_s), (own, T - 1, own_s), (partner, T - 1, partner_s),
                                (part_s, 2 * T - 1, twin_s)):
            gone(buf, count, sem)
        mate_copy.wait_send()


def shards(records, pair_rows, fir_taps, source_blocks):
    C = lax.axis_size("chan")
    T = lax.axis_size("tm")
    rows, raw = records.shape
    samples = raw // 4
    f32, bf16, i16 = jnp.float32, jnp.bfloat16, jnp.int16
    dma = pltpu.SemaphoreType.DMA
    hbm = pl.BlockSpec(memory_space=pltpu.HBM)
    operands = [pltpu.with_memory_space_constraint(x, pltpu.HBM)
                for x in (fir_taps, pair_rows, source_blocks, records)]
    out = pl.pallas_call(
        functools.partial(body, C, T, rows),
        out_shape=pltpu.VMEM((STEPS * VS, rows, LAGS // T), f32),
        in_specs=[hbm] * 4,
        out_specs=pl.BlockSpec(memory_space=pltpu.VMEM),
        scratch_shapes=[
            pltpu.SMEM(fir_taps.shape, f32),
            pltpu.SMEM(pair_rows.shape, jnp.int32),
            pltpu.SMEM(source_blocks.shape, jnp.int32),
            pltpu.VMEM(records.shape, bf16),
            dma((4,)),
            pltpu.VMEM((2, rows, samples // 2 + LANES), i16),
            pltpu.VMEM((C, rows, samples // 2 + LANES), i16),
            pltpu.VMEM((rows, samples // 2), i16),
            pltpu.VMEM((T, rows, samples), i16),
            pltpu.VMEM((T, rows, samples), i16),
            pltpu.VMEM((T, rows, samples), f32),
            pltpu.VMEM((2 * T, rows, samples // 2 + LANES), i16),
            pltpu.VMEM((T, rows, samples), bf16),
            pltpu.VMEM((rows, T * samples + LAGS + LANES), bf16),
            pltpu.VMEM((min(LAGS // T, LANES) // FINE * rows, T * samples + LANES * max(1, LAGS // T // LANES)), bf16),
            dma, dma, dma, dma((T - 1,)), dma, dma, dma, dma, dma((T - 1,)), dma, dma,
        ],
        compiler_params=pltpu.CompilerParams(
            collective_id=0, has_side_effects=True,
            vmem_limit_bytes=(24 if samples * T <= 8192 else 60) * 2**20),
        cost_estimate=pl.CostEstimate(flops=600_000_000, bytes_accessed=1_000_000, transcendentals=0),
    )(*operands)
    return out.reshape(STEPS, VS, rows, LAGS // T)


def solution(mesh):
    return jax.shard_map(
        shards,
        mesh=mesh,
        in_specs=(P("chan", "tm"), P("chan", None), P(), P()),
        out_specs=P(None, None, "chan", "tm"),
        check_vma=False,
    )
```
